32 devices in a mesh: section: 2 (over y), dp: 4 (over z), tensor: 4 (over x, core).
Axes of the slice: x: 2, y: 2, z: 4, core: 2. Of those that a mesh axis runs over, the one named last changes fastest.
Arguments:
- ends_in: bfloat16 [2, 3, 16, 128, 768], P('section', None, 'dp'), may hold values from -6 to 6
- segment_ids: int32 [3, 16, 128], P(None, 'dp'), may hold values from 0 to 3, never falling along the last dimension, each value on 1 to 64 neighbouring positions
- w_qkv: bfloat16 [2, 768, 3, 768], P('section', None, None, 'tensor'), may hold values from -0.21875 to 0.21875
- bias_qv: bfloat16 [2, 2, 768], P('section', None, 'tensor'), may hold values from -0.59765625 to 0.59765625
- w_out: bfloat16 [2, 768, 768], P('section', 'tensor'), may hold values from -0.75 to 0.75
- bias_out: bfloat16 [2, 768], P('section'), may hold values from -0.59765625 to 0.59765625
- gain_one: bfloat16 [2, 768], P('section'), may hold values from 0.5 to 1.5
- shift_one: bfloat16 [2, 768], P('section'), may hold values from -0.59765625 to 0.59765625
- w_up: bfloat16 [2, 768, 3072], P('section', None, 'tensor'), may hold values from -0.21875 to 0.21875
- bias_up: bfloat16 [2, 3072], P('section', 'tensor'), may hold values from -0.59765625 to 0.59765625
- w_down: bfloat16 [2, 3072, 768], P('section', 'tensor'), may hold values from -0.109375 to 0.109375
- bias_down: bfloat16 [2, 768], P('section'), may hold values from -0.59765625 to 0.59765625
- gain_two: bfloat16 [2, 768], P('section'), may hold values from 0.5 to 1.5
- shift_two: bfloat16 [2, 768], P('section'), may hold values from -0.59765625 to 0.59765625
Outputs:
- ends_out: float32 [2, 3, 16, 128, 768], P('section', None, 'dp')
- grad_qkv: float32 [2, 768, 3, 768], P('section', None, None, 'tensor')
- grad_bias_qv: float32 [2, 2, 768], P('section', None, 'tensor')
- grad_out: float32 [2, 768, 768], P('section', 'tensor')
- grad_bias_out: float32 [2, 768], P('section')
- grad_gain_one: float32 [2, 768], P('section')
- grad_shift_one: float32 [2, 768], P('section')
- grad_up: float32 [2, 768, 3072], P('section', None, 'tensor')
- grad_bias_up: float32 [2, 3072], P('section', 'tensor')
- grad_down: float32 [2, 3072, 768], P('section', 'tensor')
- grad_bias_down: float32 [2, 768], P('section')
- grad_gain_two: float32 [2, 768], P('section')
- grad_shift_two: float32 [2, 768], P('section')
The draws below stay inside these ranges and needn't reach their ends.
Inputs may be any that keep to these rules, and one draw needn't show every extreme that they name: `segment_ids`: within each sequence the numbers never fall; each of 0 to 3 holds 1 to 64 rows, and one holds exactly 64.
All inputs are finite; a program needn't handle non-finite values.
Results may differ from the reference program's by a relative error of at most 0.025.
Values may be sent and summed in bfloat16 or wider, within the bound.
No kernel may reach another device: no remote copies, remote signals or barrier semaphores. Data moves between devices by JAX's collectives and lax.ppermute only.
A program may use at most 192 MiB of HBM per device.

```python
import math
import jax
import jax.numpy as jnp
import numpy as np
from jax import lax

D = 768
HEAD = 64
FF = 3072
LEN = 128
MICRO = 3
SEQS = 16
LAYERS = 2


def level_of(own_key, dims, cuts, least, largest):
    factor_of, own = 1.0, jax.random.fold_in(own_key, 6)
    for axis_at, shards_of in cuts:
        draws = jnp.exp(jax.random.uniform(jax.random.fold_in(own, axis_at), (shards_of,), jnp.float32, least / len(cuts), largest / len(cuts)))
        factor_of = factor_of * jnp.repeat(draws, dims[axis_at] // shards_of).reshape([-1 if axis == axis_at else 1 for axis in range(len(dims))])
    return factor_of


def length_profile(number_of, total, limit, lean):
    loads = [(1 << 20) // math.isqrt(grade ** lean) + 1 for grade in range(2, number_of + 1)]
    rest, given = total - limit - (number_of - 1), [1] * (number_of - 1)
    while rest > 0:
        movable = [i for i in range(number_of - 1) if given[i] < limit]
        pool, budget = sum([loads[i] for i in movable]), rest
        for i in movable:
            more = min(limit - given[i], max(1, budget * loads[i] // pool), rest)
            given[i] = given[i] + more
            rest = rest - more
    return np.array([limit] + given)


def ragged_sizes(key, number_of, total, reach, lean):
    if number_of == 2:
        one = jax.random.randint(key, (), max(1, total - reach), min(reach, total - 1) + 1)
        return jnp.stack([one, total - one])
    sizes = jnp.asarray(length_profile(number_of, total, reach, lean), jnp.int32)
    couples = (number_of - 1) // 2
    giver, receiver = sizes[1:1 + 2 * couples:2], sizes[2:2 + 2 * couples:2]
    room = jnp.minimum(giver - 1, reach - receiver)
    passed = jax.random.randint(jax.random.fold_in(key, 1), (couples,), 0, 1 << 20) % (room + 1)
    sizes = sizes.at[1:1 + 2 * couples:2].set(giver - passed).at[2:2 + 2 * couples:2].set(receiver + passed)
    return sizes[jax.random.permutation(jax.random.fold_in(key, 2), number_of)]


def scatter_about(own_key, shape, spread, most, split=(), held_as=jnp.bfloat16):
    level = level_of(own_key, shape, split, -0.22, 0.18) if split else 1.0
    values = jax.random.normal(own_key, shape, jnp.float32) * spread * level
    return jnp.minimum(jnp.maximum(values, -most), most).astype(held_as)


def setup_inputs(seed: int = 0) -> dict:
    streams_of = jax.random.split(jax.random.key(seed), 15)
    return {
        "ends_in": scatter_about(streams_of[0], (2, MICRO, SEQS, LEN, D), 1.0, 6.0, ((0, 2), (2, 4))),
        "segment_ids": jax.vmap(lambda own: jnp.searchsorted(jnp.cumsum(ragged_sizes(own, 4, LEN, LEN // 2, 1)), jnp.arange(LEN), side="right"))(jax.random.split(streams_of[1], MICRO * SEQS)).reshape((MICRO, SEQS, LEN)).astype(jnp.int32),
        "w_qkv": scatter_about(streams_of[2], (LAYERS, D, 3, D), D ** -0.5, 0.21875, ((0, 2), (3, 4))),
        "bias_qv": scatter_about(streams_of[3], (LAYERS, 2, D), 0.1, 0.59765625, ((0, 2), (2, 4))),
        "w_out": scatter_about(streams_of[4], (LAYERS, D, D), HEAD ** -0.5, 0.75, ((0, 2), (1, 4))),
        "bias_out": scatter_about(streams_of[5], (LAYERS, D), 0.1, 0.59765625, ((0, 2),)),
        "gain_one": jnp.clip(1.0 + 0.1 * jax.random.normal(streams_of[6], (LAYERS, D), jnp.float32), 0.5, 1.5).astype(jnp.bfloat16),
        "shift_one": scatter_about(streams_of[7], (LAYERS, D), 0.1, 0.59765625, ((0, 2),)),
        "w_up": scatter_about(streams_of[8], (LAYERS, D, FF), D ** -0.5, 0.21875, ((0, 2), (2, 4))),
        "bias_up": scatter_about(streams_of[9], (LAYERS, FF), 0.1, 0.59765625, ((0, 2), (1, 4))),
        "w_down": scatter_about(streams_of[10], (LAYERS, FF, D), FF ** -0.5, 0.109375, ((0, 2), (1, 4))),
        "bias_down": scatter_about(streams_of[11], (LAYERS, D), 0.1, 0.59765625, ((0, 2),)),
        "gain_two": jnp.clip(1.0 + 0.1 * jax.random.normal(streams_of[12], (LAYERS, D), jnp.float32), 0.5, 1.5).astype(jnp.bfloat16),
        "shift_two": scatter_about(streams_of[13], (LAYERS, D), 0.1, 0.59765625, ((0, 2),)),
    }


@jax.custom_vjp
def low(v):
    return lax.optimization_barrier(v.astype(jnp.bfloat16)).astype(jnp.float32)

@jax.custom_vjp
def low_back(v):
    return v

def low_keep(v):
    return (low(v), None)

def low_pass(kept, grad):
    return (grad,)

def back_keep(v):
    return (v, None)

def back_low(kept, grad):
    return (low(grad),)
low.defvjp(low_keep, low_pass)
low_back.defvjp(back_keep, back_low)
epsilon = 1e-05
highest = lax.Precision.HIGHEST

def norm(summed, gain, shift):
    center = summed - lax.optimization_barrier(jnp.mean(summed, -1, keepdims=True))
    inverse = lax.rsqrt(lax.optimization_barrier(jnp.mean(center * center, -1, keepdims=True)) + epsilon)
    return center * inverse * gain + shift

def layer(rows, segments, w_qkv, bias_qv, w_out, bias_out, gain_one, shift_one, w_up, bias_up, w_down, bias_down, gain_two, shift_two):
    count, length, width = rows.shape
    flat = rows.reshape(count * length, width)
    joined = jnp.concatenate([bias_qv[0], jnp.zeros_like(bias_qv[0]), bias_qv[1]])
    mixed = jnp.dot(low(flat), w_qkv.reshape(width, 3 * width), precision=highest) + joined
    mixed = low(low_back(mixed))
    parts = mixed.reshape(count, length, 3, width // HEAD, HEAD)
    query, keys, value = (parts[:, :, 0], parts[:, :, 1], parts[:, :, 2])
    scores = low_back(HEAD ** (-0.5) * jnp.einsum('sqhd,skhd->shqk', query, keys, precision=highest))
    same = segments[:, None, :, None] == segments[:, None, None, :]
    probs = jax.nn.softmax(jnp.where(same, scores, -1000000000.0), axis=-1)
    attended = jnp.einsum('shqk,skhd->sqhd', low(probs), value, precision=highest)
    attended = low(low_back(attended.reshape(count * length, width)))
    first = low_back(jnp.dot(attended, w_out, precision=highest)) + bias_out + flat
    hidden = norm(first, gain_one, shift_one)
    upward = low_back(jnp.dot(low(hidden), w_up, precision=highest) + bias_up)
    active = low(jax.nn.gelu(upward, approximate=False))
    second = low_back(jnp.dot(active, w_down, precision=highest)) + bias_down + hidden
    return norm(second, gain_two, shift_two).reshape(count, length, width)

def reference(ends_in, segment_ids, w_qkv, bias_qv, w_out, bias_out, gain_one, shift_one, w_up, bias_up, w_down, bias_down, gain_two, shift_two):
    weights = tuple((item.astype(jnp.float32) for item in (w_qkv, bias_qv, w_out, bias_out, gain_one, shift_one, w_up, bias_up, w_down, bias_down, gain_two, shift_two)))

    def both(rows, segments, params):
        middle = layer(rows, segments, *[item[0] for item in params])
        middle = low_back(low(middle))
        return layer(middle, segments, *[item[1] for item in params])

    def one_batch(totals, batch):
        rows, cotangent, segments = batch
        output, pullback = jax.vjp(lambda given, params: both(given, segments, params), rows.astype(jnp.float32), weights)
        grad_rows, grad_params = pullback(cotangent.astype(jnp.float32))
        totals = jax.tree.map(jnp.add, totals, grad_params)
        return (totals, (grad_rows, output))
    start = jax.tree.map(jnp.zeros_like, weights)
    totals, (grad_rows, outputs) = lax.scan(one_batch, start, (ends_in[0], ends_in[1], segment_ids))
    ends_out = jnp.stack([grad_rows, outputs])
    return (ends_out,) + tuple(totals)
```

```python
import jax
import jax.numpy as jnp
from jax import lax
from jax.sharding import PartitionSpec as P

HEAD = 64
epsilon = 1e-05
bf16 = jnp.bfloat16
f32 = jnp.float32


def to_partner(x, bits):
    size = lax.axis_size("tensor")
    return lax.ppermute(x, "tensor", [(i, i ^ bits) for i in range(size)])


def gather(x):
    near = to_partner(x, 1)
    far = to_partner(x, 2)
    return [x, near, far, to_partner(far, 1)]


def dot(left, right):
    return jnp.dot(left, right, preferred_element_type=f32)


def contract_rows(left, right):
    return lax.dot_general(left, right, (((0,), (0,)), ((), ())), preferred_element_type=f32)


def contract_cols(left, right):
    return lax.dot_general(left, right, (((1,), (1,)), ((), ())), preferred_element_type=f32)


def standardize(summed):
    center = summed - jnp.mean(summed, -1, keepdims=True)
    inverse = lax.rsqrt(jnp.mean(center * center, -1, keepdims=True) + epsilon)
    return (center * inverse, inverse)


def layer_norm(summed, gain, shift):
    normed, inverse = standardize(summed)
    return normed * gain + shift


def norm_back(summed, gain, grad_output):
    normed, inverse = standardize(summed)
    scaled = grad_output * gain
    grad_summed = inverse * (
        scaled
        - jnp.mean(scaled, -1, keepdims=True)
        - normed * jnp.mean(scaled * normed, -1, keepdims=True)
    )
    return normed, grad_summed


def gelu_value(value):
    return jax.nn.gelu(value, approximate=False)


def gelu_slope(value):
    normal_cdf = 0.5 * (1.0 + lax.erf(value * 0.7071067811865476))
    density = jnp.exp(-0.5 * value * value) * 0.3989422804014327
    return normal_cdf + value * density


def split_heads(mixed, segments):
    count, length = segments.shape
    width = mixed.shape[1] // 3
    parts = mixed.reshape(count, length, 3, width // HEAD, HEAD)
    return (parts[:, :, 0], parts[:, :, 1], parts[:, :, 2])


def probabilities(query, keys, segments):
    raw = jnp.einsum("sqhd,skhd->shqk", query, keys, preferred_element_type=f32) * HEAD**-0.5
    same = segments[:, None, :, None] == segments[:, None, None, :]
    return jax.nn.softmax(jnp.where(same, raw, -1000000000.0), axis=-1)


def attend(mixed, segments):
    query, keys, value = split_heads(mixed, segments)
    probs = probabilities(query, keys, segments).astype(bf16)
    result = jnp.einsum("shqk,skhd->sqhd", probs, value, preferred_element_type=f32)
    return result.astype(bf16).reshape(mixed.shape[0], -1)


def attend_back(mixed, segments, grad_result):
    query, keys, value = split_heads(mixed, segments)
    probs = probabilities(query, keys, segments)
    grad_heads = grad_result.reshape(query.shape)
    grad_probs = jnp.einsum("sqhd,skhd->shqk", grad_heads, value, preferred_element_type=f32)
    grad_value = jnp.einsum(
        "shqk,sqhd->skhd", probs.astype(bf16), grad_heads, preferred_element_type=f32
    )
    inner = jnp.sum(probs * grad_probs, -1, keepdims=True)
    grad_scores = (probs * (grad_probs - inner)).astype(bf16)
    scale = HEAD**-0.5
    grad_query = jnp.einsum("shqk,skhd->sqhd", grad_scores, keys, preferred_element_type=f32) * scale
    grad_keys = jnp.einsum("shqk,sqhd->skhd", grad_scores, query, preferred_element_type=f32) * scale
    stacked = jnp.stack([grad_query, grad_keys, grad_value], 2)
    return stacked.reshape(mixed.shape).astype(bf16)


def forward(rows, segments, w):
    mixed = [
        (dot(rows, w["qkv"][s]) + w["bias_mixed"][s]).astype(bf16) for s in range(4)
    ]
    attended = [attend(m, segments) for m in mixed]
    first = sum(dot(attended[s], w["out"][s]) for s in range(4)) + w["bias_out"] + rows.astype(f32)
    hidden = layer_norm(first, w["gain_one"], w["shift_one"])
    hidden_low = hidden.astype(bf16)
    upward = [dot(hidden_low, w["up"][s]) + w["bias_up"][s] for s in range(4)]
    second = sum(dot(gelu_value(upward[s]).astype(bf16), w["down"][s]) for s in range(4))
    second = second + w["bias_down"] + hidden
    out = layer_norm(second, w["gain_two"], w["shift_two"])
    return out, (rows, mixed, attended, first, hidden_low, upward, second)


def backward(grad_output, segments, kept, w, weights_too):
    rows, mixed, attended, first, hidden_low, upward, second = kept
    normed, grad_second = norm_back(second, w["gain_two"], grad_output)
    branch_two = grad_second.astype(bf16)
    grad_upward = [
        (contract_cols(branch_two, w["down"][s]) * gelu_slope(upward[s])).astype(bf16)
        for s in range(4)
    ]
    grad_hidden = sum(contract_cols(grad_upward[s], w["up"][s]) for s in range(4)) + grad_second
    normed_one, grad_first = norm_back(first, w["gain_one"], grad_hidden)
    branch_one = grad_first.astype(bf16)
    grad_mixed = [
        attend_back(mixed[s], segments, contract_cols(branch_one, w["out"][s]).astype(bf16))
        for s in range(4)
    ]
    grad_in = sum(contract_cols(grad_mixed[s], w["qkv"][s]) for s in range(4)) + grad_first
    if not weights_too:
        return grad_in
    common = [
        jnp.sum(grad_first, 0),
        jnp.sum(grad_hidden * normed_one, 0),
        jnp.sum(grad_hidden, 0),
        jnp.sum(grad_second, 0),
        jnp.sum(grad_output * normed, 0),
        jnp.sum(grad_output, 0),
    ]
    grads = []
    for s in range(4):
        width = attended[s].shape[1]
        from_mixed = jnp.sum(grad_mixed[s], 0, dtype=f32)
        from_qv = jnp.concatenate([from_mixed[:width], from_mixed[2 * width :]])
        from_qv = jnp.pad(from_qv, (0, rows.shape[1] - 2 * width))
        from_up = jnp.sum(grad_upward[s], 0, dtype=f32)
        grads.append(
            (
                contract_rows(gelu_value(upward[s]).astype(bf16), branch_two).astype(bf16),
                contract_rows(hidden_low, grad_upward[s]).astype(bf16),
                contract_rows(attended[s], branch_one).astype(bf16),
                contract_rows(rows, grad_mixed[s]).astype(bf16),
                jnp.stack([from_up, from_qv] + common),
            )
        )
    return grad_in, grads


def add(left, right):
    return (left.astype(f32) + right.astype(f32)).astype(left.dtype)


def sum_over_dp(part):
    return lax.psum(part, "dp")


def combine(parts):
    far = add(parts[2], to_partner(parts[3], 1))
    own = add(parts[0], to_partner(parts[1], 1))
    return sum_over_dp(add(own, to_partner(far, 2)))


def body(
    ends_in,
    segment_ids,
    w_qkv,
    bias_qv,
    w_out,
    bias_out,
    gain_one,
    shift_one,
    w_up,
    bias_up,
    w_down,
    bias_down,
    gain_two,
    shift_two,
):
    section = lax.axis_index("section")
    place = lax.axis_index("tensor")
    _, micro, count, length, width = ends_in.shape
    share = count // lax.axis_size("tensor")
    own = lax.dynamic_slice_in_dim(ends_in[0], place * share, share, 1)
    own = own.reshape(micro * share * length, width)
    segments = lax.dynamic_slice_in_dim(segment_ids, place * share, share, 1)
    segments = segments.reshape(micro * share, length)
    third = w_qkv.shape[3]
    biases = gather(jnp.concatenate([bias_qv[0, 0], bias_qv[0, 1], bias_up[0]])[None])
    biases = [b[0].astype(f32) for b in biases]
    none = jnp.zeros((third,), f32)
    w = {
        "qkv": gather(w_qkv[0].reshape(width, 3 * third)),
        "out": gather(w_out[0]),
        "up": gather(w_up[0]),
        "down": gather(w_down[0]),
        "bias_mixed": [jnp.concatenate([b[:third], none, b[third : 2 * third]]) for b in biases],
        "bias_up": [b[2 * third :] for b in biases],
        "bias_out": bias_out[0].astype(f32),
        "gain_one": gain_one[0].astype(f32),
        "shift_one": shift_one[0].astype(f32),
        "bias_down": bias_down[0].astype(f32),
        "gain_two": gain_two[0].astype(f32),
        "shift_two": shift_two[0].astype(f32),
    }
    out, _ = forward(own, segments, w)
    received = lax.ppermute(out.astype(bf16), "section", [(0, 1)])
    rows = jnp.where(section == 0, own, received)
    out, kept = forward(rows, segments, w)
    grad_in = backward(own.astype(f32), segments, kept, w, False)
    returned = lax.ppermute(grad_in.astype(bf16), "section", [(1, 0)])
    cotangent = jnp.where(section == 1, own, returned).astype(f32)
    grad_in, grads = backward(cotangent, segments, kept, w, True)

    down, up, outer, qkv, small = [
        combine([grads[s][i] for s in range(4)]) for i in range(5)
    ]
    ends = jnp.where(section == 1, out, grad_in).astype(bf16)
    ends = ends.reshape(micro, share, length, width)
    ends = lax.all_gather(ends, "tensor", axis=1, tiled=True)
    small = small.astype(f32)
    from_qv = jnp.stack([small[1, :third], small[1, third : 2 * third]])
    results = (
        ends,
        qkv.reshape(width, 3, third),
        from_qv,
        outer,
        small[2],
        small[3],
        small[4],
        up,
        small[0],
        down,
        small[5],
        small[6],
        small[7],
    )
    return tuple(item.astype(f32)[None] for item in results)


def solution(mesh):
    return jax.shard_map(
        body,
        mesh=mesh,
        in_specs=(
            P("section", None, "dp", None, None),
            P(None, "dp", None),
            P("section", None, None, "tensor"),
            P("section", None, "tensor"),
            P("section", "tensor", None),
            P("section", None),
            P("section", None),
            P("section", None),
            P("section", None, "tensor"),
            P("section", "tensor"),
            P("section", "tensor", None),
            P("section", None),
            P("section", None),
            P("section", None),
        ),
        out_specs=(
            P("section", None, "dp", None, None),
            P("section", None, None, "tensor"),
            P("section", None, "tensor"),
            P("section", "tensor", None),
            P("section", None),
            P("section", None),
            P("section", None),
            P("section", None, "tensor"),
            P("section", "tensor"),
            P("section", "tensor", None),
            P("section", None),
            P("section", None),
            P("section", None),
        ),
        check_vma=False,
    )
```

```python
import functools
import jax
import jax.numpy as jnp
from jax import lax
from jax.experimental import pallas as pl
from jax.experimental.pallas import tpu as pltpu
from jax.sharding import PartitionSpec as P

HEAD = 64
LEN = 128
SHARDS = 4
SMALL = 16
epsilon = 1e-05
bf16 = jnp.bfloat16
f32 = jnp.float32
ANY = pl.BlockSpec(memory_space=pl.ANY)
VM = pl.BlockSpec(memory_space=pltpu.VMEM)


def nn(left, right):
    return lax.dot_general(left, right, (((1,), (0,)), ((), ())), preferred_element_type=f32)


def nt(left, right):
    return lax.dot_general(left, right, (((1,), (1,)), ((), ())), preferred_element_type=f32)


def tn(left, right):
    return lax.dot_general(left, right, (((0,), (0,)), ((), ())), preferred_element_type=f32)


def standardize(summed):
    center = summed - jnp.mean(summed, -1, keepdims=True)
    inverse = lax.rsqrt(jnp.mean(center * center, -1, keepdims=True) + epsilon)
    return center * inverse, inverse


def norm_back(normed, inverse, gain, grad_output):
    scaled = grad_output * gain
    return inverse * (
        scaled
        - jnp.mean(scaled, -1, keepdims=True)
        - normed * jnp.mean(scaled * normed, -1, keepdims=True)
    )


def begin(sources, held, sems):
    copies = [
        pltpu.make_async_copy(src, held.at[i], sems.at[i]) for i, src in enumerate(sources)
    ]
    for copy in copies:
        copy.start()
    return copies


def attention_forward(keep, count, *refs):
    (rows, seg_row, seg_col, bias_mixed, bias_out, *rest) = refs
    qkv, rest = rest[:SHARDS], rest[SHARDS:]
    outer, rest = rest[:SHARDS], rest[SHARDS:]
    if keep:
        first, mixed_out, probs_out, att_out, held_qkv, held_out, sem_qkv, sem_out = rest
    else:
        first, held_qkv, held_out, sem_qkv, sem_out = rest
    load_qkv = begin(qkv, held_qkv, sem_qkv)
    load_out = begin(outer, held_out, sem_out)
    x = rows[...]
    first[...] = x.astype(f32) + bias_out[...]
    same = [seg_col[i] == seg_row[i] for i in range(count)]
    for s in range(SHARDS):
        load_qkv[s].wait()
        mixed = (nt(held_qkv[s], x) + bias_mixed[:, s : s + 1]).astype(bf16)
        if keep:
            mixed_out[s] = mixed
        width = mixed.shape[0] // 3
        heads = []
        for h in range(width // HEAD):
            lines = []
            for i in range(count):
                cols = slice(i * LEN, (i + 1) * LEN)
                at = h * HEAD
                query = mixed[at : at + HEAD, cols]
                keys = mixed[width + at : width + at + HEAD, cols]
                value = mixed[2 * width + at : 2 * width + at + HEAD, cols]
                scores = jnp.where(same[i], tn(keys, query) * HEAD**-0.5, -1e9)
                top = jnp.max(scores, 0, keepdims=True)
                probs = jnp.exp(scores - top)
                probs = probs / jnp.sum(probs, 0, keepdims=True)
                if keep:
                    probs_out[s, h, i] = probs
                lines.append(nn(value, probs.astype(bf16)).astype(bf16))
            heads.append(jnp.concatenate(lines, 1))
        attended = jnp.concatenate(heads, 0)
        if keep:
            att_out[s] = attended
        load_out[s].wait()
        first[...] += tn(attended, held_out[s])


def mlp_forward(keep, *refs):
    (first, gain_one, shift_one, gain_two, shift_two, bias_up, bias_down, *rest) = refs
    up, rest = rest[:SHARDS], rest[SHARDS:]
    down, rest = rest[:SHARDS], rest[SHARDS:]
    if keep:
        out, hidden_out, active_out, slope_out, second, held_up, held_down, sem_up, sem_down = rest
    else:
        out, second, held_up, held_down, sem_up, sem_down = rest
    load_up = begin(up, held_up, sem_up)
    load_down = begin(down, held_down, sem_down)
    normed, _ = standardize(first[...])
    hidden = normed * gain_one[...] + shift_one[...]
    hidden_low = hidden.astype(bf16)
    second[...] = hidden + bias_down[...]
    if keep:
        hidden_out[...] = hidden_low
    for s in range(SHARDS):
        load_up[s].wait()
        upward = nn(hidden_low, held_up[s]) + bias_up[s]
        normal = 0.5 * (1.0 + lax.erf(upward * 0.7071067811865476))
        active = (upward * normal).astype(bf16)
        if keep:
            density = jnp.exp(-0.5 * upward * upward) * 0.3989422804014327
            active_out[s] = active
            slope_out[s] = (normal + upward * density).astype(bf16)
        load_down[s].wait()
        second[...] += nn(active, held_down[s])
    normed, _ = standardize(second[...])
    out[...] = (normed * gain_two[...] + shift_two[...]).astype(bf16)


def store(parts, s, value):
    half = value.shape[0] // 2
    for i in range(2):
        parts[2 * i + s % 2][s // 2] = value[i * half : (i + 1) * half]


def down_grads(*refs):
    grad_output, second, gain_two, active, *parts, branch_two, grad_second, sums = refs
    g = grad_output[...].astype(f32)
    normed, inverse = standardize(second[...])
    back = norm_back(normed, inverse, gain_two[...], g)
    grad_second[...] = back
    low = back.astype(bf16)
    branch_two[...] = low
    sums[0:1] = jnp.sum(back, 0, keepdims=True)
    sums[1:2] = jnp.sum(g * normed, 0, keepdims=True)
    sums[2:3] = jnp.sum(g, 0, keepdims=True)
    for s in range(SHARDS):
        store(parts, s, tn(active[s], low).astype(bf16))


def mlp_backward(full, *refs):
    if full:
        branch_two, grad_second, slope, hidden_low, first, gain_one, *rest = refs
    else:
        grad_output, second, gain_two, slope, first, gain_one, *rest = refs
    up, rest = rest[:SHARDS], rest[SHARDS:]
    down, rest = rest[:SHARDS], rest[SHARDS:]
    if full:
        *parts, grad_bias_up, grad_first, branch_one, sums = rest[:8]
        rest = rest[8:]
    else:
        grad_first, branch_one, *rest = rest
    total, held_up, held_down, sem_up, sem_down = rest
    load_down = begin(down, held_down, sem_down)
    load_up = begin(up, held_up, sem_up)
    if full:
        low = branch_two[...]
        total[...] = grad_second[...]
        x = hidden_low[...]
    else:
        normed, inverse = standardize(second[...])
        back = norm_back(normed, inverse, gain_two[...], grad_output[...].astype(f32))
        low = back.astype(bf16)
        total[...] = back
    for s in range(SHARDS):
        load_down[s].wait()
        grad_upward = (nt(low, held_down[s]) * slope[s].astype(f32)).astype(bf16)
        if full:
            store(parts, s, tn(x, grad_upward).astype(bf16))
            grad_bias_up[s] = jnp.sum(grad_upward.astype(f32), 0, keepdims=True)
        load_up[s].wait()
        total[...] += nt(grad_upward, held_up[s])
    grad_hidden = total[...]
    normed, inverse = standardize(first[...])
    back = norm_back(normed, inverse, gain_one[...], grad_hidden)
    grad_first[...] = back
    branch_one[...] = back.astype(bf16)
    if full:
        sums[0:1] = jnp.sum(back, 0, keepdims=True)
        sums[1:2] = jnp.sum(grad_hidden * normed, 0, keepdims=True)
        sums[2:3] = jnp.sum(grad_hidden, 0, keepdims=True)


def attention_backward(full, count, *refs):
    branch_one, grad_first, mixed_in, probs_in, *rest = refs
    if full:
        rows, attended, sums_two, sums_one, grad_bias_up, *rest = rest
    qkv, rest = rest[:SHARDS], rest[SHARDS:]
    outer, rest = rest[:SHARDS], rest[SHARDS:]
    if full:
        grad_in, *parts = rest[:5]
        rest = rest[5:]
        ones = jnp.ones((16, rows.shape[0]), bf16)
    else:
        grad_in, *rest = rest
    total, held_qkv, held_out, sem_qkv, sem_out = rest
    load_out = begin(outer, held_out, sem_out)
    load_qkv = begin(qkv, held_qkv, sem_qkv)
    branch = branch_one[...]
    total[...] = grad_first[...]
    scale = HEAD**-0.5
    for s in range(SHARDS):
        load_out[s].wait()
        if full:
            parts[s % 2][s // 2, : attended.shape[1]] = nn(attended[s], branch).astype(bf16)
        grad_att = nt(held_out[s], branch).astype(bf16)
        width = grad_att.shape[0]
        pieces = ([], [], [])
        for h in range(width // HEAD):
            lines = ([], [], [])
            for i in range(count):
                cols = slice(i * LEN, (i + 1) * LEN)
                at = h * HEAD
                query = mixed_in[s, at : at + HEAD, cols]
                keys = mixed_in[s, width + at : width + at + HEAD, cols]
                value = mixed_in[s, 2 * width + at : 2 * width + at + HEAD, cols]
                probs = probs_in[s, h, i]
                grad_head = grad_att[at : at + HEAD, cols]
                grad_probs = tn(value, grad_head)
                lines[2].append(nt(grad_head, probs.astype(bf16)).astype(bf16))
                inner = jnp.sum(probs * grad_probs, 0, keepdims=True)
                grad_scores = (probs * (grad_probs - inner)).astype(bf16)
                lines[0].append((nn(keys, grad_scores) * scale).astype(bf16))
                lines[1].append((nt(query, grad_scores) * scale).astype(bf16))
            for piece, line in zip(pieces, lines):
                piece.append(jnp.concatenate(line, 1))
        grad_mixed = jnp.concatenate([p for piece in pieces for p in piece], 0)
        load_qkv[s].wait()
        if full:
            grad_qkv = nn(grad_mixed, rows[...]).astype(bf16)
            parts[s % 2][s // 2, width:] = grad_qkv[:width]
            last = parts[2 + s % 2]
            last[s // 2, : 2 * width] = grad_qkv[width:]
            columns = nt(ones, grad_mixed)
            blank = jnp.zeros((1, last.shape[2] - width), f32)
            small = [
                grad_bias_up[s],
                jnp.concatenate([columns[:1, :width], blank], 1),
                jnp.concatenate([columns[:1, 2 * width :], blank], 1),
                sums_two[...],
                sums_one[...],
                jnp.zeros((SMALL - 9, last.shape[2]), f32),
            ]
            last[s // 2, 2 * width :] = jnp.concatenate(small, 0).astype(bf16)
        total[...] += tn(grad_mixed, held_qkv[s])
    grad_in[...] = total[...].astype(bf16)


def shape(dims, dtype):
    return jax.ShapeDtypeStruct(dims, dtype)


def launch(kernel, name, operands, weights, outputs, scratch):
    many = len(weights)
    return pl.pallas_call(
        kernel,
        name=name,
        out_shape=outputs,
        in_specs=[VM] * len(operands) + [ANY] * many,
        out_specs=[VM] * len(outputs),
        scratch_shapes=list(scratch)
        + [pltpu.VMEM((SHARDS,) + weights[i].shape, bf16) for i in range(0, many, SHARDS)]
        + [pltpu.SemaphoreType.DMA((SHARDS,)) for _ in range(0, many, SHARDS)],
        compiler_params=pltpu.CompilerParams(vmem_limit_bytes=56 << 20),
    )(*operands, *weights)


def run_attention_forward(keep, rows, seg, w):
    size, width = rows.shape
    third, count = w["out"][0].shape[0], size // LEN
    outputs = [shape((size, width), f32)]
    if keep:
        outputs += [
            shape((SHARDS, 3 * third, size), bf16),
            shape((SHARDS, third // HEAD, count, LEN, LEN), f32),
            shape((SHARDS, third, size), bf16),
        ]
    return launch(
        functools.partial(attention_forward, keep, count),
        "attention_forward",
        [rows, *seg, w["bias_mixed"], w["bias_out"]],
        w["qkv"] + w["out"],
        outputs,
        [],
    )


def run_mlp_forward(keep, first, w):
    size, width = first.shape
    units = w["up"][0].shape[1]
    outputs = [shape((size, width), bf16)]
    if keep:
        outputs += [
            shape((size, width), bf16),
            shape((SHARDS, size, units), bf16),
            shape((SHARDS, size, units), bf16),
            shape((size, width), f32),
        ]
    return launch(
        functools.partial(mlp_forward, keep),
        "mlp_forward",
        [first, w["gain_one"], w["shift_one"], w["gain_two"], w["shift_two"], w["bias_up"], w["bias_down"]],
        w["up"] + w["down"],
        outputs,
        [] if keep else [pltpu.VMEM((size, width), f32)],
    )


def run_down_grads(grad_output, second, active, w):
    size, width = second.shape
    units = active.shape[2]
    return launch(
        down_grads,
        "down_grads",
        [grad_output, second, w["gain_two"], active],
        [],
        [
            *[shape((SHARDS // 2, units // 2, width), bf16)] * 4,
            shape((size, width), bf16),
            shape((size, width), f32),
            shape((3, width), f32),
        ],
        [],
    )


def run_mlp_backward(full, operands, w):
    units = w["up"][0].shape[1]
    size, width = operands[0].shape
    outputs = [shape((size, width), f32), shape((size, width), bf16)]
    if full:
        outputs = [
            *[shape((SHARDS // 2, width // 2, units), bf16)] * 4,
            shape((SHARDS, 1, units), f32),
            *outputs,
            shape((3, width), f32),
        ]
    return launch(
        functools.partial(mlp_backward, full),
        "mlp_backward",
        operands,
        w["up"] + w["down"],
        outputs,
        [pltpu.VMEM((size, width), f32)],
    )


def run_attention_backward(full, operands, w):
    size, width = operands[0].shape
    third = w["out"][0].shape[0]
    outputs = [shape((size, width), bf16)]
    if full:
        outputs += [
            *[shape((SHARDS // 2, 2 * third, width), bf16)] * 2,
            *[shape((SHARDS // 2, 2 * third + SMALL, width), bf16)] * 2,
        ]
    return launch(
        functools.partial(attention_backward, full, size // LEN),
        "attention_backward",
        operands,
        w["qkv"] + w["out"],
        outputs,
        [pltpu.VMEM((size, width), f32)],
    )


def to_partner(x, bits):
    size = lax.axis_size("tensor")
    return lax.ppermute(x, "tensor", [(i, i ^ bits) for i in range(size)])


def gather(x):
    near = to_partner(x, 1)
    far = to_partner(x, 2)
    return [x, near, far, to_partner(far, 1)]


def add(*items):
    return sum(item.astype(f32) for item in items).astype(bf16)


def over_dp(part):
    size = lax.axis_size("dp")
    if size != 4:
        return lax.psum(part, "dp")
    pair = add(part, lax.ppermute(part, "dp", [(0, 1), (3, 2)]))
    total = add(pair, lax.ppermute(pair, "dp", [(1, 2), (2, 1)]))
    back = lax.ppermute(total, "dp", [(1, 0), (2, 3)])
    place = lax.axis_index("dp")
    return jnp.where((place == 1) | (place == 2), total, back)


def over_devices(keep, send):
    near = to_partner(send, 1)
    far = to_partner(add(keep[1], near[1]), 2)
    return over_dp(add(keep[0], near[0], far))


def all_rows(own):
    place = lax.axis_index("tensor")
    low, high = place % 2 == 1, place // 2 == 1
    own, near, far, both = gather(own)
    first = [jnp.where(low, near, own), jnp.where(low, own, near)]
    second = [jnp.where(low, both, far), jnp.where(low, far, both)]
    return [jnp.where(high, b, a) for a, b in zip(first, second)] + [
        jnp.where(high, a, b) for a, b in zip(first, second)
    ]


def body(
    ends_in,
    segment_ids,
    w_qkv,
    bias_qv,
    w_out,
    bias_out,
    gain_one,
    shift_one,
    w_up,
    bias_up,
    w_down,
    bias_down,
    gain_two,
    shift_two,
):
    section = lax.axis_index("section")
    place = lax.axis_index("tensor")
    _, micro, count, length, width = ends_in.shape
    share = count // lax.axis_size("tensor")
    own = lax.dynamic_slice_in_dim(ends_in[0], place * share, share, 1)
    own = own.reshape(micro * share * length, width)
    segments = lax.dynamic_slice_in_dim(segment_ids, place * share, share, 1)
    segments = segments.reshape(micro * share, length)
    seg = (segments[:, None, :], segments[:, :, None])
    third = w_qkv.shape[3]
    biases = gather(jnp.concatenate([bias_qv[0, 0], bias_qv[0, 1], bias_up[0]])[None])
    biases = jnp.concatenate(biases, 0).astype(f32)
    none = jnp.zeros((SHARDS, third), f32)
    w = {
        "qkv": gather(w_qkv[0].reshape(width, 3 * third).T),
        "out": gather(w_out[0]),
        "up": gather(w_up[0]),
        "down": gather(w_down[0]),
        "bias_mixed": jnp.concatenate([biases[:, :third], none, biases[:, third : 2 * third]], 1).T,
        "bias_up": biases[:, None, 2 * third :],
        "bias_out": bias_out.astype(f32),
        "gain_one": gain_one.astype(f32),
        "shift_one": shift_one.astype(f32),
        "bias_down": bias_down.astype(f32),
        "gain_two": gain_two.astype(f32),
        "shift_two": shift_two.astype(f32),
    }
    (first,) = run_attention_forward(False, own, seg, w)
    (out,) = run_mlp_forward(False, first, w)
    received = lax.ppermute(out, "section", [(0, 1)])
    rows = jnp.where(section == 0, own, received)
    first, mixed, probs, attended = run_attention_forward(True, rows, seg, w)
    out, hidden, active, slope, second = run_mlp_forward(True, first, w)
    grad_first, branch_one = run_mlp_backward(
        False, [own, second, w["gain_two"], slope, first, w["gain_one"]], w
    )
    (grad_in,) = run_attention_backward(False, [branch_one, grad_first, mixed, probs], w)
    returned = lax.ppermute(grad_in, "section", [(1, 0)])
    cotangent = jnp.where(section == 1, own, returned)

    *parts, branch_two, grad_second, sums_two = run_down_grads(cotangent, second, active, w)
    down = [over_devices(*parts[:2]), over_devices(*parts[2:])]
    *parts, grad_bias_up, grad_first, branch_one, sums_one = run_mlp_backward(
        True, [branch_two, grad_second, slope, hidden, first, w["gain_one"]], w
    )
    up = [over_devices(*parts[:2]), over_devices(*parts[2:])]
    grad_in, *parts = run_attention_backward(
        True,
        [branch_one, grad_first, mixed, probs, rows, attended, sums_two, sums_one, grad_bias_up],
        w,
    )
    mixer = [over_devices(*parts[:2]), over_devices(*parts[2:])]
    ends = all_rows(jnp.where(section == 1, out, grad_in).reshape(micro, share, length, width))
    qkv = jnp.concatenate([mixer[0][third:], mixer[1][: 2 * third]], 0)
    small = mixer[1][2 * third :]
    results = (
        jnp.concatenate(ends, 1),
        qkv.T.reshape(width, 3, third),
        small[1:3, :third],
        mixer[0][:third],
        small[6],
        small[7],
        small[8],
        jnp.concatenate(up, 0),
        small[0],
        jnp.concatenate(down, 0),
        small[3],
        small[4],
        small[5],
    )
    return tuple(item.astype(f32)[None] for item in results)


def solution(mesh):
    return jax.shard_map(
        body,
        mesh=mesh,
        in_specs=(
            P("section", None, "dp", None, None),
            P(None, "dp", None),
            P("section", None, None, "tensor"),
            P("section", None, "tensor"),
            P("section", "tensor", None),
            P("section", None),
            P("section", None),
            P("section", None),
            P("section", None, "tensor"),
            P("section", "tensor"),
            P("section", "tensor", None),
            P("section", None),
            P("section", None),
            P("section", None),
        ),
        out_specs=(
            P("section", None, "dp", None, None),
            P("section", None, None, "tensor"),
            P("section", None, "tensor"),
            P("section", "tensor", None),
            P("section", None),
            P("section", None),
            P("section", None),
            P("section", None, "tensor"),
            P("section", "tensor"),
            P("section", "tensor", None),
            P("section", None),
            P("section", None),
            P("section", None),
        ),
        check_vma=False,
    )
```

```python
import functools
import jax
import jax.numpy as jnp
from jax import lax
from jax.experimental import pallas as pl
from jax.experimental.pallas import tpu as pltpu
from jax.sharding import PartitionSpec as P

HEAD = 64
LEN = 128
SHARDS = 4
SMALL = 16
NEAR_PAIR, FAR_PAIR, ALL = (0, 1), (2, 3), (0, 1, 2, 3)
epsilon = 1e-05
bf16 = jnp.bfloat16
f32 = jnp.float32
ANY = pl.BlockSpec(memory_space=pl.ANY)
VM = pl.BlockSpec(memory_space=pltpu.VMEM)
SM = pl.BlockSpec(memory_space=pltpu.SMEM)


def nn(left, right):
    return lax.dot_general(left, right, (((1,), (0,)), ((), ())), preferred_element_type=f32)


def nt(left, right):
    return lax.dot_general(left, right, (((1,), (1,)), ((), ())), preferred_element_type=f32)


def tn(left, right):
    return lax.dot_general(left, right, (((0,), (0,)), ((), ())), preferred_element_type=f32)


def standardize(summed):
    center = summed - jnp.mean(summed, -1, keepdims=True)
    inverse = lax.rsqrt(jnp.mean(center * center, -1, keepdims=True) + epsilon)
    return center * inverse, inverse


def norm_back(normed, inverse, gain, grad_output):
    scaled = grad_output * gain
    return inverse * (
        scaled
        - jnp.mean(scaled, -1, keepdims=True)
        - normed * jnp.mean(scaled * normed, -1, keepdims=True)
    )


def wide(ref):
    return ref[...].astype(f32)


def load(sources, held, sems):
    copies = [
        pltpu.make_async_copy(src, held.at[n], sems.at[n]) for n, src in enumerate(sources)
    ]
    for copy in copies:
        copy.start()
    return copies


def load_mlp(kinds, refs, rotation, held_up, held_down, sems, up_first):
    refs = list(refs)
    ups, downs = [], []
    for n, kind in enumerate(kinds):
        first = refs.pop(0)
        half = first.shape[0]
        up = [pltpu.make_async_copy(first, held_up.at[n, pl.ds(0, half)], sems.at[n, 0])]
        down = []
        if kind == 1:
            down.append(pltpu.make_async_copy(refs.pop(0), held_down.at[n], sems.at[n, 1]))
        else:
            size = held_down.shape[1] // kind
            rest = (held_up.shape[1] - half) // kind
            for turn in range(kind):
                piece = refs.pop(0)
                place = lax.rem(rotation[0] + (kind - turn), kind)
                at = pl.ds(pl.multiple_of(place * size, 16), size)
                down.append(
                    pltpu.make_async_copy(
                        piece.at[pl.ds(0, size)], held_down.at[n, at], sems.at[n, 1 + turn]
                    )
                )
                at = pl.ds(pl.multiple_of(half + place * rest, 16), rest)
                up.append(
                    pltpu.make_async_copy(
                        piece.at[pl.ds(size, rest)], held_up.at[n, at], sems.at[n, 1 + kind + turn]
                    )
                )
        for copy in up + down if up_first else down + up:
            copy.start()
        ups.append(up)
        downs.append(down)
    return ups, downs


def wait(copies):
    for copy in copies:
        copy.wait()


def by_sequence(count, value):
    return jnp.concatenate([value(slice(i * LEN, (i + 1) * LEN)) for i in range(count)], 1)


def attention_forward(which, more, keep, *refs):
    rows, segments, start, *rest = refs
    count = segments.shape[0]
    many = len(which)
    mixers, rest = rest[:many], rest[many:]
    if keep:
        first, mixed_out, probs_out, att_out, held, sems = rest
    else:
        first, held, sems = rest
    copies = load(mixers, held, sems)
    x = rows[...]
    first[...] = start[...] if more else x.astype(f32) + wide(start)
    ids = segments[...].astype(f32)
    ids_down = jnp.concatenate([ids, jnp.zeros((8 - count, LEN), f32)], 0).T
    same = jnp.concatenate([ids_down[:, i : i + 1] == ids[i : i + 1] for i in range(count)], 1)
    for n in range(many):
        copies[n].wait()
        third = (held.shape[1] - SMALL) // 4
        bias = held[n, 4 * third :].astype(f32)[:8].T[: 3 * third, :1]
        mixed = (nt(held[n, : 3 * third], x) + bias).astype(bf16)
        query, keys, value = mixed[:third] * HEAD**-0.5, mixed[third : 2 * third], mixed[2 * third :]
        if keep:
            mixed_out[n, :third] = query
            mixed_out[n, third:] = mixed[third:]
        heads = []
        for h in range(third // HEAD):
            at = slice(h * HEAD, (h + 1) * HEAD)
            scores = by_sequence(count, lambda cols: tn(keys[at, cols], query[at, cols]))
            scores = jnp.where(same, scores, -1e9)
            probs = jnp.exp(scores - jnp.max(scores, 0, keepdims=True))
            probs = probs * (1.0 / jnp.sum(probs, 0, keepdims=True))
            if keep:
                probs_out[n, h] = probs
            low = probs.astype(bf16)
            heads.append(by_sequence(count, lambda cols: nn(value[at, cols], low[:, cols])))
        attended = jnp.concatenate(heads, 0).astype(bf16)
        if keep:
            att_out[n] = attended
        first[...] += tn(attended, held[n, 3 * third : 4 * third])


def mlp_forward(kinds, more, last, keep, *refs):
    rotation, first, gain_one, shift_one, gain_two, shift_two, bias_down, *rest = refs
    if more:
        start, *rest = rest
    many = len(kinds)
    *rest, held_up, held_down, held_tail, sems, sem_tail = rest
    outs = 5 if keep else 2 if last else 1
    rest, outs = rest[:-outs], rest[-outs:]
    mixers, weights = rest[:many], rest[many:]
    edge = mixers[0].shape[0] - SMALL
    tails = load([item.at[pl.ds(edge, SMALL)] for item in mixers], held_tail, sem_tail)
    ups, downs = load_mlp(kinds, weights, rotation, held_up, held_down, sems, True)
    second = outs[-1]
    normed, _ = standardize(first[...])
    hidden = normed * wide(gain_one) + wide(shift_one)
    hidden_low = hidden.astype(bf16)
    second[...] = start[...] if more else hidden + wide(bias_down)
    if keep:
        out, hidden_out, active_out, slope_out, _ = outs
        hidden_out[...] = hidden_low
    wait(tails)
    for n in range(many):
        wait(ups[n])
        upward = nn(hidden_low, held_up[n]) + held_tail[n].astype(f32)[1:2]
        normal = 0.5 * (1.0 + lax.erf(upward * 0.7071067811865476))
        active = (upward * normal).astype(bf16)
        if keep:
            density = jnp.exp(-0.5 * upward * upward) * 0.3989422804014327
            active_out[n] = active
            slope_out[n] = (normal + upward * density).astype(bf16)
        wait(downs[n])
        second[...] += nn(active, held_down[n])
    if last:
        normed, _ = standardize(second[...])
        outs[0][...] = (normed * wide(gain_two) + wide(shift_two)).astype(bf16)


def down_grads(which, *refs):
    if which == FAR_PAIR:
        grad_output, second, gain_two, active, *parts, branch_two, grad_second, sums = refs
        g = wide(grad_output)
        normed, inverse = standardize(second[...])
        back = norm_back(normed, inverse, wide(gain_two), g)
        grad_second[...] = back
        low = back.astype(bf16)
        branch_two[...] = low
        sums[0:1] = jnp.sum(back, 0, keepdims=True)
        sums[1:2] = jnp.sum(g * normed, 0, keepdims=True)
        sums[2:3] = jnp.sum(g, 0, keepdims=True)
    else:
        branch_two, active, *parts = refs
        low = branch_two[...]
    for n, s in enumerate(which):
        parts[n][...] = tn(active[s], low).astype(bf16)


def mlp_backward(which, kinds, last, full, *refs):
    if full:
        rotation, branch_two, start, slope, hidden_low, first, gain_one, *rest = refs
    else:
        rotation, grad_output, second, gain_two, slope, first, gain_one, *rest = refs
    *rest, held_up, held_down, sems = rest
    many = len(which)
    ins = sum(1 + kind for kind in kinds)
    weights, rest = rest[:ins], rest[ins:]
    ups, downs = load_mlp(kinds, weights, rotation, held_up, held_down, sems, False)
    if full:
        parts, grad_bias_up, rest = rest[:many], rest[many], rest[many + 1 :]
    if last:
        grad_first, branch_one, *rest = rest
        sums = rest[0] if full else None
    total = rest[-1]
    if full:
        low = branch_two[...]
        total[...] = start[...]
        x = hidden_low[...]
    else:
        normed, inverse = standardize(second[...])
        back = norm_back(normed, inverse, wide(gain_two), wide(grad_output))
        low = back.astype(bf16)
        total[...] = back
    for n, s in enumerate(which):
        wait(downs[n])
        grad_upward = (nt(low, held_down[n]) * slope[s].astype(f32)).astype(bf16)
        if full:
            parts[n][...] = tn(x, grad_upward).astype(bf16)
            grad_bias_up[n] = jnp.sum(grad_upward.astype(f32), 0, keepdims=True)
        wait(ups[n])
        total[...] += nt(grad_upward, held_up[n])
    if not last:
        return
    grad_hidden = total[...]
    normed, inverse = standardize(first[...])
    back = norm_back(normed, inverse, wide(gain_one), grad_hidden)
    grad_first[...] = back
    branch_one[...] = back.astype(bf16)
    if full:
        sums[0:1] = jnp.sum(back, 0, keepdims=True)
        sums[1:2] = jnp.sum(grad_hidden * normed, 0, keepdims=True)
        sums[2:3] = jnp.sum(grad_hidden, 0, keepdims=True)


def attention_backward(which, last, full, count, *refs):
    branch_one, start, mixed_in, probs_in, *rest = refs
    if full:
        rows, attended, sums_two, sums_one, grad_bias_up, *rest = rest
        ones = jnp.ones((16, rows.shape[0]), bf16)
    many = len(which)
    *rest, held, sems = rest
    mixers, rest = rest[:many], rest[many:]
    copies = load(mixers, held, sems)
    total = rest[-1]
    if full:
        parts = rest[:many]
    if last:
        grad_in = rest[-2]
    branch = branch_one[...]
    total[...] = start[...]
    scale = HEAD**-0.5
    for n, s in enumerate(which):
        copies[n].wait()
        third = (held.shape[1] - SMALL) // 4
        if full:
            parts[n][:third] = nn(attended[s], branch).astype(bf16)
        grad_att = nt(held[n, 3 * third : 4 * third], branch).astype(bf16)
        pieces = ([], [], [])
        for h in range(third // HEAD):
            at = slice(h * HEAD, (h + 1) * HEAD)
            query = mixed_in[s, at]
            keys = mixed_in[s, third + at.start : third + at.stop]
            value = mixed_in[s, 2 * third + at.start : 2 * third + at.stop]
            probs = probs_in[s, h]
            low = probs.astype(bf16)
            grads = grad_att[at]
            grad_probs = by_sequence(count, lambda cols: tn(value[:, cols], grads[:, cols]))
            inner = jnp.sum(probs * grad_probs, 0, keepdims=True)
            grad_scores = (probs * (grad_probs - inner)).astype(bf16)
            pieces[0].append(
                by_sequence(count, lambda cols: nn(keys[:, cols], grad_scores[:, cols])) * scale
            )
            pieces[1].append(
                by_sequence(count, lambda cols: nt(query[:, cols], grad_scores[:, cols]))
            )
            pieces[2].append(by_sequence(count, lambda cols: nt(grads[:, cols], low[:, cols])))
        grad_mixed = jnp.concatenate([p for piece in pieces for p in piece], 0).astype(bf16)
        if full:
            parts[n][third : 4 * third] = nn(grad_mixed, rows[...]).astype(bf16)
            columns = nt(ones, grad_mixed)
            blank = jnp.zeros((1, rows.shape[1] - third), f32)
            small = [
                grad_bias_up[n],
                jnp.concatenate([columns[:1, :third], blank], 1),
                jnp.concatenate([columns[:1, 2 * third :], blank], 1),
                sums_two[...],
                sums_one[...],
                jnp.zeros((SMALL - 9, rows.shape[1]), f32),
            ]
            parts[n][4 * third :] = jnp.concatenate(small, 0).astype(bf16)
        total[...] += tn(grad_mixed, held[n, : 3 * third])
    if last:
        grad_in[...] = total[...].astype(bf16)


def pack(count, rotation, bias_qv, bias_up, qkv, outer, up, down, *refs):
    third = outer.shape[0]
    mixer, *refs = refs
    copies = [
        (qkv, mixer.at[pl.ds(0, 3 * third)]),
        (outer, mixer.at[pl.ds(3 * third, third)]),
    ]
    if count > 1:
        piece, *refs = refs
        size, half = down.shape[0] // count, up.shape[0] // 2
        part = half // count
        at = pl.multiple_of(rotation[0] * size, 16)
        copies.append((down.at[pl.ds(at, size)], piece.at[pl.ds(0, size)]))
        at = pl.multiple_of(half + rotation[0] * part, 16)
        copies.append((up.at[pl.ds(at, part)], piece.at[pl.ds(size, part)]))
    copies = [pltpu.make_async_copy(*pair, refs[0].at[n]) for n, pair in enumerate(copies)]
    for copy in copies:
        copy.start()
    none = jnp.zeros((1, third), f32)
    biases = jnp.concatenate([wide(bias_qv)[:1], none, wide(bias_qv)[1:], none], 1)
    rest = jnp.zeros((SMALL - 2, biases.shape[1]), f32)
    mixer[4 * third :] = jnp.concatenate([biases, wide(bias_up), rest], 0).astype(bf16)
    wait(copies)


def run_pack(count, rotation, bias_qv, bias_up, qkv, outer, up, down):
    third, width = outer.shape
    outputs = [shape((4 * third + SMALL, width), bf16)]
    if count > 1:
        outputs += [shape((down.shape[0] // count + up.shape[0] // 2 // count, width), bf16)]
    return pl.pallas_call(
        functools.partial(pack, count),
        name="pack",
        out_shape=outputs,
        in_specs=[SM, VM, VM, ANY, ANY, ANY, ANY],
        out_specs=[VM] * len(outputs),
        scratch_shapes=[pltpu.SemaphoreType.DMA((4,))],
    )(rotation, bias_qv, bias_up, qkv, outer, up, down)


def shape(dims, dtype):
    return jax.ShapeDtypeStruct(dims, dtype)


def launch(kernel, name, operands, weights, outputs, scratch, flops, scalars=0):
    size = sum(item.size * item.dtype.itemsize for item in [*operands, *weights, *outputs])
    return pl.pallas_call(
        kernel,
        name=name,
        out_shape=outputs,
        in_specs=[SM] * scalars + [VM] * (len(operands) - scalars) + [ANY] * len(weights),
        out_specs=[VM] * len(outputs),
        scratch_shapes=scratch,
        compiler_params=pltpu.CompilerParams(vmem_limit_bytes=56 << 20),
        cost_estimate=pl.CostEstimate(flops=flops, bytes_accessed=size, transcendentals=0),
    )(*operands, *weights)


def mixer_scratch(many, mixer):
    return [pltpu.VMEM((many,) + mixer.shape, bf16), pltpu.SemaphoreType.DMA((many,))]


def mlp_scratch(w, which):
    size = w["mlp"][0][0].shape
    most = max(len(w["mlp"][s]) - 1 for s in which)
    return [
        pltpu.VMEM((len(which),) + size, bf16),
        pltpu.VMEM((len(which),) + size[::-1], bf16),
        pltpu.SemaphoreType.DMA((len(which), 1 + 2 * most)),
    ]


def kinds_of(w, which):
    return tuple(len(w["mlp"][s]) - 1 for s in which)


def take(items, which):
    return [items[s] for s in which]


def flat(items, which):
    return [item for s in which for item in items[s]]


def run_attention_forward(which, keep, rows, segments, w, start=None):
    size, width = rows.shape
    many = len(which)
    third = (w["mix"][0].shape[0] - SMALL) // 4
    outputs = [shape((size, width), f32)]
    if keep:
        outputs += [
            shape((many, 3 * third, size), bf16),
            shape((many, third // HEAD, LEN, size), f32),
            shape((many, third, size), bf16),
        ]
    more = start is not None
    return launch(
        functools.partial(attention_forward, which, more, keep),
        "attention_forward",
        [rows, segments, start if more else w["bias_out"]],
        take(w["mix"], which),
        outputs,
        mixer_scratch(many, w["mix"][0]),
        8 * many * size * third * width,
    )


def run_mlp_forward(which, last, keep, first, w, start=None):
    size, width = first.shape
    units, many = w["mlp"][0][0].shape[1], len(which)
    outputs = [shape((size, width), bf16)] if last else []
    if keep:
        outputs += [
            shape((size, width), bf16),
            shape((many, size, units), bf16),
            shape((many, size, units), bf16),
        ]
    outputs += [shape((size, width), f32)]
    names = ("gain_one", "shift_one", "gain_two", "shift_two", "bias_down")
    operands = [w["rotation"], first, *[w[name] for name in names]]
    more = start is not None
    if more:
        operands += [start]
    held_up, held_down, sems = mlp_scratch(w, which)
    return launch(
        functools.partial(mlp_forward, kinds_of(w, which), more, last, keep),
        "mlp_forward",
        operands,
        take(w["mix"], which) + flat(w["mlp"], which),
        outputs,
        [
            held_up,
            held_down,
            pltpu.VMEM((many, SMALL, width), bf16),
            sems,
            pltpu.SemaphoreType.DMA((many,)),
        ],
        4 * many * size * units * width,
        1,
    )


def run_down_grads(which, operands):
    size, width = operands[0].shape
    units = operands[-1].shape[2]
    outputs = [shape((units, width), bf16)] * len(which)
    if which == FAR_PAIR:
        outputs += [shape((size, width), bf16), shape((size, width), f32), shape((3, width), f32)]
    return launch(
        functools.partial(down_grads, which),
        "down_grads",
        operands,
        [],
        outputs,
        [],
        4 * size * units * width,
    )


def run_mlp_backward(which, last, full, operands, w):
    units, many = w["mlp"][0][0].shape[1], len(which)
    size, width = operands[0].shape
    outputs = []
    if full:
        outputs = [shape((width, units), bf16)] * many + [shape((many, 1, units), f32)]
    if last:
        outputs += [shape((size, width), f32), shape((size, width), bf16)]
        if full:
            outputs += [shape((3, width), f32)]
    outputs += [shape((size, width), f32)]
    return launch(
        functools.partial(mlp_backward, which, kinds_of(w, which), last, full),
        "mlp_backward",
        [w["rotation"], *operands],
        flat(w["mlp"], which),
        outputs,
        mlp_scratch(w, which),
        (6 if full else 4) * many * size * units * width,
        1,
    )


def run_attention_backward(which, last, full, operands, w):
    size, width = operands[0].shape
    many = len(which)
    third = (w["mix"][0].shape[0] - SMALL) // 4
    outputs = []
    if full:
        outputs = [shape((4 * third + SMALL, width), bf16)] * many
    if last:
        outputs += [shape((size, width), bf16)]
    outputs += [shape((size, width), f32)]
    return launch(
        functools.partial(attention_backward, which, last, full, size // LEN),
        "attention_backward",
        operands,
        take(w["mix"], which),
        outputs,
        mixer_scratch(many, w["mix"][0]),
        (16 if full else 8) * many * size * third * width,
    )


def to_partner(x, bits):
    size = lax.axis_size("tensor")
    return lax.ppermute(x, "tensor", [(i, i ^ bits) for i in range(size)])


def add(*items):
    return sum(item.astype(f32) for item in items).astype(bf16)


def tie(value, *others):
    return lax.optimization_barrier((value, *others))[0]


class Line:
    lag = 3

    def __init__(self):
        self.size = lax.axis_size("dp")
        place = lax.axis_index("dp")
        self.middle = (place == 1) | (place == 2)
        self.parts, self.sent, self.pairs, self.totals, self.done = [], [], [], [], []
        self.last = jnp.zeros((8, 128), bf16)

    def add(self, *items):
        *items, _ = lax.optimization_barrier((*items, self.last))
        self.last = add(*items)
        return self.last

    def exchange(self, *fresh):
        if self.size != 4:
            if fresh:
                self.done.append(lax.psum(self.add(*fresh), "dp"))
            return
        routes, items = [], []
        step = len(self.sent)
        back = step - self.lag
        if back >= 0:
            items += list(self.pairs[back])
            routes += [(1, 0), (2, 3)]
        if fresh:
            routes += [(0, 1), (3, 2)]
        *values, _ = lax.optimization_barrier((*items, *fresh, self.last))
        total = add(*values[:2]) if back >= 0 else None
        part = add(*values[len(items) :]) if fresh else None
        if back >= 0:
            self.totals.append(total)
        if fresh:
            self.parts.append(values[len(items) :])
        if total is None or part is None:
            operand = part if total is None else total
        else:
            rows = max(total.shape[0], part.shape[0])
            total, part = [jnp.pad(v, ((0, rows - v.shape[0]), (0, 0))) for v in (total, part)]
            operand = jnp.where(self.middle, total, part)
        self.last = operand
        received = lax.ppermute(operand, "dp", routes)
        self.sent.append(received)
        if back >= 0:
            total = self.totals[back]
            self.done.append(jnp.where(self.middle, total, received[: total.shape[0]]))

    def inner(self):
        if self.size != 4:
            return
        part = self.parts[len(self.pairs)]
        received = self.sent[len(self.pairs)]
        pair = self.add(*part, received[: part[0].shape[0]])
        self.pairs.append((pair, lax.ppermute(pair, "dp", [(1, 2), (2, 1)])))


def all_rows(own, near, far, both):
    place = lax.axis_index("tensor")
    low, high = place % 2 == 1, place // 2 == 1
    first = [jnp.where(low, near, own), jnp.where(low, own, near)]
    second = [jnp.where(low, both, far), jnp.where(low, far, both)]
    return [jnp.where(high, b, a) for a, b in zip(first, second)] + [
        jnp.where(high, a, b) for a, b in zip(first, second)
    ]


def body(
    ends_in,
    segment_ids,
    w_qkv,
    bias_qv,
    w_out,
    bias_out,
    gain_one,
    shift_one,
    w_up,
    bias_up,
    w_down,
    bias_down,
    gain_two,
    shift_two,
):
    section = lax.axis_index("section")
    place = lax.axis_index("tensor")
    _, micro, count, length, width = ends_in.shape
    share = count // lax.axis_size("tensor")
    own = lax.dynamic_slice_in_dim(ends_in[0], place * share, share, 1)
    own = own.reshape(micro * share * length, width)
    segments = lax.dynamic_slice_in_dim(segment_ids, place * share, share, 1)
    segments = segments.reshape(micro * share, length)
    third = w_qkv.shape[3]
    rotation = lax.axis_index("dp").astype(jnp.int32).reshape(1)
    w = {
        "rotation": rotation,
        "bias_out": bias_out,
        "gain_one": gain_one,
        "shift_one": shift_one,
        "bias_down": bias_down,
        "gain_two": gain_two,
        "shift_two": shift_two,
    }
    up, down = w_up[0], w_down[0]
    turns = lax.axis_size("dp") if lax.axis_size("dp") == 4 else 1
    mixer, *pieces = run_pack(
        turns, rotation, bias_qv[0], bias_up, w_qkv[0].reshape(width, -1).T, w_out[0], up, down
    )
    pieces = [to_partner(item, 2) for item in pieces]
    mixer_near, up_near, down_near = [to_partner(item, 1) for item in (mixer, up, down)]
    mixer_far = to_partner(mixer, 2)
    w["mix"] = [mixer, mixer_near]
    w["mlp"] = [[up, down], [up_near, down_near]]
    (first,) = run_attention_forward(NEAR_PAIR, False, own, segments, w)
    if turns > 1:
        pieces[0] = tie(pieces[0], first, up_near, down_near)
        near_pieces = [to_partner(pieces[0], 1)]
        for turn in range(1, turns):
            pairs = [(i, (i + turn) % turns) for i in range(turns)]
            pieces.append(lax.ppermute(pieces[0], "dp", pairs))
        rest = [up[: up.shape[0] // 2]]
    else:
        near_pieces, rest = [], [up, down]
    mixer_far = tie(mixer_far, first, *near_pieces)
    w["mix"] += [mixer_far, to_partner(mixer_far, 1)]
    rest = [to_partner(tie(item, mixer_far), 2) for item in rest]
    (first,) = run_attention_forward(FAR_PAIR, False, own, segments, w, first)
    (second,) = run_mlp_forward(NEAR_PAIR, False, False, first, w)
    far = rest + pieces
    *far, _ = lax.optimization_barrier((*far, second))
    near = [to_partner(item, 1) for item in far]
    w["mlp"] += [far, near[: len(rest)] + (near_pieces or []) + near[len(rest) + len(near_pieces) :]]
    out, _ = run_mlp_forward(FAR_PAIR, True, False, first, w, second)
    received = lax.ppermute(out, "section", [(0, 1)])
    rows = jnp.where(section == 0, own, received)
    first, mixed, probs, attended = run_attention_forward(ALL, True, rows, segments, w)
    out, hidden, active, slope, second = run_mlp_forward(ALL, True, True, first, w)
    grad_first, branch_one, _ = run_mlp_backward(
        ALL, True, False, [own, second, gain_two, slope, first, gain_one], w
    )
    grad_in, _ = run_attention_backward(
        ALL, True, False, [branch_one, grad_first, mixed, probs], w
    )
    returned = lax.ppermute(grad_in, "section", [(1, 0)])
    cotangent = jnp.where(section == 1, own, returned)

    line = Line()

    def swap(send):
        return to_partner(tie(send, line.last), 1)

    def halves(keep):
        half = keep.shape[0] // 2 // 16 * 16
        return slice(0, half), slice(half, None)

    def cross(keep, received):
        return [to_partner(line.add(keep[cut], received[cut]), 2) for cut in halves(keep)]

    def chunks(keep, received, far):
        return [(keep[cut], received[cut], item) for cut, item in zip(halves(keep), far)]

    keep, send, branch_two, grad_second, sums_two = run_down_grads(
        FAR_PAIR, [cotangent, second, gain_two, active]
    )
    line.last = branch_two
    received = swap(send)
    keep_near, send_near = run_down_grads(NEAR_PAIR, [branch_two, active])
    line.last = keep_near
    far = cross(keep, received)
    received = swap(send_near)
    keep, send, bias_far, total = run_mlp_backward(
        FAR_PAIR,
        False,
        True,
        [tie(branch_two, line.last), grad_second, slope, hidden, first, gain_one],
        w,
    )
    line.last = total
    down = chunks(keep_near, received, far)
    line.exchange(*down[0])
    received = swap(send)
    keep_near, send_near, bias_near, grad_first, branch_one, sums_one, line.last = run_mlp_backward(
        NEAR_PAIR,
        True,
        True,
        [tie(branch_two, line.last), total, slope, hidden, first, gain_one],
        w,
    )
    line.exchange(*down[1])
    line.inner()
    far = cross(keep, received)
    received = swap(send_near)
    keep, send, total = run_attention_backward(
        FAR_PAIR,
        False,
        True,
        [
            tie(branch_one, line.last),
            *(grad_first, mixed, probs, rows, attended, sums_two, sums_one, bias_far),
        ],
        w,
    )
    line.last = total
    up = chunks(keep_near, received, far)
    line.exchange(*up[0])
    line.inner()
    received = swap(send)
    keep_near, send_near, grad_in, line.last = run_attention_backward(
        NEAR_PAIR,
        True,
        True,
        [
            tie(branch_one, line.last),
            *(total, mixed, probs, rows, attended, sums_two, sums_one, bias_near),
        ],
        w,
    )
    line.exchange(*up[1])
    line.inner()
    far = cross(keep, received)
    mixer = chunks(keep_near, swap(send_near), far)
    mine = jnp.where(section == 1, out, grad_in).reshape(micro, share, length, width)
    line.exchange(*mixer[0])
    line.inner()
    line.exchange(*mixer[1])
    mine = tie(mine, line.last)
    mine_far = to_partner(mine, 2)
    line.inner()
    line.exchange()
    line.inner()
    line.exchange()
    mine, mine_far, _ = lax.optimization_barrier((mine, mine_far, line.last))
    near = to_partner(mine, 1), to_partner(mine_far, 1)
    line.exchange()
    mine, near, mine_far, both, _ = lax.optimization_barrier(
        (mine, near[0], mine_far, near[1], line.last)
    )
    ends = all_rows(mine, near, mine_far, both)
    down, up, mixer = line.done[:2], line.done[2:4], line.done[4:]
    half = mixer[0].shape[0]
    qkv = jnp.concatenate([mixer[0][third:], mixer[1][: 4 * third - half]], 0)
    small = mixer[1][4 * third - half :]
    results = (
        jnp.concatenate(ends, 1),
        qkv.T.reshape(width, 3, third),
        small[1:3, :third],
        mixer[0][:third],
        small[6],
        small[7],
        small[8],
        jnp.concatenate(up, 0),
        small[0],
        jnp.concatenate(down, 0),
        small[3],
        small[4],
        small[5],
    )
    return tuple(item.astype(f32)[None] for item in results)


def solution(mesh):
    return jax.shard_map(
        body,
        mesh=mesh,
        in_specs=(
            P("section", None, "dp", None, None),
            P(None, "dp", None),
            P("section", None, None, "tensor"),
            P("section", None, "tensor"),
            P("section", "tensor", None),
            P("section", None),
            P("section", None),
            P("section", None),
            P("section", None, "tensor"),
            P("section", "tensor"),
            P("section", "tensor", None),
            P("section", None),
            P("section", None),
            P("section", None),
        ),
        out_specs=(
            P("section", None, "dp", None, None),
            P("section", None, None, "tensor"),
            P("section", None, "tensor"),
            P("section", "tensor", None),
            P("section", None),
            P("section", None),
            P("section", None),
            P("section", None, "tensor"),
            P("section", "tensor"),
            P("section", "tensor", None),
            P("section", None),
            P("section", None),
            P("section", None),
        ),
        check_vma=False,
    )
```

```python
import functools
import jax
import jax.numpy as jnp
from jax import lax
from jax.experimental import pallas as pl
from jax.experimental.pallas import tpu as pltpu
from jax.sharding import PartitionSpec as P

HEAD = 64
LEN = 128
SHARDS = 4
SMALL = 16
ROOM = 56
NEAR_PAIR, FAR_PAIR, ALL = (0, 1), (2, 3), (0, 1, 2, 3)
epsilon = 1e-05
bf16 = jnp.bfloat16
f32 = jnp.float32
ANY = pl.BlockSpec(memory_space=pl.ANY)
VM = pl.BlockSpec(memory_space=pltpu.VMEM)
SM = pl.BlockSpec(memory_space=pltpu.SMEM)


def nn(left, right):
    return lax.dot_general(left, right, (((1,), (0,)), ((), ())), preferred_element_type=f32)


def nt(left, right):
    return lax.dot_general(left, right, (((1,), (1,)), ((), ())), preferred_element_type=f32)


def tn(left, right):
    return lax.dot_general(left, right, (((0,), (0,)), ((), ())), preferred_element_type=f32)


def standardize(summed):
    center = summed - jnp.mean(summed, -1, keepdims=True)
    inverse = lax.rsqrt(jnp.mean(center * center, -1, keepdims=True) + epsilon)
    return center * inverse, inverse


def norm_back(normed, inverse, gain, grad_output):
    scaled = grad_output * gain
    return inverse * (
        scaled
        - jnp.mean(scaled, -1, keepdims=True)
        - normed * jnp.mean(scaled * normed, -1, keepdims=True)
    )


def wide(ref):
    return ref[...].astype(f32)


def load(sources, held, sems):
    copies = [
        pltpu.make_async_copy(src, held.at[n], sems.at[n]) for n, src in enumerate(sources)
    ]
    for copy in copies:
        copy.start()
    return copies


def load_mlp(kinds, refs, rotation, held_up, held_down, sems, up_first):
    refs = list(refs)
    ups, downs = [], []
    for n, kind in enumerate(kinds):
        first = refs.pop(0)
        half = first.shape[0]
        up = [pltpu.make_async_copy(first, held_up.at[n, pl.ds(0, half)], sems.at[n, 0])]
        down = []
        if kind == 1:
            down.append(pltpu.make_async_copy(refs.pop(0), held_down.at[n], sems.at[n, 1]))
        else:
            size = held_down.shape[1] // kind
            rest = (held_up.shape[1] - half) // kind
            for turn in range(kind):
                piece = refs.pop(0)
                place = lax.rem(rotation[0] + (kind - turn), kind)
                at = pl.ds(pl.multiple_of(place * size, 16), size)
                down.append(
                    pltpu.make_async_copy(
                        piece.at[pl.ds(0, size)], held_down.at[n, at], sems.at[n, 1 + turn]
                    )
                )
                at = pl.ds(pl.multiple_of(half + place * rest, 16), rest)
                up.append(
                    pltpu.make_async_copy(
                        piece.at[pl.ds(size, rest)], held_up.at[n, at], sems.at[n, 1 + kind + turn]
                    )
                )
        for copy in up + down if up_first else down + up:
            copy.start()
        ups.append(up)
        downs.append(down)
    return ups, downs


def wait(copies):
    for copy in copies:
        copy.wait()


def by_sequence(count, value):
    return jnp.concatenate([value(slice(i * LEN, (i + 1) * LEN)) for i in range(count)], 1)


def same_segment(segments):
    count = segments.shape[0]
    ids = segments[...].astype(f32)
    ids_down = jnp.concatenate([ids, jnp.zeros((8 - count, LEN), f32)], 0).T
    return jnp.concatenate([ids_down[:, i : i + 1] == ids[i : i + 1] for i in range(count)], 1)


def attend(weights, x, same, mixed_out, probs_out):
    count = x.shape[0] // LEN
    third = (weights.shape[0] - SMALL) // 4
    bias = weights[4 * third :].astype(f32)[:8].T[: 3 * third, :1]
    mixed = (nt(weights[: 3 * third], x) + bias).astype(bf16)
    mixed_out[:third] = mixed[:third] * HEAD**-0.5
    mixed_out[third:] = mixed[third:]
    heads = range(third // HEAD)
    for h in heads:
        query = mixed_out[h * HEAD : (h + 1) * HEAD]
        keys = mixed_out[third + h * HEAD : third + (h + 1) * HEAD]
        probs_out[h] = by_sequence(count, lambda cols: tn(keys[:, cols], query[:, cols]))
    for h in heads:
        scores = jnp.where(same, probs_out[h], -1e9)
        probs = jnp.exp(scores - jnp.max(scores, 0, keepdims=True))
        probs_out[h] = probs * (1.0 / jnp.sum(probs, 0, keepdims=True))
    attended = []
    for h in heads:
        value = mixed_out[2 * third + h * HEAD : 2 * third + (h + 1) * HEAD]
        low = probs_out[h].astype(bf16)
        attended.append(by_sequence(count, lambda cols: nn(value[:, cols], low[:, cols])))
    return jnp.concatenate(attended, 0).astype(bf16)


def attend_back(mixed, probs, grads, scores, result):
    third, size = grads.shape
    count = size // LEN
    heads = range(third // HEAD)
    for h in heads:
        at = slice(h * HEAD, (h + 1) * HEAD)
        value, grad = mixed[2 * third + at.start : 2 * third + at.stop], grads[at]
        scores[h] = by_sequence(count, lambda cols: tn(value[:, cols], grad[:, cols]))
    for h in heads:
        prob, grad = probs[h], scores[h]
        inner = jnp.sum(prob * grad, 0, keepdims=True)
        scores[h] = prob * (grad - inner)
    for h in heads:
        at = slice(h * HEAD, (h + 1) * HEAD)
        query, keys = mixed[at], mixed[third + at.start : third + at.stop]
        grad, low, score = grads[at], probs[h].astype(bf16), scores[h].astype(bf16)
        queries = by_sequence(count, lambda cols: nn(keys[:, cols], score[:, cols])) * HEAD**-0.5
        result[at] = queries.astype(bf16)
        result[third + at.start : third + at.stop] = by_sequence(
            count, lambda cols: nt(query[:, cols], score[:, cols])
        ).astype(bf16)
        result[2 * third + at.start : 2 * third + at.stop] = by_sequence(
            count, lambda cols: nt(grad[:, cols], low[:, cols])
        ).astype(bf16)


def attention_forward(which, more, *refs):
    rows, segments, start, *rest = refs
    many = len(which)
    mixers, (first, held, mixed, probs, sems) = rest[:many], rest[many:]
    copies = load(mixers, held, sems)
    x = rows[...]
    first[...] = start[...] if more else x.astype(f32) + wide(start)
    same = same_segment(segments)
    third = (held.shape[1] - SMALL) // 4
    for n in range(many):
        copies[n].wait()
        attended = attend(held.at[n], x, same, mixed.at[n], probs.at[n])
        first[...] += tn(attended, held[n, 3 * third : 4 * third])


def gelu(upward):
    normal = 0.5 * (1.0 + lax.erf(upward * 0.7071067811865476))
    return normal, (upward * normal).astype(bf16)


def mlp_forward(kinds, more, last, *refs):
    rotation, first, gain_one, shift_one, gain_two, shift_two, bias_down, *rest = refs
    if more:
        start, *rest = rest
    many = len(kinds)
    *rest, held_up, held_down, held_tail, sems, sem_tail = rest
    outs = 2 if last else 1
    rest, outs = rest[:-outs], rest[-outs:]
    mixers, weights = rest[:many], rest[many:]
    edge = mixers[0].shape[0] - SMALL
    tails = load([item.at[pl.ds(edge, SMALL)] for item in mixers], held_tail, sem_tail)
    ups, downs = load_mlp(kinds, weights, rotation, held_up, held_down, sems, True)
    second = outs[-1]
    normed, _ = standardize(first[...])
    hidden = normed * wide(gain_one) + wide(shift_one)
    hidden_low = hidden.astype(bf16)
    second[...] = start[...] if more else hidden + wide(bias_down)
    wait(tails)
    for n in range(many):
        wait(ups[n])
        upward = nn(hidden_low, held_up[n]) + held_tail[n].astype(f32)[1:2]
        _, active = gelu(upward)
        wait(downs[n])
        second[...] += nn(active, held_down[n])
    if last:
        normed, _ = standardize(second[...])
        outs[0][...] = (normed * wide(gain_two) + wide(shift_two)).astype(bf16)


KEPT = ("first", "mixed", "probs", "attended", "hidden", "active", "slope", "second")


def middle(kinds, *refs):
    rotation, rows, cotangent, segments, *rest = refs
    gain_one, shift_one, gain_two, shift_two, bias_out, bias_down, *rest = rest
    many = len(kinds)
    mixers, rest = rest[:many], rest[many:]
    ins = sum(1 + kind for kind in kinds)
    weights, rest = rest[:ins], rest[ins:]
    out, grad_in, *rest = rest
    leaving, rest = rest[: len(KEPT)], rest[len(KEPT) :]
    first, mixed, probs, attended, hidden_out, active_out, slope_out, second = rest[: len(KEPT)]
    held, held_up, held_down, total, scores, grad_mixed, *rest = rest[len(KEPT) :]
    sem_mix, sem_mlp, sem_out = rest
    staying = first, mixed, probs, attended, hidden_out, active_out, slope_out, second
    leave = [pltpu.make_async_copy(*pair, sem_out.at[n]) for n, pair in enumerate(zip(staying, leaving))]

    copies = load(mixers, held, sem_mix)
    x = rows[...]
    first[...] = x.astype(f32) + wide(bias_out)
    same = same_segment(segments)
    third = (held.shape[1] - SMALL) // 4
    wait(copies)
    ups, downs = load_mlp(kinds, weights, rotation, held_up, held_down, sem_mlp, True)

    @pl.loop(0, many)
    def _(n):
        attended[n] = attend(held.at[n], x, same, mixed.at[n], probs.at[n])
        first[...] += tn(attended[n], held[n, 3 * third : 4 * third])

    for copy in leave[:4]:
        copy.start()
    normed_one, inverse_one = standardize(first[...])
    hidden = normed_one * wide(gain_one) + wide(shift_one)
    hidden_low = hidden.astype(bf16)
    hidden_out[...] = hidden_low
    second[...] = hidden + wide(bias_down)
    wait(sum(ups + downs, []))

    @pl.loop(0, many)
    def _(n):
        upward = nn(hidden_out[...], held_up[n]) + held[n, 4 * third :].astype(f32)[1:2]
        normal, active = gelu(upward)
        active_out[n] = active
        density = jnp.exp(-0.5 * upward * upward) * 0.3989422804014327
        slope_out[n] = (normal + upward * density).astype(bf16)
        second[...] += nn(active, held_down[n])

    for copy in leave[4:]:
        copy.start()
    normed, inverse = standardize(second[...])
    out[...] = (normed * wide(gain_two) + wide(shift_two)).astype(bf16)

    back = norm_back(normed, inverse, wide(gain_two), wide(cotangent))
    grad_in[...] = back.astype(bf16)
    total[...] = back

    @pl.loop(0, many)
    def _(n):
        grad_upward = (nt(grad_in[...], held_down[n]) * slope_out[n].astype(f32)).astype(bf16)
        total[...] += nt(grad_upward, held_up[n])

    normed, inverse = standardize(first[...])
    back = norm_back(normed, inverse, wide(gain_one), total[...])
    grad_in[...] = back.astype(bf16)
    total[...] = back

    @pl.loop(0, many)
    def _(n):
        grads = nt(held[n, 3 * third : 4 * third], grad_in[...]).astype(bf16)
        attend_back(mixed.at[n], probs.at[n], grads, scores, grad_mixed)
        total[...] += tn(grad_mixed[...], held[n, : 3 * third])

    grad_in[...] = total[...].astype(bf16)
    wait(leave)


ORDER = (2, 3, 0, 1)


def fetch(pairs, sems):
    copies = [pltpu.make_async_copy(*pair, sems.at[n]) for n, pair in enumerate(pairs)]
    for copy in copies:
        copy.start()
    return copies


def down_grads(*refs):
    cotangent, gain_two, *rest = refs
    kept, parts, rest = rest[:2], rest[2 : 2 + SHARDS], rest[2 + SHARDS :]
    branch_two, grad_second, sums, second, active, store, sem_kept, sem_out = rest
    loads = fetch(
        [(kept[0], second)] + [(kept[1].at[s], active.at[s]) for s in ORDER], sem_kept
    )
    g = wide(cotangent)
    loads[0].wait()
    normed, inverse = standardize(second[...])
    back = norm_back(normed, inverse, wide(gain_two), g)
    grad_second[...] = back
    low = back.astype(bf16)
    branch_two[...] = low
    leave = []
    for n, s in enumerate(ORDER):
        loads[1 + n].wait()
        store[n] = tn(active[s], low).astype(bf16)
        leave.append(pltpu.make_async_copy(store.at[n], parts[n], sem_out.at[n]))
        leave[-1].start()
    sums[0:1] = jnp.sum(back, 0, keepdims=True)
    sums[1:2] = jnp.sum(g * normed, 0, keepdims=True)
    sums[2:3] = jnp.sum(g, 0, keepdims=True)
    wait(leave)


def up_grads(kinds, *refs):
    rotation, branch_two, gain_one, sums_two, *rest = refs
    kept, rest = rest[:4], rest[4:]
    many = len(kinds)
    ins = sum(1 + kind for kind in kinds)
    weights, rest = rest[:ins], rest[ins:]
    parts, rest = rest[:many], rest[many:]
    grad_bias_up, sums, grad_first, branch_one, *rest = rest
    total, slope, hidden, first, held_up, held_down, store, *rest = rest
    sem_kept, sem_mlp, sem_out = rest
    ups, downs = load_mlp(kinds, weights, rotation, held_up, held_down, sem_mlp, False)
    loads = fetch(zip(kept, (hidden, slope, total, first)), sem_kept)
    low = branch_two[...]
    loads[0].wait()
    flipped = hidden[...].T
    wait(loads[1:])
    leave = []
    for n, s in enumerate(ORDER):
        wait(downs[n])
        grad_upward = (nt(low, held_down[n]) * slope[s].astype(f32)).astype(bf16)
        store[n] = nn(flipped, grad_upward).astype(bf16)
        leave.append(pltpu.make_async_copy(store.at[n], parts[n], sem_out.at[n]))
        leave[-1].start()
        grad_bias_up[n] = jnp.sum(grad_upward.astype(f32), 0, keepdims=True)
        wait(ups[n])
        total[...] += nt(grad_upward, held_up[n])
    grad_hidden = total[...]
    normed, inverse = standardize(first[...])
    back = norm_back(normed, inverse, wide(gain_one), grad_hidden)
    grad_first[...] = back
    branch_one[...] = back.astype(bf16)
    sums[0:3] = sums_two[...]
    sums[3:4] = jnp.sum(back, 0, keepdims=True)
    sums[4:5] = jnp.sum(grad_hidden * normed, 0, keepdims=True)
    sums[5:6] = jnp.sum(grad_hidden, 0, keepdims=True)
    wait(leave)


def attention_grads(*refs):
    branch_one, rows, sums, grad_bias_up, *rest = refs
    kept, rest = rest[:4], rest[4:]
    mixers, parts, rest = rest[:SHARDS], rest[SHARDS : 2 * SHARDS], rest[2 * SHARDS :]
    grad_in, total, mixed, probs, attended, held, store, scores, grad_mixed, *rest = rest
    sem_kept, sem_mix, sem_out = rest
    pairs = []
    for s in ORDER:
        pairs += [(kept[i].at[s], item.at[s]) for i, item in enumerate((mixed, probs, attended))]
    pairs.append((kept[3], total))
    copies = load(mixers, held, sem_mix)
    loads = fetch(pairs, sem_kept)
    branch = branch_one[...]
    x = rows[...]
    ones = jnp.ones((16, x.shape[0]), bf16)
    third = (held.shape[1] - SMALL) // 4
    blank = jnp.zeros((1, x.shape[1] - third), f32)
    leave = []
    for n, s in enumerate(ORDER):
        copies[n].wait()
        wait(loads[3 * n : 3 * n + 3])
        grads = nt(held[n, 3 * third : 4 * third], branch).astype(bf16)
        store[n, :third] = nn(attended[s], branch).astype(bf16)
        attend_back(mixed.at[s], probs.at[s], grads, scores.at[n], grad_mixed.at[n])
        back = grad_mixed[n]
        store[n, third : 4 * third] = nn(back, x).astype(bf16)
        columns = nt(ones, back)
        small = [
            grad_bias_up[n],
            jnp.concatenate([columns[:1, :third], blank], 1),
            jnp.concatenate([columns[:1, 2 * third :], blank], 1),
            sums[...],
            jnp.zeros((SMALL - 9, x.shape[1]), f32),
        ]
        store[n, 4 * third :] = jnp.concatenate(small, 0).astype(bf16)
        leave.append(pltpu.make_async_copy(store.at[n], parts[n], sem_out.at[n]))
        leave[-1].start()
        if n == 0:
            loads[-1].wait()
        total[...] += tn(back, held[n, : 3 * third])
    grad_in[...] = total[...].astype(bf16)
    wait(leave)


def pack(count, rotation, bias_qv, bias_up, qkv, outer, up, down, *refs):
    third = outer.shape[0]
    mixer, *refs = refs
    copies = [
        (qkv, mixer.at[pl.ds(0, 3 * third)]),
        (outer, mixer.at[pl.ds(3 * third, third)]),
    ]
    if count > 1:
        piece, *refs = refs
        size, half = down.shape[0] // count, up.shape[0] // 2
        part = half // count
        at = pl.multiple_of(rotation[0] * size, 16)
        copies.append((down.at[pl.ds(at, size)], piece.at[pl.ds(0, size)]))
        at = pl.multiple_of(half + rotation[0] * part, 16)
        copies.append((up.at[pl.ds(at, part)], piece.at[pl.ds(size, part)]))
    copies = [pltpu.make_async_copy(*pair, refs[0].at[n]) for n, pair in enumerate(copies)]
    for copy in copies:
        copy.start()
    none = jnp.zeros((1, third), f32)
    biases = jnp.concatenate([wide(bias_qv)[:1], none, wide(bias_qv)[1:], none], 1)
    rest = jnp.zeros((SMALL - 2, biases.shape[1]), f32)
    mixer[4 * third :] = jnp.concatenate([biases, wide(bias_up), rest], 0).astype(bf16)
    wait(copies)


def run_pack(count, rotation, bias_qv, bias_up, qkv, outer, up, down):
    third, width = outer.shape
    outputs = [shape((4 * third + SMALL, width), bf16)]
    if count > 1:
        outputs += [shape((down.shape[0] // count + up.shape[0] // 2 // count, width), bf16)]
    return pl.pallas_call(
        functools.partial(pack, count),
        name="pack",
        out_shape=outputs,
        in_specs=[SM, VM, VM, ANY, ANY, ANY, ANY],
        out_specs=[VM] * len(outputs),
        scratch_shapes=[pltpu.SemaphoreType.DMA((4,))],
    )(rotation, bias_qv, bias_up, qkv, outer, up, down)


def shape(dims, dtype):
    return jax.ShapeDtypeStruct(dims, dtype)


def launch(kernel, name, operands, weights, outputs, leaving, scratch, flops, scalars=0):
    size = sum(i.size * i.dtype.itemsize for i in [*operands, *weights, *outputs, *leaving])
    return pl.pallas_call(
        kernel,
        name=name,
        out_shape=list(leaving) + list(outputs),
        in_specs=[SM] * scalars + [VM] * (len(operands) - scalars) + [ANY] * len(weights),
        out_specs=[ANY] * len(leaving) + [VM] * len(outputs),
        scratch_shapes=scratch,
        compiler_params=pltpu.CompilerParams(vmem_limit_bytes=ROOM << 20),
        cost_estimate=pl.CostEstimate(flops=flops, bytes_accessed=size, transcendentals=0),
    )(*operands, *weights)


def vmem(*items):
    return [pltpu.VMEM(item.shape, item.dtype) for item in items]


def sems(*counts):
    return [pltpu.SemaphoreType.DMA((count if isinstance(count, tuple) else (count,))) for count in counts]


def sizes(w, which):
    up = w["mlp"][0][0].shape
    most = max(len(w["mlp"][s]) - 1 for s in which)
    return (
        shape((len(which),) + w["mix"][0].shape, bf16),
        shape((len(which),) + up, bf16),
        shape((len(which),) + up[::-1], bf16),
        (len(which), 1 + 2 * most),
    )


def kinds_of(w, which):
    return tuple(len(w["mlp"][s]) - 1 for s in which)


def take(items, which):
    return [items[s] for s in which]


def flat(items, which):
    return [item for s in which for item in items[s]]


def kept_shapes(rows, w, which):
    size, width = rows.shape
    many, units = len(which), w["mlp"][0][0].shape[1]
    third = (w["mix"][0].shape[0] - SMALL) // 4
    return (
        shape((size, width), f32),
        shape((many, 3 * third, size), bf16),
        shape((many, third // HEAD, LEN, size), f32),
        shape((many, third, size), bf16),
        shape((size, width), bf16),
        shape((many, size, units), bf16),
        shape((many, size, units), bf16),
        shape((size, width), f32),
    )


def run_attention_forward(which, rows, segments, w, start=None):
    size, width = rows.shape
    held = shape((len(which),) + w["mix"][0].shape, bf16)
    first, mixed, probs, *_ = kept_shapes(rows, w, which)
    more = start is not None
    return launch(
        functools.partial(attention_forward, which, more),
        "attention_forward",
        [rows, segments, start if more else w["bias_out"]],
        take(w["mix"], which),
        [first],
        [],
        vmem(held, mixed, probs) + sems(len(which)),
        8 * size * width * width * len(which) // SHARDS,
    )[0]


def run_mlp_forward(which, last, first, w, start=None):
    size, width = first.shape
    many = len(which)
    names = ("gain_one", "shift_one", "gain_two", "shift_two", "bias_down")
    operands = [w["rotation"], first, *[w[name] for name in names]]
    more = start is not None
    if more:
        operands += [start]
    _, held_up, held_down, sem_mlp = sizes(w, which)
    return launch(
        functools.partial(mlp_forward, kinds_of(w, which), more, last),
        "mlp_forward",
        operands,
        take(w["mix"], which) + flat(w["mlp"], which),
        ([shape((size, width), bf16)] if last else []) + [shape((size, width), f32)],
        [],
        vmem(held_up, held_down, shape((many, SMALL, width), bf16)) + sems(sem_mlp, many),
        4 * size * width * held_up.size // width,
        1,
    )[0]


def run_middle(rows, cotangent, segments, w):
    size, width = rows.shape
    held, held_up, held_down, sem_mlp = sizes(w, ALL)
    kept = kept_shapes(rows, w, ALL)
    names = ("gain_one", "shift_one", "gain_two", "shift_two", "bias_out", "bias_down")
    low = shape((size, width), bf16)
    _, mixed, probs, *_ = kept
    scratch = (
        vmem(*kept, held, held_up, held_down, shape((size, width), f32))
        + vmem(shape(probs.shape[1:], f32), shape(mixed.shape[1:], bf16))
        + sems(SHARDS, sem_mlp, len(kept))
    )

    def kernel(kinds, *refs):
        ins = 10 + len(take(w["mix"], ALL) + flat(w["mlp"], ALL))
        ends = ins + len(kept)
        middle(kinds, *refs[:ins], *refs[ends : ends + 2], *refs[ins:ends], *refs[ends + 2 :])

    *kept, out, grad_in = launch(
        functools.partial(kernel, kinds_of(w, ALL)),
        "middle",
        [w["rotation"], rows, cotangent, segments, *[w[name] for name in names]],
        take(w["mix"], ALL) + flat(w["mlp"], ALL),
        [low, low],
        kept,
        scratch,
        8 * size * (held.size + held_up.size),
        1,
    )
    return out, grad_in, dict(zip(KEPT, kept))


def run_down_grads(cotangent, kept, w):
    size, width = cotangent.shape
    second, active = kept["second"], kept["active"]
    units = active.shape[2]
    part = shape((units, width), bf16)
    *parts, branch_two, grad_second, sums = launch(
        down_grads,
        "down_grads",
        [cotangent, w["gain_two"]],
        [second, active],
        [shape((size, width), bf16), shape((size, width), f32), shape((3, width), f32)],
        [part] * SHARDS,
        vmem(second, active, shape((SHARDS,) + part.shape, bf16)) + sems(1 + SHARDS, SHARDS),
        2 * SHARDS * size * units * width,
    )
    return parts, branch_two, grad_second, sums


def run_up_grads(branch_two, grad_second, sums, kept, w):
    size, width = branch_two.shape
    _, held_up, held_down, sem_mlp = sizes(w, ORDER)
    names = ("hidden", "slope", "first")
    hidden, slope, first = take(kept, names)
    part = shape(held_up.shape[1:], bf16)
    whole = shape((size, width), f32)
    *parts, grad_bias_up, sums, grad_first, branch_one = launch(
        functools.partial(up_grads, kinds_of(w, ORDER)),
        "up_grads",
        [w["rotation"], branch_two, w["gain_one"], sums],
        [hidden, slope, grad_second, first] + flat(w["mlp"], ORDER),
        [
            shape((SHARDS, 1, held_up.shape[2]), f32),
            shape((6, width), f32),
            whole,
            shape((size, width), bf16),
        ],
        [part] * SHARDS,
        vmem(whole, slope, hidden, first, held_up, held_down, held_up) + sems(4, sem_mlp, SHARDS),
        6 * size * held_up.size,
        1,
    )
    return parts, grad_bias_up, sums, grad_first, branch_one


def run_attention_grads(branch_one, grad_first, rows, sums, grad_bias_up, kept, w):
    size, width = rows.shape
    held, _, _, _ = sizes(w, ORDER)
    names = ("mixed", "probs", "attended")
    mixed, probs, attended = take(kept, names)
    part = shape(held.shape[1:], bf16)
    *parts, grad_in = launch(
        attention_grads,
        "attention_grads",
        [branch_one, rows, sums, grad_bias_up],
        [mixed, probs, attended, grad_first] + take(w["mix"], ORDER),
        [shape((size, width), bf16)],
        [part] * SHARDS,
        vmem(grad_first, mixed, probs, attended, held, held, probs, mixed)
        + sems(3 * SHARDS + 1, SHARDS, SHARDS),
        4 * size * held.size,
    )
    return parts, grad_in


def to_partner(x, bits):
    size = lax.axis_size("tensor")
    return lax.ppermute(x, "tensor", [(i, i ^ bits) for i in range(size)])


def add(*items):
    return sum(item.astype(f32) for item in items).astype(bf16)


def tie(value, *others):
    return lax.optimization_barrier((value, *others))[0]


class Line:
    lag = 3

    def __init__(self):
        self.size = lax.axis_size("dp")
        place = lax.axis_index("dp")
        self.middle = (place == 1) | (place == 2)
        self.parts, self.sent, self.pairs, self.totals, self.done = [], [], [], [], []
        self.last = jnp.zeros((8, 128), bf16)

    def add(self, *items, cut=slice(None)):
        *items, _ = lax.optimization_barrier((*items, self.last))
        self.last = add(*[item[cut] for item in items])
        return self.last

    def exchange(self, keep=None, received=None, cut=None, far=None):
        fresh = [] if far is None else [keep, received, far]
        if self.size != 4:
            if fresh:
                *values, _ = lax.optimization_barrier((*fresh, self.last))
                self.last = add(values[0][cut], values[1][cut], values[2])
                self.done.append(lax.psum(self.last, "dp"))
            return
        routes, items = [], []
        back = len(self.sent) - self.lag
        if back >= 0:
            items += list(self.pairs[back])
            routes += [(1, 0), (2, 3)]
        if fresh:
            routes += [(0, 1), (3, 2)]
        *values, _ = lax.optimization_barrier((*items, *fresh, self.last))
        total = part = None
        if fresh:
            keep, received, far = values[len(items) :]
            self.parts.append((keep, received, cut, far))
            part = add(keep[cut], received[cut], far)
        if back >= 0:
            total = add(*values[:2])
            self.totals.append(total)
        if total is None or part is None:
            operand = part if total is None else total
        else:
            rows = max(total.shape[0], part.shape[0])
            wide_total, part = [
                jnp.pad(v, ((0, rows - v.shape[0]), (0, 0))) for v in (total, part)
            ]
            operand = jnp.where(self.middle, wide_total, part)
        self.last = operand
        answer = lax.ppermute(operand, "dp", routes)
        self.sent.append(answer)
        if back >= 0:
            self.done.append(jnp.where(self.middle, total, answer[: total.shape[0]]))

    def inner(self):
        if self.size != 4:
            return
        keep, received, cut, far = self.parts[len(self.pairs)]
        answer = self.sent[len(self.pairs)]
        *values, _ = lax.optimization_barrier((keep, received, far, answer, self.last))
        keep, received, far, answer = values
        self.last = add(keep[cut], received[cut], far, answer[: far.shape[0]])
        self.pairs.append((self.last, lax.ppermute(self.last, "dp", [(1, 2), (2, 1)])))


def all_rows(own, near, far, both):
    place = lax.axis_index("tensor")
    low, high = place % 2 == 1, place // 2 == 1
    first = [jnp.where(low, near, own), jnp.where(low, own, near)]
    second = [jnp.where(low, both, far), jnp.where(low, far, both)]
    return [jnp.where(high, b, a) for a, b in zip(first, second)] + [
        jnp.where(high, a, b) for a, b in zip(first, second)
    ]


def body(
    ends_in,
    segment_ids,
    w_qkv,
    bias_qv,
    w_out,
    bias_out,
    gain_one,
    shift_one,
    w_up,
    bias_up,
    w_down,
    bias_down,
    gain_two,
    shift_two,
):
    section = lax.axis_index("section")
    place = lax.axis_index("tensor")
    _, micro, count, length, width = ends_in.shape
    share = count // lax.axis_size("tensor")
    own = lax.dynamic_slice_in_dim(ends_in[0], place * share, share, 1)
    own = own.reshape(micro * share * length, width)
    segments = lax.dynamic_slice_in_dim(segment_ids, place * share, share, 1)
    segments = segments.reshape(micro * share, length)
    third = w_qkv.shape[3]
    rotation = lax.axis_index("dp").astype(jnp.int32).reshape(1)
    w = {
        "rotation": rotation,
        "bias_out": bias_out,
        "gain_one": gain_one,
        "shift_one": shift_one,
        "bias_down": bias_down,
        "gain_two": gain_two,
        "shift_two": shift_two,
    }
    up, down = w_up[0], w_down[0]
    turns = lax.axis_size("dp") if lax.axis_size("dp") == 4 else 1
    mixer, *pieces = run_pack(
        turns, rotation, bias_qv[0], bias_up, w_qkv[0].reshape(width, -1).T, w_out[0], up, down
    )
    pieces = [to_partner(item, 2) for item in pieces]
    mixer_near, up_near, down_near = [to_partner(item, 1) for item in (mixer, up, down)]
    w["mix"] = [mixer, mixer_near]
    w["mlp"] = [[up, down], [up_near, down_near]]
    first = run_attention_forward(NEAR_PAIR, own, segments, w)
    mixer_far = to_partner(tie(mixer, first, *pieces), 2)
    if turns > 1:

        def turned(piece, turn):
            return lax.ppermute(piece, "dp", [(i, (i + turn) % turns) for i in range(turns)])

        piece = tie(pieces[0], first, up_near, down_near)
        one, three = turned(piece, 1), turned(piece, turns - 1)
        two = turned(one, 1)
        mixer_far, piece, one, three = lax.optimization_barrier((mixer_far, piece, one, three))
        half = to_partner(tie(up[: up.shape[0] // 2], mixer_far), 2)
        w["mix"] += [mixer_far, to_partner(mixer_far, 1)]
        near = [to_partner(item, 1) for item in (piece, one, three)]
        first = run_attention_forward(FAR_PAIR, own, segments, w, first)
        first, two, *near = lax.optimization_barrier((first, two, *near))
        two_near = to_partner(two, 1)
        second = run_mlp_forward(NEAR_PAIR, False, first, w)
        half, two_near, _ = lax.optimization_barrier((half, two_near, second))
        w["mlp"] += [
            [half, piece, one, two, three],
            [to_partner(half, 1), near[0], near[1], two_near, near[2]],
        ]
    else:
        far = [to_partner(item, 2) for item in (up, down)]
        w["mix"] += [mixer_far, to_partner(mixer_far, 1)]
        w["mlp"] += [far, [to_partner(item, 1) for item in far]]
        first = run_attention_forward(FAR_PAIR, own, segments, w, first)
        second = run_mlp_forward(NEAR_PAIR, False, first, w)
    out = run_mlp_forward(FAR_PAIR, True, first, w, second)
    received = lax.ppermute(out, "section", [(0, 1)])
    rows = jnp.where(section == 0, own, received)
    out, grad_in, kept = run_middle(rows, own, segments, w)
    returned = lax.ppermute(grad_in, "section", [(1, 0)])
    cotangent = jnp.where(section == 1, own, returned)

    line = Line()

    def swap(send):
        return to_partner(tie(send, line.last), 1)

    def halves(keep):
        half = keep.shape[0] // 2 // 16 * 16
        return slice(0, half), slice(half, None)

    def cross(keep, received):
        return [to_partner(line.add(keep, received, cut=cut), 2) for cut in halves(keep)]

    def chunks(keep, received, far):
        return [(keep, received, cut, item) for cut, item in zip(halves(keep), far)]

    down, branch_two, grad_second, sums = run_down_grads(cotangent, kept, w)
    line.last = branch_two
    down_far = cross(down[0], swap(down[1]))
    received = swap(down[3])
    up, grad_bias_up, sums, grad_first, branch_one = run_up_grads(
        tie(branch_two, line.last), grad_second, sums, kept, w
    )
    line.last = branch_one
    down = chunks(down[2], received, down_far)
    line.exchange(*down[0])
    received = swap(up[1])
    mixer, grad_in = run_attention_grads(
        tie(branch_one, line.last), grad_first, rows, sums, grad_bias_up, kept, w
    )
    line.last = grad_in
    up_far = cross(up[0], received)
    line.exchange(*down[1])
    line.inner()
    mixer_received, up_received = swap(mixer[1]), swap(up[3])
    up = chunks(up[2], up_received, up_far)
    mixer_far = cross(mixer[0], mixer_received)
    line.exchange(*up[0])
    line.inner()
    mixer = chunks(mixer[2], swap(mixer[3]), mixer_far)
    line.exchange(*up[1])
    line.inner()
    mine = jnp.where(section == 1, out, grad_in).reshape(micro, share, length, width)
    line.exchange(*mixer[0])
    line.inner()
    line.exchange(*mixer[1])
    mine = tie(mine, line.last)
    mine_far = to_partner(mine, 2)
    line.inner()
    line.exchange()
    line.inner()
    line.exchange()
    mine, mine_far, _ = lax.optimization_barrier((mine, mine_far, line.last))
    near = to_partner(mine, 1), to_partner(mine_far, 1)
    line.exchange()
    mine, near, mine_far, both, _ = lax.optimization_barrier(
        (mine, near[0], mine_far, near[1], line.last)
    )
    ends = all_rows(mine, near, mine_far, both)
    down, up, mixer = line.done[:2], line.done[2:4], line.done[4:]
    half = mixer[0].shape[0]
    qkv = jnp.concatenate([mixer[0][third:], mixer[1][: 4 * third - half]], 0)
    small = mixer[1][4 * third - half :]
    results = (
        jnp.concatenate(ends, 1),
        qkv.T.reshape(width, 3, third),
        small[1:3, :third],
        mixer[0][:third],
        small[6],
        small[7],
        small[8],
        jnp.concatenate(up, 0),
        small[0],
        jnp.concatenate(down, 0),
        small[3],
        small[4],
        small[5],
    )
    return tuple(item.astype(f32)[None] for item in results)


def solution(mesh):
    return jax.shard_map(
        body,
        mesh=mesh,
        in_specs=(
            P("section", None, "dp", None, None),
            P(None, "dp", None),
            P("section", None, None, "tensor"),
            P("section", None, "tensor"),
            P("section", "tensor", None),
            P("section", None),
            P("section", None),
            P("section", None),
            P("section", None, "tensor"),
            P("section", "tensor"),
            P("section", "tensor", None),
            P("section", None),
            P("section", None),
            P("section", None),
        ),
        out_specs=(
            P("section", None, "dp", None, None),
            P("section", None, None, "tensor"),
            P("section", None, "tensor"),
            P("section", "tensor", None),
            P("section", None),
            P("section", None),
            P("section", None),
            P("section", None, "tensor"),
            P("section", "tensor"),
            P("section", "tensor", None),
            P("section", None),
            P("section", None),
            P("section", None),
        ),
        check_vma=False,
    )
```

```python
import functools
import jax
import jax.numpy as jnp
from jax import lax
from jax.experimental import pallas as pl
from jax.experimental.pallas import tpu as pltpu
from jax.sharding import PartitionSpec as P

HEAD = 64
LEN = 128
SHARDS = 4
SMALL = 16
TURNED = 256
ROOM = 56
NEAR_PAIR, FAR_PAIR, ALL = (0, 1), (2, 3), (0, 1, 2, 3)
epsilon = 1e-05
bf16 = jnp.bfloat16
f32 = jnp.float32
ANY = pl.BlockSpec(memory_space=pl.ANY)
VM = pl.BlockSpec(memory_space=pltpu.VMEM)
SM = pl.BlockSpec(memory_space=pltpu.SMEM)


def nn(left, right):
    return lax.dot_general(left, right, (((1,), (0,)), ((), ())), preferred_element_type=f32)


def nt(left, right):
    return lax.dot_general(left, right, (((1,), (1,)), ((), ())), preferred_element_type=f32)


def tn(left, right):
    return lax.dot_general(left, right, (((0,), (0,)), ((), ())), preferred_element_type=f32)


def standardize(summed):
    center = summed - jnp.mean(summed, -1, keepdims=True)
    inverse = lax.rsqrt(jnp.mean(center * center, -1, keepdims=True) + epsilon)
    return center * inverse, inverse


def norm_back(normed, inverse, gain, grad_output):
    scaled = grad_output * gain
    return inverse * (
        scaled
        - jnp.mean(scaled, -1, keepdims=True)
        - normed * jnp.mean(scaled * normed, -1, keepdims=True)
    )


def wide(ref):
    return ref[...].astype(f32)


def load(sources, held, sems):
    copies = [
        pltpu.make_async_copy(src, held.at[n], sems.at[n]) for n, src in enumerate(sources)
    ]
    for copy in copies:
        copy.start()
    return copies


def load_mixers(groups, refs, held, sems, after=lambda n: None):
    refs = list(refs)
    loads = []
    for n, group in enumerate(groups):
        at, copies = 0, []
        for i in range(group):
            block = refs.pop(0)
            size = block.shape[0]
            target = held.at[n, pl.ds(at, size)]
            copies.append(pltpu.make_async_copy(block, target, sems.at[n, i]))
            copies[-1].start()
            at += size
        loads.append(copies)
        after(n)
    return loads


def load_mlp(kinds, refs, rotation, held_up, held_down, sems, up_first, before=lambda n: None):
    refs = list(refs)
    ups, downs = [], []
    for n, kind in enumerate(kinds):
        first = refs.pop(0)
        half = first.shape[0]
        up = [pltpu.make_async_copy(first, held_up.at[n, pl.ds(0, half)], sems.at[n, 0])]
        down = []
        if kind == 1:
            down.append(pltpu.make_async_copy(refs.pop(0), held_down.at[n], sems.at[n, 1]))
        else:
            size = held_down.shape[1] // kind
            rest = (held_up.shape[1] - half) // kind
            for turn in range(kind):
                piece = refs.pop(0)
                place = lax.rem(rotation[0] + (kind - turn), kind)
                at = pl.ds(pl.multiple_of(place * size, 16), size)
                down.append(
                    pltpu.make_async_copy(
                        piece.at[pl.ds(0, size)], held_down.at[n, at], sems.at[n, 1 + turn]
                    )
                )
                at = pl.ds(pl.multiple_of(half + place * rest, 16), rest)
                up.append(
                    pltpu.make_async_copy(
                        piece.at[pl.ds(size, rest)], held_up.at[n, at], sems.at[n, 1 + kind + turn]
                    )
                )
        before(n)
        for copy in up + down if up_first else down + up:
            copy.start()
        ups.append(up)
        downs.append(down)
    return ups, downs


def wait(copies):
    for copy in copies:
        copy.wait()


def by_sequence(count, value):
    return jnp.concatenate([value(slice(i * LEN, (i + 1) * LEN)) for i in range(count)], 1)


def same_segment(segments):
    count = segments.shape[0]
    ids = segments[...].astype(f32)
    ids_down = jnp.concatenate([ids, jnp.zeros((-count % 8, LEN), f32)], 0).T
    return jnp.concatenate([ids_down[:, i : i + 1] == ids[i : i + 1] for i in range(count)], 1)


def attend(weights, x, same, mixed_out, probs_out):
    count = x.shape[0] // LEN
    third = (weights.shape[0] - SMALL) // 4
    bias = weights[4 * third :].astype(f32)[:8].T[: 3 * third, :1]
    mixed = (nt(weights[: 3 * third], x) + bias).astype(bf16)
    mixed_out[:third] = mixed[:third] * HEAD**-0.5
    mixed_out[third:] = mixed[third:]
    heads = range(third // HEAD)
    for h in heads:
        query = mixed_out[h * HEAD : (h + 1) * HEAD]
        keys = mixed_out[third + h * HEAD : third + (h + 1) * HEAD]
        probs_out[h] = by_sequence(count, lambda cols: tn(keys[:, cols], query[:, cols]))
    for h in heads:
        scores = jnp.where(same, probs_out[h], -1e9)
        probs = jnp.exp(scores - jnp.max(scores, 0, keepdims=True))
        probs_out[h] = probs * (1.0 / jnp.sum(probs, 0, keepdims=True))
    attended = []
    for h in heads:
        value = mixed_out[2 * third + h * HEAD : 2 * third + (h + 1) * HEAD]
        low = probs_out[h].astype(bf16)
        attended.append(by_sequence(count, lambda cols: nn(value[:, cols], low[:, cols])))
    return jnp.concatenate(attended, 0).astype(bf16)


def attend_back(mixed, probs, grads, scores, result):
    third, size = grads.shape
    count = size // LEN
    heads = range(third // HEAD)
    for h in heads:
        at = slice(h * HEAD, (h + 1) * HEAD)
        value, grad = mixed[2 * third + at.start : 2 * third + at.stop], grads[at]
        scores[h] = by_sequence(count, lambda cols: tn(value[:, cols], grad[:, cols]))
    for h in heads:
        prob, grad = probs[h], scores[h]
        inner = jnp.sum(prob * grad, 0, keepdims=True)
        scores[h] = prob * (grad - inner)
    for h in heads:
        at = slice(h * HEAD, (h + 1) * HEAD)
        query, keys = mixed[at], mixed[third + at.start : third + at.stop]
        grad, low, score = grads[at], probs[h].astype(bf16), scores[h].astype(bf16)
        queries = by_sequence(count, lambda cols: nn(keys[:, cols], score[:, cols])) * HEAD**-0.5
        result[at] = queries.astype(bf16)
        result[third + at.start : third + at.stop] = by_sequence(
            count, lambda cols: nt(query[:, cols], score[:, cols])
        ).astype(bf16)
        result[2 * third + at.start : 2 * third + at.stop] = by_sequence(
            count, lambda cols: nt(grad[:, cols], low[:, cols])
        ).astype(bf16)


def head_attention(group, share, place, rows, segments, *refs):
    blocks, (near, far, held, mixed, probs, sems) = refs[:group], refs[group:]
    copies = load_mixers([group], blocks, held, sems)
    same = same_segment(segments)
    wait(copies[0])
    attended = attend(held.at[0], rows[...], same, mixed, probs)
    count = share * SHARDS
    for i in range(segments.shape[0]):
        owner = lax.bitwise_xor(place[0], i % count // share)
        at = i // count * share + i % share
        cols = slice(at * LEN, (at + 1) * LEN)
        block = attended[:, i * LEN : (i + 1) * LEN]

        @pl.when(owner < 2)
        def _(owner=owner, cols=cols, block=block):
            near[owner, :, cols] = block

        @pl.when(owner >= 2)
        def _(owner=owner, cols=cols, block=block):
            far[owner - 2, :, cols] = block


def gelu(upward):
    normal = 0.5 * (1.0 + lax.erf(upward * 0.7071067811865476))
    return normal, (upward * normal).astype(bf16)


def mlp_forward(kinds, last, *refs):
    rotation, gain_one, shift_one, gain_two, shift_two, bias_down, *rest = refs
    many = len(kinds)
    if last:
        first, start, *rest = rest
    else:
        rows, bias_out, near, near_in, far_in, both_in, *rest = rest
    count = many if last else SHARDS
    outers, rest = rest[:count], rest[count:]
    ins = sum(1 + kind for kind in kinds)
    weights, rest = rest[:ins], rest[ins:]
    result, second, held_up, held_down, held_outer, sems, sem_outer = rest
    loads = load(outers, held_outer, sem_outer)
    ups, downs = load_mlp(kinds, weights, rotation, held_up, held_down, sems, True)
    third = held_outer.shape[1] - SMALL
    if not last:
        first = result
        first[...] = rows[...].astype(f32) + wide(bias_out)
        parts = near[0], near_in[1], far_in[0], both_in[1]
        for n, part in enumerate(parts):
            loads[n].wait()
            first[...] += tn(part, held_outer[n, :third])
    else:
        wait(loads)
    normed, _ = standardize(first[...])
    hidden = normed * wide(gain_one) + wide(shift_one)
    hidden_low = hidden.astype(bf16)
    second[...] = start[...] if last else hidden + wide(bias_down)
    for n in range(many):
        wait(ups[n])
        upward = nn(hidden_low, held_up[n]) + held_outer[n, third:].astype(f32)[1:2]
        _, active = gelu(upward)
        wait(downs[n])
        second[...] += nn(active, held_down[n])
    if last:
        normed, _ = standardize(second[...])
        result[...] = (normed * wide(gain_two) + wide(shift_two)).astype(bf16)


KEPT = ("first", "mixed", "probs", "attended", "hidden", "active", "slope", "second")


def middle(kinds, groups, *refs):
    rotation, rows, cotangent, segments, *rest = refs
    gain_one, shift_one, gain_two, shift_two, bias_out, bias_down, *rest = rest
    many = len(kinds)
    mixers, rest = rest[: sum(groups)], rest[sum(groups) :]
    ins = sum(1 + kind for kind in kinds)
    weights, rest = rest[:ins], rest[ins:]
    out, grad_in, *rest = rest
    leaving, rest = rest[: len(KEPT)], rest[len(KEPT) :]
    first, mixed, probs, attended, hidden_out, active_out, slope_out, second = rest[: len(KEPT)]
    held, held_up, held_down, total, scores, grad_mixed, *rest = rest[len(KEPT) :]
    sem_mix, sem_mlp, sem_out = rest
    staying = first, mixed, probs, attended, hidden_out, active_out, slope_out, second
    leave = [pltpu.make_async_copy(*pair, sem_out.at[n]) for n, pair in enumerate(zip(staying, leaving))]

    copies = load_mixers(groups, mixers, held, sem_mix)
    x = rows[...]
    first[...] = x.astype(f32) + wide(bias_out)
    same = same_segment(segments)
    third = (held.shape[1] - SMALL) // 4
    wait(sum(copies, []))
    ups, downs = load_mlp(kinds, weights, rotation, held_up, held_down, sem_mlp, True)

    @pl.loop(0, many, unroll=2)
    def _(n):
        attended[n] = attend(held.at[n], x, same, mixed.at[n], probs.at[n])
        first[...] += tn(attended[n], held[n, 3 * third : 4 * third])

    for copy in leave[:4]:
        copy.start()
    normed_one, inverse_one = standardize(first[...])
    hidden = normed_one * wide(gain_one) + wide(shift_one)
    hidden_low = hidden.astype(bf16)
    hidden_out[...] = hidden_low
    second[...] = hidden + wide(bias_down)
    wait(sum(ups + downs, []))

    @pl.loop(0, many, unroll=4)
    def _(n):
        upward = nn(hidden_out[...], held_up[n]) + held[n, 4 * third :].astype(f32)[1:2]
        normal, active = gelu(upward)
        active_out[n] = active
        density = jnp.exp(-0.5 * upward * upward) * 0.3989422804014327
        slope_out[n] = (normal + upward * density).astype(bf16)
        second[...] += nn(active, held_down[n])

    for copy in leave[4:]:
        copy.start()
    normed, inverse = standardize(second[...])
    out[...] = (normed * wide(gain_two) + wide(shift_two)).astype(bf16)

    back = norm_back(normed, inverse, wide(gain_two), wide(cotangent))
    grad_in[...] = back.astype(bf16)
    total[...] = back

    @pl.loop(0, many, unroll=4)
    def _(n):
        grad_upward = (nt(grad_in[...], held_down[n]) * slope_out[n].astype(f32)).astype(bf16)
        total[...] += nt(grad_upward, held_up[n])

    normed, inverse = standardize(first[...])
    back = norm_back(normed, inverse, wide(gain_one), total[...])
    grad_in[...] = back.astype(bf16)
    total[...] = back

    @pl.loop(0, many, unroll=2)
    def _(n):
        grads = nt(held[n, 3 * third : 4 * third], grad_in[...]).astype(bf16)
        attend_back(mixed.at[n], probs.at[n], grads, scores, grad_mixed)
        total[...] += tn(grad_mixed[...], held[n, : 3 * third])

    grad_in[...] = total[...].astype(bf16)
    wait(leave)


ORDER = (2, 3, 0, 1)


def fetch(pairs, sems):
    copies = [pltpu.make_async_copy(*pair, sems.at[n]) for n, pair in enumerate(pairs)]
    for copy in copies:
        copy.start()
    return copies


def down_grads(*refs):
    cotangent, gain_two, *rest = refs
    kept, parts, rest = rest[:2], rest[2 : 2 + SHARDS], rest[2 + SHARDS :]
    branch_two, grad_second, sums, second, active, store, sem_kept, sem_out = rest
    loads = fetch(
        [(kept[0], second)] + [(kept[1].at[s], active.at[s]) for s in ORDER], sem_kept
    )
    g = wide(cotangent)
    loads[0].wait()
    normed, inverse = standardize(second[...])
    back = norm_back(normed, inverse, wide(gain_two), g)
    grad_second[...] = back
    low = back.astype(bf16)
    branch_two[...] = low
    leave = []
    for n, s in enumerate(ORDER):
        loads[1 + n].wait()
        store[n] = tn(active[s], low).astype(bf16)
        leave.append(pltpu.make_async_copy(store.at[n], parts[n], sem_out.at[n]))
        leave[-1].start()
    sums[0:1] = jnp.sum(back, 0, keepdims=True)
    sums[1:2] = jnp.sum(g * normed, 0, keepdims=True)
    sums[2:3] = jnp.sum(g, 0, keepdims=True)
    wait(leave)


def up_grads(kinds, *refs):
    rotation, branch_two, gain_one, sums_two, *rest = refs
    kept, rest = rest[:4], rest[4:]
    many = len(kinds)
    ins = sum(1 + kind for kind in kinds)
    weights, rest = rest[:ins], rest[ins:]
    parts, rest = rest[:many], rest[many:]
    grad_bias_up, sums, grad_first, branch_one, *rest = rest
    total, slope, hidden, first, held_up, held_down, store, *rest = rest
    sem_kept, sem_mlp, sem_out = rest
    loads = [
        pltpu.make_async_copy(source, target, sem_kept.at[n])
        for n, (source, target) in enumerate(
            [(kept[0], hidden)]
            + [(kept[1].at[s], slope.at[s]) for s in ORDER]
            + [(kept[2], total), (kept[3], first)]
        )
    ]
    loads[0].start()
    ups, downs = load_mlp(
        kinds, weights, rotation, held_up, held_down, sem_mlp, False, lambda n: loads[1 + n].start()
    )
    loads[-2].start()
    loads[-1].start()
    low = branch_two[...]
    loads[0].wait()
    flipped = hidden[...].T
    leave = []
    for n, s in enumerate(ORDER):
        wait(downs[n])
        loads[1 + n].wait()
        grad_upward = (nt(low, held_down[n]) * slope[s].astype(f32)).astype(bf16)
        store[n] = nn(flipped, grad_upward).astype(bf16)
        leave.append(pltpu.make_async_copy(store.at[n], parts[n], sem_out.at[n]))
        leave[-1].start()
        grad_bias_up[n] = jnp.sum(grad_upward.astype(f32), 0, keepdims=True)
        wait(ups[n])
        if n == 0:
            loads[-2].wait()
        total[...] += nt(grad_upward, held_up[n])
    grad_hidden = total[...]
    loads[-1].wait()
    normed, inverse = standardize(first[...])
    back = norm_back(normed, inverse, wide(gain_one), grad_hidden)
    grad_first[...] = back
    branch_one[...] = back.astype(bf16)
    sums[0:3] = sums_two[...]
    sums[3:4] = jnp.sum(back, 0, keepdims=True)
    sums[4:5] = jnp.sum(grad_hidden * normed, 0, keepdims=True)
    sums[5:6] = jnp.sum(grad_hidden, 0, keepdims=True)
    wait(leave)


def attention_grads(groups, *refs):
    branch_one, rows, sums, grad_bias_up, *rest = refs
    kept, rest = rest[:4], rest[4:]
    mixers, rest = rest[: sum(groups)], rest[sum(groups) :]
    parts, rest = rest[:SHARDS], rest[SHARDS:]
    grad_in, total, mixed, probs, attended, held, store, scores, grad_mixed, *rest = rest
    sem_kept, sem_mix, sem_out = rest
    pairs = []
    for s in ORDER:
        pairs += [(kept[i].at[s], item.at[s]) for i, item in enumerate((mixed, probs, attended))]
    pairs.append((kept[3], total))
    loads = [pltpu.make_async_copy(*pair, sem_kept.at[n]) for n, pair in enumerate(pairs)]

    def begin(n):
        for copy in loads[3 * n : 3 * n + 3]:
            copy.start()

    copies = load_mixers(groups, mixers, held, sem_mix, begin)
    loads[-1].start()
    branch = branch_one[...]
    x = rows[...]
    ones = jnp.ones((16, x.shape[0]), bf16)
    third = (held.shape[1] - SMALL) // 4
    blank = jnp.zeros((1, x.shape[1] - third), f32)
    leave = []
    for n, s in enumerate(ORDER):
        wait(copies[n])
        wait(loads[3 * n : 3 * n + 3])
        grads = nt(held[n, 3 * third : 4 * third], branch).astype(bf16)
        store[n, :third] = nn(attended[s], branch).astype(bf16)
        attend_back(mixed.at[s], probs.at[s], grads, scores.at[n], grad_mixed.at[n])
        back = grad_mixed[n]
        store[n, third : 4 * third] = nn(back, x).astype(bf16)
        columns = nt(ones, back)
        small = [
            grad_bias_up[n],
            jnp.concatenate([columns[:1, :third], blank], 1),
            jnp.concatenate([columns[:1, 2 * third :], blank], 1),
            sums[...],
            jnp.zeros((SMALL - 9, x.shape[1]), f32),
        ]
        store[n, 4 * third :] = jnp.concatenate(small, 0).astype(bf16)
        leave.append(pltpu.make_async_copy(store.at[n], parts[n], sem_out.at[n]))
        leave[-1].start()
        if n == 0:
            loads[-1].wait()
        total[...] += tn(back, held[n, : 3 * third])
    grad_in[...] = total[...].astype(bf16)
    wait(leave)


def pack(count, rotation, bias_qv, bias_up, outer, up, down, *refs):
    third = outer.shape[0]
    result, *refs = refs
    copies = [(outer, result.at[pl.ds(0, third)])]
    if count > 1:
        piece, *refs = refs
        size, part = down.shape[0] // count, TURNED // count
        at = pl.multiple_of(rotation[0] * size, 16)
        copies.append((down.at[pl.ds(at, size)], piece.at[pl.ds(0, size)]))
        at = pl.multiple_of(up.shape[0] - TURNED + rotation[0] * part, 16)
        copies.append((up.at[pl.ds(at, part)], piece.at[pl.ds(size, part)]))
    copies = [pltpu.make_async_copy(*pair, refs[0].at[n]) for n, pair in enumerate(copies)]
    for copy in copies:
        copy.start()
    none = jnp.zeros((1, third), f32)
    biases = jnp.concatenate([wide(bias_qv)[:1], none, wide(bias_qv)[1:], none], 1)
    rest = jnp.zeros((SMALL - 2, biases.shape[1]), f32)
    result[third:] = jnp.concatenate([biases, wide(bias_up), rest], 0).astype(bf16)
    wait(copies)


def run_pack(count, rotation, bias_qv, bias_up, outer, up, down):
    third, width = outer.shape
    outputs = [shape((third + SMALL, width), bf16)]
    if count > 1:
        outputs += [shape(((down.shape[0] + TURNED) // count, width), bf16)]
    return pl.pallas_call(
        functools.partial(pack, count),
        name="pack",
        out_shape=outputs,
        in_specs=[SM, VM, VM, ANY, ANY, ANY],
        out_specs=[VM] * len(outputs),
        scratch_shapes=[pltpu.SemaphoreType.DMA((3,))],
    )(rotation, bias_qv, bias_up, outer, up, down)


def shape(dims, dtype):
    return jax.ShapeDtypeStruct(dims, dtype)


def launch(kernel, name, operands, weights, outputs, leaving, scratch, flops, scalars=0):
    size = sum(i.size * i.dtype.itemsize for i in [*operands, *weights, *outputs, *leaving])
    return pl.pallas_call(
        kernel,
        name=name,
        out_shape=list(leaving) + list(outputs),
        in_specs=[SM] * scalars + [VM] * (len(operands) - scalars) + [ANY] * len(weights),
        out_specs=[ANY] * len(leaving) + [VM] * len(outputs),
        scratch_shapes=scratch,
        compiler_params=pltpu.CompilerParams(vmem_limit_bytes=ROOM << 20),
        cost_estimate=pl.CostEstimate(flops=flops, bytes_accessed=size, transcendentals=0),
    )(*operands, *weights)


def vmem(*items):
    return [pltpu.VMEM(item.shape, item.dtype) for item in items]


def sems(*counts):
    return [pltpu.SemaphoreType.DMA((count if isinstance(count, tuple) else (count,))) for count in counts]


def sizes(w, which):
    up = w["mlp"][0][0].shape
    most = max(len(w["mlp"][s]) - 1 for s in which)
    rows = sum(block.shape[0] for block in w["mix"][0])
    return (
        shape((len(which), rows, up[0]), bf16),
        shape((len(which),) + up, bf16),
        shape((len(which),) + up[::-1], bf16),
        (len(which), 1 + 2 * most),
    )


def groups_of(w, which):
    return tuple(len(w["mix"][s]) for s in which)


def kinds_of(w, which):
    return tuple(len(w["mlp"][s]) - 1 for s in which)


def take(items, which):
    return [items[s] for s in which]


def flat(items, which):
    return [item for s in which for item in items[s]]


def kept_shapes(rows, w, which):
    size, width = rows.shape
    many, units = len(which), w["mlp"][0][0].shape[1]
    third = w["mix"][0][-1].shape[0] - SMALL
    return (
        shape((size, width), f32),
        shape((many, 3 * third, size), bf16),
        shape((many, third // HEAD, LEN, size), f32),
        shape((many, third, size), bf16),
        shape((size, width), bf16),
        shape((many, size, units), bf16),
        shape((many, size, units), bf16),
        shape((size, width), f32),
    )


def run_head_attention(place, share, rows, segments, blocks):
    size, width = rows.shape
    third = blocks[-1].shape[0] - SMALL
    sorted_rows = shape((2, third, size // SHARDS), bf16)
    return launch(
        functools.partial(head_attention, len(blocks), share),
        "head_attention",
        [place, rows, segments],
        blocks,
        [sorted_rows, sorted_rows],
        [],
        vmem(
            shape((1, 4 * third + SMALL, width), bf16),
            shape((3 * third, size), bf16),
            shape((third // HEAD, LEN, size), f32),
        )
        + sems((1, len(blocks))),
        6 * size * width * third,
        1,
    )


def run_mlp_forward(which, operands, outers, w):
    last = which == FAR_PAIR
    size, width = operands[0].shape
    many = len(outers)
    names = ("gain_one", "shift_one", "gain_two", "shift_two", "bias_down")
    whole = shape((size, width), f32)
    _, held_up, held_down, sem_mlp = sizes(w, which)
    return launch(
        functools.partial(mlp_forward, kinds_of(w, which), last),
        "mlp_forward",
        [w["rotation"], *[w[name] for name in names], *operands],
        outers + flat(w["mlp"], which),
        [shape((size, width), bf16) if last else whole, whole],
        [],
        vmem(held_up, held_down, shape((many,) + outers[0].shape, bf16)) + sems(sem_mlp, many),
        4 * size * held_up.size,
        1,
    )


def run_middle(rows, cotangent, segments, w):
    size, width = rows.shape
    held, held_up, held_down, sem_mlp = sizes(w, ALL)
    kept = kept_shapes(rows, w, ALL)
    names = ("gain_one", "shift_one", "gain_two", "shift_two", "bias_out", "bias_down")
    low = shape((size, width), bf16)
    _, mixed, probs, *_ = kept
    scratch = (
        vmem(*kept, held, held_up, held_down, shape((size, width), f32))
        + vmem(shape(probs.shape[1:], f32), shape(mixed.shape[1:], bf16))
        + sems((SHARDS, 3), sem_mlp, len(kept))
    )

    def kernel(*refs):
        ins = 10 + len(flat(w["mix"], ALL) + flat(w["mlp"], ALL))
        ends = ins + len(kept)
        middle(kinds_of(w, ALL), groups_of(w, ALL), *refs[:ins], *refs[ends : ends + 2], *refs[ins:ends], *refs[ends + 2 :])

    *kept, out, grad_in = launch(
        kernel,
        "middle",
        [w["rotation"], rows, cotangent, segments, *[w[name] for name in names]],
        flat(w["mix"], ALL) + flat(w["mlp"], ALL),
        [low, low],
        kept,
        scratch,
        8 * size * (held.size + held_up.size),
        1,
    )
    return out, grad_in, dict(zip(KEPT, kept))


def run_down_grads(cotangent, kept, w):
    size, width = cotangent.shape
    second, active = kept["second"], kept["active"]
    units = active.shape[2]
    part = shape((units, width), bf16)
    *parts, branch_two, grad_second, sums = launch(
        down_grads,
        "down_grads",
        [cotangent, w["gain_two"]],
        [second, active],
        [shape((size, width), bf16), shape((size, width), f32), shape((3, width), f32)],
        [part] * SHARDS,
        vmem(second, active, shape((SHARDS,) + part.shape, bf16)) + sems(1 + SHARDS, SHARDS),
        2 * SHARDS * size * units * width,
    )
    return parts, branch_two, grad_second, sums


def run_up_grads(branch_two, grad_second, sums, kept, w):
    size, width = branch_two.shape
    _, held_up, held_down, sem_mlp = sizes(w, ORDER)
    names = ("hidden", "slope", "first")
    hidden, slope, first = take(kept, names)
    part = shape(held_up.shape[1:], bf16)
    whole = shape((size, width), f32)
    *parts, grad_bias_up, sums, grad_first, branch_one = launch(
        functools.partial(up_grads, kinds_of(w, ORDER)),
        "up_grads",
        [w["rotation"], branch_two, w["gain_one"], sums],
        [hidden, slope, grad_second, first] + flat(w["mlp"], ORDER),
        [
            shape((SHARDS, 1, held_up.shape[2]), f32),
            shape((6, width), f32),
            whole,
            shape((size, width), bf16),
        ],
        [part] * SHARDS,
        vmem(whole, slope, hidden, first, held_up, held_down, held_up)
        + sems(3 + SHARDS, sem_mlp, SHARDS),
        6 * size * held_up.size,
        1,
    )
    return parts, grad_bias_up, sums, grad_first, branch_one


def run_attention_grads(branch_one, grad_first, rows, sums, grad_bias_up, kept, w):
    size, width = rows.shape
    held, _, _, _ = sizes(w, ORDER)
    names = ("mixed", "probs", "attended")
    mixed, probs, attended = take(kept, names)
    part = shape(held.shape[1:], bf16)
    *parts, grad_in = launch(
        functools.partial(attention_grads, groups_of(w, ORDER)),
        "attention_grads",
        [branch_one, rows, sums, grad_bias_up],
        [mixed, probs, attended, grad_first] + flat(w["mix"], ORDER),
        [shape((size, width), bf16)],
        [part] * SHARDS,
        vmem(grad_first, mixed, probs, attended, held, held, probs, mixed)
        + sems(3 * SHARDS + 1, (SHARDS, 3), SHARDS),
        4 * size * held.size,
    )
    return parts, grad_in


def to_partner(x, bits):
    size = lax.axis_size("tensor")
    return lax.ppermute(x, "tensor", [(i, i ^ bits) for i in range(size)])


def add(*items):
    return sum(item.astype(f32) for item in items).astype(bf16)


def tie(value, *others):
    return lax.optimization_barrier((value, *others))[0]


class Line:
    lag = 3

    def __init__(self):
        self.size = lax.axis_size("dp")
        place = lax.axis_index("dp")
        self.middle = (place == 1) | (place == 2)
        self.parts, self.sent, self.pairs, self.totals, self.done = [], [], [], [], []
        self.last = jnp.zeros((8, 128), bf16)

    def add(self, *items, cut=slice(None)):
        *items, _ = lax.optimization_barrier((*items, self.last))
        self.last = add(*[item[cut] for item in items])
        return self.last

    def exchange(self, keep=None, received=None, cut=None, far=None, settle=False):
        fresh = [] if far is None else [keep, received, far]
        if self.size != 4:
            if fresh:
                *values, _ = lax.optimization_barrier((*fresh, self.last))
                self.last = add(values[0][cut], values[1][cut], values[2])
                self.done.append(lax.psum(self.last, "dp"))
            return
        routes, items = [], []
        back = len(self.sent) - self.lag
        if back >= 0:
            items += list(self.pairs[back])
            routes += [(1, 0), (2, 3)]
        if fresh:
            routes += [(0, 1), (3, 2)]
        pair = self.pairs[-1:] if settle else []
        *values, pair, _ = lax.optimization_barrier((*items, *fresh, pair, self.last))
        if settle:
            self.pairs[-1:] = pair
        total = part = None
        if fresh:
            keep, received, far = values[len(items) :]
            self.parts.append((keep, received, cut, far))
            part = add(keep[cut], received[cut], far)
        if back >= 0:
            total = add(*values[:2])
            self.totals.append(total)
        if total is None or part is None:
            operand = part if total is None else total
        else:
            rows = max(total.shape[0], part.shape[0])
            wide_total, part = [
                jnp.pad(v, ((0, rows - v.shape[0]), (0, 0))) for v in (total, part)
            ]
            operand = jnp.where(self.middle, wide_total, part)
        self.last = operand
        answer = lax.ppermute(operand, "dp", routes)
        self.sent.append(answer)
        if back >= 0:
            self.done.append(jnp.where(self.middle, total, answer[: total.shape[0]]))

    def inner(self):
        if self.size != 4:
            return
        keep, received, cut, far = self.parts[len(self.pairs)]
        answer = self.sent[len(self.pairs)]
        *values, _ = lax.optimization_barrier((keep, received, far, answer, self.last))
        keep, received, far, answer = values
        self.last = add(keep[cut], received[cut], far, answer[: far.shape[0]])
        self.pairs.append((self.last, lax.ppermute(self.last, "dp", [(1, 2), (2, 1)])))


def all_rows(own, near, far, both):
    place = lax.axis_index("tensor")
    low, high = place % 2 == 1, place // 2 == 1
    first = [jnp.where(low, near, own), jnp.where(low, own, near)]
    second = [jnp.where(low, both, far), jnp.where(low, far, both)]
    return [jnp.where(high, b, a) for a, b in zip(first, second)] + [
        jnp.where(high, a, b) for a, b in zip(first, second)
    ]


def body(
    ends_in,
    segment_ids,
    w_qkv,
    bias_qv,
    w_out,
    bias_out,
    gain_one,
    shift_one,
    w_up,
    bias_up,
    w_down,
    bias_down,
    gain_two,
    shift_two,
):
    section = lax.axis_index("section")
    place = lax.axis_index("tensor")
    _, micro, count, length, width = ends_in.shape
    share = count // lax.axis_size("tensor")
    own = lax.dynamic_slice_in_dim(ends_in[0], place * share, share, 1)
    own = own.reshape(micro * share * length, width)
    segments = lax.dynamic_slice_in_dim(segment_ids, place * share, share, 1)
    segments = segments.reshape(micro * share, length)
    third = w_qkv.shape[3]
    rotation = lax.axis_index("dp").astype(jnp.int32).reshape(1)
    w = {
        "rotation": rotation,
        "bias_out": bias_out,
        "gain_one": gain_one,
        "shift_one": shift_one,
        "bias_down": bias_down,
        "gain_two": gain_two,
        "shift_two": shift_two,
    }
    up, down, qkv = w_up[0], w_down[0], w_qkv[0].reshape(width, -1).T
    turns = lax.axis_size("dp") if lax.axis_size("dp") == 4 else 1
    outer, *piece = run_pack(turns, rotation, bias_qv[0], bias_up, w_out[0], up, down)
    piece = [to_partner(item, 2) for item in piece]
    outer_near, up_near, down_near = [to_partner(item, 1) for item in (outer, up, down)]
    near_sent, far_sent = run_head_attention(
        lax.axis_index("tensor").astype(jnp.int32).reshape(1),
        share,
        ends_in[0].reshape(-1, width),
        segment_ids.reshape(-1, length),
        [qkv, outer],
    )
    far_sent, near_sent, outer_near, up_near, down_near, *piece = lax.optimization_barrier(
        (far_sent, near_sent, outer_near, up_near, down_near, *piece)
    )

    def turned(item, turn):
        return lax.ppermute(item, "dp", [(i, (i + turn) % turns) for i in range(turns)])

    one, three = [[turned(item, turn) for item in piece] for turn in (1, turns - 1)]
    outer_far = to_partner(tie(outer, far_sent), 2)
    far_in = to_partner(far_sent, 2)
    near_in = to_partner(near_sent, 1)
    far_in, near_in, outer_far, *one = lax.optimization_barrier((far_in, near_in, outer_far, *one))
    both_in, outer_both = to_partner(far_in, 1), to_partner(outer_far, 1)
    two = [turned(item, 1) for item in one]
    direct = up.shape[0] - (TURNED if turns > 1 else 0)
    far = [to_partner(tie(up[:direct], far_in), 2)]
    if turns == 1:
        far.append(to_partner(tie(down, far_in), 2))
    w["mlp"] = [[up, down], [up_near, down_near]]
    outers = [outer, outer_near, outer_far, outer_both]
    w["mix"] = [[qkv, outer]]
    first, second = run_mlp_forward(
        NEAR_PAIR, [own, bias_out, near_sent, near_in, far_in, both_in], outers, w
    )
    pieces, _ = lax.optimization_barrier((piece + one + two + three, first))
    pieces_near = [to_partner(item, 1) for item in pieces]
    far, pieces_near = lax.optimization_barrier((far, pieces_near))
    w["mlp"] += [far + pieces, [to_partner(item, 1) for item in far] + pieces_near]
    cut = 5 * qkv.shape[0] // 9
    query_far = to_partner(tie(qkv[:cut], *far), 2)
    qkv_near = to_partner(tie(qkv, *pieces_near), 1)
    out, _ = run_mlp_forward(FAR_PAIR, [first, second], outers[2:], w)
    out, query_far, qkv_near = lax.optimization_barrier((out, query_far, qkv_near))
    keys_far = to_partner(tie(qkv[cut:], query_far), 2)
    w["mix"] += [
        [qkv_near, outer_near],
        [query_far, keys_far, outer_far],
        [to_partner(query_far, 1), to_partner(keys_far, 1), outer_both],
    ]
    received = lax.ppermute(out, "section", [(0, 1)])
    rows = jnp.where(section == 0, own, received)
    out, grad_in, kept = run_middle(rows, own, segments, w)
    returned = lax.ppermute(grad_in, "section", [(1, 0)])
    cotangent = jnp.where(section == 1, own, returned)

    line = Line()

    def swap(send):
        return to_partner(tie(send, line.last), 1)

    def halves(keep):
        half = keep.shape[0] // 2 // 16 * 16
        return slice(0, half), slice(half, None)

    def cross(keep, received):
        return [to_partner(line.add(keep, received, cut=cut), 2) for cut in halves(keep)]

    def chunks(keep, received, far):
        return [(keep, received, cut, item) for cut, item in zip(halves(keep), far)]

    down, branch_two, grad_second, sums = run_down_grads(cotangent, kept, w)
    line.last = branch_two
    down_far = cross(down[0], swap(down[1]))
    received = swap(down[3])
    up, grad_bias_up, sums, grad_first, branch_one = run_up_grads(
        tie(branch_two, line.last), grad_second, sums, kept, w
    )
    line.last = branch_one
    down = chunks(down[2], received, down_far)
    line.exchange(*down[0])
    received = swap(up[1])
    mixer, grad_in = run_attention_grads(
        tie(branch_one, line.last), grad_first, rows, sums, grad_bias_up, kept, w
    )
    line.last = grad_in
    up_far = cross(up[0], received)
    line.exchange(*down[1])
    line.inner()
    mixer_received, up_received = swap(mixer[1]), swap(up[3])
    up = chunks(up[2], up_received, up_far)
    mixer_far = cross(mixer[0], mixer_received)
    line.exchange(*up[0])
    line.inner()
    mixer = chunks(mixer[2], swap(mixer[3]), mixer_far)
    line.exchange(*up[1])
    line.inner()
    mine = jnp.where(section == 1, out, grad_in).reshape(micro, share, length, width)
    line.exchange(*mixer[0], settle=True)
    line.inner()
    line.exchange(*mixer[1])
    mine = tie(mine, line.last)
    mine_far = to_partner(mine, 2)
    line.inner()
    line.exchange()
    line.inner()
    line.exchange()
    mine, mine_far, _ = lax.optimization_barrier((mine, mine_far, line.last))
    near = to_partner(mine, 1), to_partner(mine_far, 1)
    line.exchange()
    mine, near, mine_far, both, _ = lax.optimization_barrier(
        (mine, near[0], mine_far, near[1], line.last)
    )
    ends = all_rows(mine, near, mine_far, both)
    down, up, mixer = line.done[:2], line.done[2:4], line.done[4:]
    half = mixer[0].shape[0]
    qkv = jnp.concatenate([mixer[0][third:], mixer[1][: 4 * third - half]], 0)
    small = mixer[1][4 * third - half :]
    results = (
        jnp.concatenate(ends, 1),
        qkv.T.reshape(width, 3, third),
        small[1:3, :third],
        mixer[0][:third],
        small[6],
        small[7],
        small[8],
        jnp.concatenate(up, 0),
        small[0],
        jnp.concatenate(down, 0),
        small[3],
        small[4],
        small[5],
    )
    return tuple(item.astype(f32)[None] for item in results)


def solution(mesh):
    return jax.shard_map(
        body,
        mesh=mesh,
        in_specs=(
            P("section", None, "dp", None, None),
            P(None, "dp", None),
            P("section", None, None, "tensor"),
            P("section", None, "tensor"),
            P("section", "tensor", None),
            P("section", None),
            P("section", None),
            P("section", None),
            P("section", None, "tensor"),
            P("section", "tensor"),
            P("section", "tensor", None),
            P("section", None),
            P("section", None),
            P("section", None),
        ),
        out_specs=(
            P("section", None, "dp", None, None),
            P("section", None, None, "tensor"),
            P("section", None, "tensor"),
            P("section", "tensor", None),
            P("section", None),
            P("section", None),
            P("section", None),
            P("section", None, "tensor"),
            P("section", "tensor"),
            P("section", "tensor", None),
            P("section", None),
            P("section", None),
            P("section", None),
        ),
        check_vma=False,
    )
```

```python
import functools
import jax
import jax.numpy as jnp
from jax import lax
from jax.experimental import pallas as pl
from jax.experimental.pallas import tpu as pltpu
from jax.sharding import PartitionSpec as P

HEAD = 64
LEN = 128
SHARDS = 4
SMALL = 16
TURNED = 256
ROOM = 56
NEAR_PAIR, FAR_PAIR, ALL = (0, 1), (2, 3), (0, 1, 2, 3)
epsilon = 1e-05
bf16 = jnp.bfloat16
f32 = jnp.float32
ANY = pl.BlockSpec(memory_space=pl.ANY)
VM = pl.BlockSpec(memory_space=pltpu.VMEM)
SM = pl.BlockSpec(memory_space=pltpu.SMEM)


def nn(left, right):
    return lax.dot_general(left, right, (((1,), (0,)), ((), ())), preferred_element_type=f32)


def nt(left, right):
    return lax.dot_general(left, right, (((1,), (1,)), ((), ())), preferred_element_type=f32)


def tn(left, right):
    return lax.dot_general(left, right, (((0,), (0,)), ((), ())), preferred_element_type=f32)


def standardize(summed):
    center = summed - jnp.mean(summed, -1, keepdims=True)
    inverse = lax.rsqrt(jnp.mean(center * center, -1, keepdims=True) + epsilon)
    return center * inverse, inverse


def norm_back(normed, inverse, gain, grad_output):
    scaled = grad_output * gain
    return inverse * (
        scaled
        - jnp.mean(scaled, -1, keepdims=True)
        - normed * jnp.mean(scaled * normed, -1, keepdims=True)
    )


def wide(ref):
    return ref[...].astype(f32)


def load(sources, held, sems):
    copies = [
        pltpu.make_async_copy(src, held.at[n], sems.at[n]) for n, src in enumerate(sources)
    ]
    for copy in copies:
        copy.start()
    return copies


def load_mixers(groups, refs, held, sems, after=lambda n: None):
    refs = list(refs)
    loads = []
    for n, group in enumerate(groups):
        at, copies = 0, []
        for i in range(group):
            block = refs.pop(0)
            size = block.shape[0]
            target = held.at[n, pl.ds(at, size)]
            copies.append(pltpu.make_async_copy(block, target, sems.at[n, i]))
            copies[-1].start()
            at += size
        loads.append(copies)
        after(n)
    return loads


def load_mlp(kinds, refs, rotation, held_up, held_down, sems, up_first, before=lambda n: None):
    refs = list(refs)
    ups, downs = [], []
    for n, kind in enumerate(kinds):
        first = refs.pop(0)
        half = first.shape[0]
        up = [pltpu.make_async_copy(first, held_up.at[n, pl.ds(0, half)], sems.at[n, 0])]
        down = []
        if kind == 1:
            down.append(pltpu.make_async_copy(refs.pop(0), held_down.at[n], sems.at[n, 1]))
        else:
            size = held_down.shape[1] // kind
            rest = (held_up.shape[1] - half) // kind
            for turn in range(kind):
                piece = refs.pop(0)
                place = lax.rem(rotation[0] + (kind - turn), kind)
                at = pl.ds(pl.multiple_of(place * size, 16), size)
                down.append(
                    pltpu.make_async_copy(
                        piece.at[pl.ds(0, size)], held_down.at[n, at], sems.at[n, 1 + turn]
                    )
                )
                at = pl.ds(pl.multiple_of(half + place * rest, 16), rest)
                up.append(
                    pltpu.make_async_copy(
                        piece.at[pl.ds(size, rest)], held_up.at[n, at], sems.at[n, 1 + kind + turn]
                    )
                )
        before(n)
        for copy in up + down if up_first else down + up:
            copy.start()
        ups.append(up)
        downs.append(down)
    return ups, downs


def wait(copies):
    for copy in copies:
        copy.wait()


def fetch(pairs, sems):
    copies = [pltpu.make_async_copy(*pair, sems.at[n]) for n, pair in enumerate(pairs)]
    for copy in copies:
        copy.start()
    return copies


def fetch_own(place, ends, own, sems):
    micro, count, length, _ = ends.shape
    share = count // SHARDS
    pairs = [
        (ends.at[m, place[0] * share + j], own.at[pl.ds((m * share + j) * length, length)])
        for m in range(micro)
        for j in range(share)
    ]
    return fetch(pairs, sems)


def by_sequence(count, value):
    return jnp.concatenate([value(slice(i * LEN, (i + 1) * LEN)) for i in range(count)], 1)


def same_segment(segments):
    ids = segments[...].astype(f32)
    if ids.ndim == 3:
        ids = jnp.concatenate([ids[i] for i in range(ids.shape[0])], 0)
    count = ids.shape[0]
    ids_down = jnp.concatenate([ids, jnp.zeros((-count % 8, LEN), f32)], 0).T
    return jnp.concatenate([ids_down[:, i : i + 1] == ids[i : i + 1] for i in range(count)], 1)


def attend(weights, x, same, mixed_out, probs_out):
    count = x.shape[0] // LEN
    third = (weights.shape[0] - SMALL) // 4
    bias = weights[4 * third :].astype(f32)[:8].T[: 3 * third, :1]
    mixed = (nt(weights[: 3 * third], x) + bias).astype(bf16)
    mixed_out[:third] = mixed[:third] * HEAD**-0.5
    mixed_out[third:] = mixed[third:]
    heads = range(third // HEAD)
    for h in heads:
        query = mixed_out[h * HEAD : (h + 1) * HEAD]
        keys = mixed_out[third + h * HEAD : third + (h + 1) * HEAD]
        probs_out[h] = by_sequence(count, lambda cols: tn(keys[:, cols], query[:, cols]))
    for h in heads:
        scores = jnp.where(same, probs_out[h], -1e9)
        probs = jnp.exp(scores - jnp.max(scores, 0, keepdims=True))
        probs_out[h] = probs * (1.0 / jnp.sum(probs, 0, keepdims=True))
    attended = []
    for h in heads:
        value = mixed_out[2 * third + h * HEAD : 2 * third + (h + 1) * HEAD]
        low = probs_out[h].astype(bf16)
        attended.append(by_sequence(count, lambda cols: nn(value[:, cols], low[:, cols])))
    return jnp.concatenate(attended, 0).astype(bf16)


def attend_back(mixed, probs, grads, scores, result):
    third, size = grads.shape
    count = size // LEN
    heads = range(third // HEAD)
    for h in heads:
        at = slice(h * HEAD, (h + 1) * HEAD)
        value, grad = mixed[2 * third + at.start : 2 * third + at.stop], grads[at]
        scores[h] = by_sequence(count, lambda cols: tn(value[:, cols], grad[:, cols]))
    for h in heads:
        prob, grad = probs[h], scores[h]
        inner = jnp.sum(prob * grad, 0, keepdims=True)
        scores[h] = prob * (grad - inner)
    for h in heads:
        at = slice(h * HEAD, (h + 1) * HEAD)
        query, keys = mixed[at], mixed[third + at.start : third + at.stop]
        grad, low, score = grads[at], probs[h].astype(bf16), scores[h].astype(bf16)
        queries = by_sequence(count, lambda cols: nn(keys[:, cols], score[:, cols])) * HEAD**-0.5
        result[at] = queries.astype(bf16)
        result[third + at.start : third + at.stop] = by_sequence(
            count, lambda cols: nt(query[:, cols], score[:, cols])
        ).astype(bf16)
        result[2 * third + at.start : 2 * third + at.stop] = by_sequence(
            count, lambda cols: nt(grad[:, cols], low[:, cols])
        ).astype(bf16)


def head_attention(group, share, place, rows, segments, *refs):
    blocks, (near, far, held, mixed, probs, sems) = refs[:group], refs[group:]
    copies = load_mixers([group], blocks, held, sems)
    same = same_segment(segments)
    wait(copies[0])
    attended = attend(held.at[0], rows[...], same, mixed, probs)
    count = share * SHARDS
    for i in range(rows.shape[0] // LEN):
        owner = lax.bitwise_xor(place[0], i % count // share)
        at = i // count * share + i % share
        cols = slice(at * LEN, (at + 1) * LEN)
        block = attended[:, i * LEN : (i + 1) * LEN]

        @pl.when(owner < 2)
        def _(owner=owner, cols=cols, block=block):
            near[owner, :, cols] = block

        @pl.when(owner >= 2)
        def _(owner=owner, cols=cols, block=block):
            far[owner - 2, :, cols] = block


def gelu(upward):
    normal = 0.5 * (1.0 + lax.erf(upward * 0.7071067811865476))
    return normal, (upward * normal).astype(bf16)


def mlp_forward(kinds, last, *refs):
    rotation, *refs = refs
    if not last:
        place, *refs = refs
    gain_one, shift_one, gain_two, shift_two, bias_down, *rest = refs
    many = len(kinds)
    if last:
        kept, rest = rest[:2], rest[2:]
    else:
        bias_out, near, near_in, far_in, both_in, ends, *rest = rest
    count = many if last else SHARDS
    outers, rest = rest[:count], rest[count:]
    ins = sum(1 + kind for kind in kinds)
    weights, rest = rest[:ins], rest[ins:]
    if last:
        result, first, second, held_up, held_down, held_outer, sems, sem_outer, sem_kept = rest
        starts = fetch(zip(kept, (first, second)), sem_kept)
    else:
        result, second, rows, held_up, held_down, held_outer, sems, sem_outer, sem_own = rest
        own_loads = fetch_own(place, ends, rows, sem_own)
    loads = load(outers, held_outer, sem_outer)
    ups, downs = load_mlp(kinds, weights, rotation, held_up, held_down, sems, True)
    third = held_outer.shape[1] - SMALL
    if not last:
        first = result
        wait(own_loads)
        first[...] = rows[...].astype(f32) + wide(bias_out)
        parts = near[0], near_in[1], far_in[0], both_in[1]
        for n, part in enumerate(parts):
            loads[n].wait()
            first[...] += tn(part, held_outer[n, :third])
    else:
        starts[0].wait()
    normed, _ = standardize(first[...])
    hidden = normed * wide(gain_one) + wide(shift_one)
    hidden_low = hidden.astype(bf16)
    if last:
        wait([*loads, starts[1]])
    else:
        second[...] = hidden + wide(bias_down)
    for n in range(many):
        wait(ups[n])
        upward = nn(hidden_low, held_up[n]) + held_outer[n, third:].astype(f32)[1:2]
        _, active = gelu(upward)
        wait(downs[n])
        second[...] += nn(active, held_down[n])
    if last:
        normed, _ = standardize(second[...])
        result[...] = (normed * wide(gain_two) + wide(shift_two)).astype(bf16)


KEPT = ("first", "mixed", "probs", "attended", "hidden", "active", "slope", "second")


def middle(kinds, groups, *refs):
    rotation, section, received, cotangent, segments, *rest = refs
    gain_one, shift_one, gain_two, shift_two, bias_out, bias_down, *rest = rest
    many = len(kinds)
    mixers, rest = rest[: sum(groups)], rest[sum(groups) :]
    ins = sum(1 + kind for kind in kinds)
    weights, rest = rest[:ins], rest[ins:]
    out, grad_in, rows, *rest = rest
    leaving, rest = rest[: len(KEPT)], rest[len(KEPT) :]
    first, mixed, probs, attended, hidden_out, active_out, slope_out, second = rest[: len(KEPT)]
    held, held_up, held_down, total, scores, grad_mixed, *rest = rest[len(KEPT) :]
    sem_mix, sem_mlp, sem_out = rest
    staying = first, mixed, probs, attended, hidden_out, active_out, slope_out, second
    leave = [pltpu.make_async_copy(*pair, sem_out.at[n]) for n, pair in enumerate(zip(staying, leaving))]

    copies = load_mixers(groups, mixers, held, sem_mix)
    x = jnp.where(section[0] == 0, wide(cotangent), wide(received)).astype(bf16)
    rows[...] = x
    first[...] = x.astype(f32) + wide(bias_out)
    same = same_segment(segments)
    third = (held.shape[1] - SMALL) // 4
    wait(sum(copies, []))
    ups, downs = load_mlp(kinds, weights, rotation, held_up, held_down, sem_mlp, True)

    @pl.loop(0, many, unroll=2)
    def _(n):
        attended[n] = attend(held.at[n], x, same, mixed.at[n], probs.at[n])
        first[...] += tn(attended[n], held[n, 3 * third : 4 * third])

    for copy in leave[:4]:
        copy.start()
    normed_one, inverse_one = standardize(first[...])
    hidden = normed_one * wide(gain_one) + wide(shift_one)
    hidden_low = hidden.astype(bf16)
    hidden_out[...] = hidden_low
    second[...] = hidden + wide(bias_down)
    wait(sum(ups + downs, []))

    @pl.loop(0, many, unroll=4)
    def _(n):
        upward = nn(hidden_out[...], held_up[n]) + held[n, 4 * third :].astype(f32)[1:2]
        normal, active = gelu(upward)
        active_out[n] = active
        density = jnp.exp(-0.5 * upward * upward) * 0.3989422804014327
        slope_out[n] = (normal + upward * density).astype(bf16)
        second[...] += nn(active, held_down[n])

    for copy in leave[4:]:
        copy.start()
    normed, inverse = standardize(second[...])
    out[...] = (normed * wide(gain_two) + wide(shift_two)).astype(bf16)

    back = norm_back(normed, inverse, wide(gain_two), wide(cotangent))
    grad_in[...] = back.astype(bf16)
    total[...] = back

    @pl.loop(0, many, unroll=4)
    def _(n):
        grad_upward = (nt(grad_in[...], held_down[n]) * slope_out[n].astype(f32)).astype(bf16)
        total[...] += nt(grad_upward, held_up[n])

    normed, inverse = standardize(first[...])
    back = norm_back(normed, inverse, wide(gain_one), total[...])
    grad_in[...] = back.astype(bf16)
    total[...] = back

    @pl.loop(0, many, unroll=2)
    def _(n):
        grads = nt(held[n, 3 * third : 4 * third], grad_in[...]).astype(bf16)
        attend_back(mixed.at[n], probs.at[n], grads, scores, grad_mixed)
        total[...] += tn(grad_mixed[...], held[n, : 3 * third])

    grad_in[...] = total[...].astype(bf16)
    wait(leave)


ORDER = (2, 3, 0, 1)


def down_grads(*refs):
    section, own, returned, gain_two, *rest = refs
    kept, parts, rest = rest[:2], rest[2 : 2 + SHARDS], rest[2 + SHARDS :]
    branch_two, grad_second, sums, second, active, store, sem_kept, sem_out = rest
    loads = fetch(
        [(kept[0], second)] + [(kept[1].at[s], active.at[s]) for s in ORDER], sem_kept
    )
    g = jnp.where(section[0] == 0, wide(returned), wide(own))
    loads[0].wait()
    normed, inverse = standardize(second[...])
    back = norm_back(normed, inverse, wide(gain_two), g)
    grad_second[...] = back
    low = back.astype(bf16)
    branch_two[...] = low
    leave = []
    for n, s in enumerate(ORDER):
        loads[1 + n].wait()
        store[n] = tn(active[s], low).astype(bf16)
        leave.append(pltpu.make_async_copy(store.at[n], parts[n], sem_out.at[n]))
        leave[-1].start()
    sums[0:1] = jnp.sum(back, 0, keepdims=True)
    sums[1:2] = jnp.sum(g * normed, 0, keepdims=True)
    sums[2:3] = jnp.sum(g, 0, keepdims=True)
    wait(leave)


def up_grads(kinds, *refs):
    rotation, branch_two, gain_one, sums_two, *rest = refs
    kept, rest = rest[:4], rest[4:]
    many = len(kinds)
    ins = sum(1 + kind for kind in kinds)
    weights, rest = rest[:ins], rest[ins:]
    parts, rest = rest[:many], rest[many:]
    grad_bias_up, sums, grad_first, branch_one, *rest = rest
    total, slope, hidden, first, held_up, held_down, store, *rest = rest
    sem_kept, sem_mlp, sem_out = rest
    loads = [
        pltpu.make_async_copy(source, target, sem_kept.at[n])
        for n, (source, target) in enumerate(
            [(kept[0], hidden)]
            + [(kept[1].at[s], slope.at[s]) for s in ORDER]
            + [(kept[2], total), (kept[3], first)]
        )
    ]
    loads[0].start()
    ups, downs = load_mlp(
        kinds, weights, rotation, held_up, held_down, sem_mlp, False, lambda n: loads[1 + n].start()
    )
    loads[-2].start()
    loads[-1].start()
    low = branch_two[...]
    loads[0].wait()
    flipped = hidden[...].T
    leave = []
    for n, s in enumerate(ORDER):
        wait(downs[n])
        loads[1 + n].wait()
        grad_upward = (nt(low, held_down[n]) * slope[s].astype(f32)).astype(bf16)
        store[n] = nn(flipped, grad_upward).astype(bf16)
        leave.append(pltpu.make_async_copy(store.at[n], parts[n], sem_out.at[n]))
        leave[-1].start()
        grad_bias_up[n] = jnp.sum(grad_upward.astype(f32), 0, keepdims=True)
        wait(ups[n])
        if n == 0:
            loads[-2].wait()
        total[...] += nt(grad_upward, held_up[n])
    grad_hidden = total[...]
    loads[-1].wait()
    normed, inverse = standardize(first[...])
    back = norm_back(normed, inverse, wide(gain_one), grad_hidden)
    grad_first[...] = back
    branch_one[...] = back.astype(bf16)
    sums[0:3] = sums_two[...]
    sums[3:4] = jnp.sum(back, 0, keepdims=True)
    sums[4:5] = jnp.sum(grad_hidden * normed, 0, keepdims=True)
    sums[5:6] = jnp.sum(grad_hidden, 0, keepdims=True)
    wait(leave)


def attention_grads(groups, *refs):
    branch_one, rows, sums, grad_bias_up, *rest = refs
    kept, rest = rest[:4], rest[4:]
    mixers, rest = rest[: sum(groups)], rest[sum(groups) :]
    parts, rest = rest[:SHARDS], rest[SHARDS:]
    grad_in, total, mixed, probs, attended, held, store, scores, grad_mixed, *rest = rest
    sem_kept, sem_mix, sem_out = rest
    pairs = []
    for s in ORDER:
        pairs += [(kept[i].at[s], item.at[s]) for i, item in enumerate((mixed, probs, attended))]
    pairs.append((kept[3], total))
    loads = [pltpu.make_async_copy(*pair, sem_kept.at[n]) for n, pair in enumerate(pairs)]

    def begin(n):
        for copy in loads[3 * n : 3 * n + 3]:
            copy.start()

    copies = load_mixers(groups, mixers, held, sem_mix, begin)
    loads[-1].start()
    branch = branch_one[...]
    x = rows[...]
    ones = jnp.ones((16, x.shape[0]), bf16)
    third = (held.shape[1] - SMALL) // 4
    blank = jnp.zeros((1, x.shape[1] - third), f32)
    leave = []
    for n, s in enumerate(ORDER):
        wait(copies[n])
        wait(loads[3 * n : 3 * n + 3])
        grads = nt(held[n, 3 * third : 4 * third], branch).astype(bf16)
        store[n, :third] = nn(attended[s], branch).astype(bf16)
        attend_back(mixed.at[s], probs.at[s], grads, scores.at[n], grad_mixed.at[n])
        back = grad_mixed[n]
        store[n, third : 4 * third] = nn(back, x).astype(bf16)
        columns = nt(ones, back)
        small = [
            grad_bias_up[n],
            jnp.concatenate([columns[:1, :third], blank], 1),
            jnp.concatenate([columns[:1, 2 * third :], blank], 1),
            sums[...],
            jnp.zeros((SMALL - 9, x.shape[1]), f32),
        ]
        store[n, 4 * third :] = jnp.concatenate(small, 0).astype(bf16)
        leave.append(pltpu.make_async_copy(store.at[n], parts[n], sem_out.at[n]))
        leave[-1].start()
        if n == 0:
            loads[-1].wait()
        total[...] += tn(back, held[n, : 3 * third])
    grad_in[...] = total[...].astype(bf16)
    wait(leave)


def pack(count, rotation, bias_qv, bias_up, outer, up, down, *refs):
    third = outer.shape[0]
    result, *refs = refs
    copies = [(outer, result.at[pl.ds(0, third)])]
    if count > 1:
        piece, *refs = refs
        size, part = down.shape[0] // count, TURNED // count
        at = pl.multiple_of(rotation[0] * size, 16)
        copies.append((down.at[pl.ds(at, size)], piece.at[pl.ds(0, size)]))
        at = pl.multiple_of(up.shape[0] - TURNED + rotation[0] * part, 16)
        copies.append((up.at[pl.ds(at, part)], piece.at[pl.ds(size, part)]))
    copies = [pltpu.make_async_copy(*pair, refs[0].at[n]) for n, pair in enumerate(copies)]
    for copy in copies:
        copy.start()
    none = jnp.zeros((1, third), f32)
    biases = jnp.concatenate([wide(bias_qv)[:1], none, wide(bias_qv)[1:], none], 1)
    rest = jnp.zeros((SMALL - 2, biases.shape[1]), f32)
    result[third:] = jnp.concatenate([biases, wide(bias_up), rest], 0).astype(bf16)
    wait(copies)


def run_pack(count, rotation, bias_qv, bias_up, outer, up, down):
    third, width = outer.shape
    outputs = [shape((third + SMALL, width), bf16)]
    if count > 1:
        outputs += [shape(((down.shape[0] + TURNED) // count, width), bf16)]
    return pl.pallas_call(
        functools.partial(pack, count),
        name="pack",
        out_shape=outputs,
        in_specs=[SM, VM, VM, ANY, ANY, ANY],
        out_specs=[VM] * len(outputs),
        scratch_shapes=[pltpu.SemaphoreType.DMA((3,))],
    )(rotation, bias_qv, bias_up, outer, up, down)


def shape(dims, dtype):
    return jax.ShapeDtypeStruct(dims, dtype)


def launch(kernel, name, operands, weights, outputs, leaving, scratch, flops, scalars=0):
    size = sum(i.size * i.dtype.itemsize for i in [*operands, *weights, *outputs, *leaving])
    return pl.pallas_call(
        kernel,
        name=name,
        out_shape=list(leaving) + list(outputs),
        in_specs=[SM] * scalars + [VM] * (len(operands) - scalars) + [ANY] * len(weights),
        out_specs=[ANY] * len(leaving) + [VM] * len(outputs),
        scratch_shapes=scratch,
        compiler_params=pltpu.CompilerParams(vmem_limit_bytes=ROOM << 20),
        cost_estimate=pl.CostEstimate(flops=flops, bytes_accessed=size, transcendentals=0),
    )(*operands, *weights)


def vmem(*items):
    return [pltpu.VMEM(item.shape, item.dtype) for item in items]


def sems(*counts):
    return [pltpu.SemaphoreType.DMA((count if isinstance(count, tuple) else (count,))) for count in counts]


def sizes(w, which):
    up = w["mlp"][0][0].shape
    most = max(len(w["mlp"][s]) - 1 for s in which)
    rows = sum(block.shape[0] for block in w["mix"][0])
    return (
        shape((len(which), rows, up[0]), bf16),
        shape((len(which),) + up, bf16),
        shape((len(which),) + up[::-1], bf16),
        (len(which), 1 + 2 * most),
    )


def groups_of(w, which):
    return tuple(len(w["mix"][s]) for s in which)


def kinds_of(w, which):
    return tuple(len(w["mlp"][s]) - 1 for s in which)


def take(items, which):
    return [items[s] for s in which]


def flat(items, which):
    return [item for s in which for item in items[s]]


def kept_shapes(rows, w, which):
    size, width = rows.shape
    many, units = len(which), w["mlp"][0][0].shape[1]
    third = w["mix"][0][-1].shape[0] - SMALL
    return (
        shape((size, width), f32),
        shape((many, 3 * third, size), bf16),
        shape((many, third // HEAD, LEN, size), f32),
        shape((many, third, size), bf16),
        shape((size, width), bf16),
        shape((many, size, units), bf16),
        shape((many, size, units), bf16),
        shape((size, width), f32),
    )


def run_head_attention(place, share, rows, segments, blocks):
    size, width = rows.shape
    third = blocks[-1].shape[0] - SMALL
    sorted_rows = shape((2, third, size // SHARDS), bf16)
    return launch(
        functools.partial(head_attention, len(blocks), share),
        "head_attention",
        [place, rows, segments],
        blocks,
        [sorted_rows, sorted_rows],
        [],
        vmem(
            shape((1, 4 * third + SMALL, width), bf16),
            shape((3 * third, size), bf16),
            shape((third // HEAD, LEN, size), f32),
        )
        + sems((1, len(blocks))),
        6 * size * width * third,
        1,
    )


def run_mlp_forward(which, operands, sources, outers, w):
    last = which == FAR_PAIR
    width = w["bias_out"].shape[1]
    size = sources[0].size // width // (1 if last else SHARDS)
    names = ("gain_one", "shift_one", "gain_two", "shift_two", "bias_down")
    whole = shape((size, width), f32)
    low = shape((size, width), bf16)
    _, held_up, held_down, sem_mlp = sizes(w, which)
    many = len(outers)
    scratch = vmem(held_up, held_down, shape((many,) + outers[0].shape, bf16)) + sems(sem_mlp, many)
    scalars = [w["rotation"]] if last else [w["rotation"], w["place"]]
    return launch(
        functools.partial(mlp_forward, kinds_of(w, which), last),
        "mlp_forward",
        [*scalars, *[w[name] for name in names], *operands],
        sources + outers + flat(w["mlp"], which),
        [low] if last else [whole, whole],
        [],
        vmem(whole, whole) + scratch + sems(2)
        if last
        else vmem(low) + scratch + sems(size // LEN),
        4 * size * held_up.size,
        len(scalars),
    )


def run_middle(received, cotangent, segments, w):
    size, width = received.shape
    held, held_up, held_down, sem_mlp = sizes(w, ALL)
    kept = kept_shapes(received, w, ALL)
    names = ("gain_one", "shift_one", "gain_two", "shift_two", "bias_out", "bias_down")
    low = shape((size, width), bf16)
    _, mixed, probs, *_ = kept
    scratch = (
        vmem(*kept, held, held_up, held_down, shape((size, width), f32))
        + vmem(shape(probs.shape[1:], f32), shape(mixed.shape[1:], bf16))
        + sems((SHARDS, 3), sem_mlp, len(kept))
    )

    def kernel(*refs):
        ins = 11 + len(flat(w["mix"], ALL) + flat(w["mlp"], ALL))
        ends = ins + len(kept)
        middle(
            kinds_of(w, ALL),
            groups_of(w, ALL),
            *refs[:ins],
            *refs[ends : ends + 3],
            *refs[ins:ends],
            *refs[ends + 3 :],
        )

    *kept, out, grad_in, rows = launch(
        kernel,
        "middle",
        [w["rotation"], w["section"], received, cotangent, segments, *[w[name] for name in names]],
        flat(w["mix"], ALL) + flat(w["mlp"], ALL),
        [low, low, low],
        kept,
        scratch,
        8 * size * (held.size + held_up.size),
        2,
    )
    return out, grad_in, rows, dict(zip(KEPT, kept))


def run_down_grads(own, returned, kept, w):
    size, width = own.shape
    second, active = kept["second"], kept["active"]
    units = active.shape[2]
    part = shape((units, width), bf16)
    *parts, branch_two, grad_second, sums = launch(
        down_grads,
        "down_grads",
        [w["section"], own, returned, w["gain_two"]],
        [second, active],
        [shape((size, width), bf16), shape((size, width), f32), shape((3, width), f32)],
        [part] * SHARDS,
        vmem(second, active, shape((SHARDS,) + part.shape, bf16)) + sems(1 + SHARDS, SHARDS),
        2 * SHARDS * size * units * width,
        1,
    )
    return parts, branch_two, grad_second, sums


def run_up_grads(branch_two, grad_second, sums, kept, w):
    size, width = branch_two.shape
    _, held_up, held_down, sem_mlp = sizes(w, ORDER)
    names = ("hidden", "slope", "first")
    hidden, slope, first = take(kept, names)
    part = shape(held_up.shape[1:], bf16)
    whole = shape((size, width), f32)
    *parts, grad_bias_up, sums, grad_first, branch_one = launch(
        functools.partial(up_grads, kinds_of(w, ORDER)),
        "up_grads",
        [w["rotation"], branch_two, w["gain_one"], sums],
        [hidden, slope, grad_second, first] + flat(w["mlp"], ORDER),
        [
            shape((SHARDS, 1, held_up.shape[2]), f32),
            shape((6, width), f32),
            whole,
            shape((size, width), bf16),
        ],
        [part] * SHARDS,
        vmem(whole, slope, hidden, first, held_up, held_down, held_up)
        + sems(3 + SHARDS, sem_mlp, SHARDS),
        6 * size * held_up.size,
        1,
    )
    return parts, grad_bias_up, sums, grad_first, branch_one


def run_attention_grads(branch_one, grad_first, rows, sums, grad_bias_up, kept, w):
    size, width = rows.shape
    held, _, _, _ = sizes(w, ORDER)
    names = ("mixed", "probs", "attended")
    mixed, probs, attended = take(kept, names)
    part = shape(held.shape[1:], bf16)
    *parts, grad_in = launch(
        functools.partial(attention_grads, groups_of(w, ORDER)),
        "attention_grads",
        [branch_one, rows, sums, grad_bias_up],
        [mixed, probs, attended, grad_first] + flat(w["mix"], ORDER),
        [shape((size, width), bf16)],
        [part] * SHARDS,
        vmem(grad_first, mixed, probs, attended, held, held, probs, mixed)
        + sems(3 * SHARDS + 1, (SHARDS, 3), SHARDS),
        4 * size * held.size,
    )
    return parts, grad_in


def to_partner(x, bits):
    size = lax.axis_size("tensor")
    return lax.ppermute(x, "tensor", [(i, i ^ bits) for i in range(size)])


def add(*items):
    return sum(item.astype(f32) for item in items).astype(bf16)


def tie(value, *others):
    return lax.optimization_barrier((value, *others))[0]


class Line:
    lag = 3

    def __init__(self):
        self.size = lax.axis_size("dp")
        place = lax.axis_index("dp")
        self.middle = (place == 1) | (place == 2)
        self.parts, self.sent, self.pairs, self.totals, self.done = [], [], [], [], []
        self.last = jnp.zeros((8, 128), bf16)

    def add(self, *items, cut=slice(None)):
        *items, _ = lax.optimization_barrier((*items, self.last))
        self.last = add(*[item[cut] for item in items])
        return self.last

    def exchange(self, keep=None, received=None, cut=None, far=None, settle=False):
        fresh = [] if far is None else [keep, received, far]
        if self.size != 4:
            if fresh:
                *values, _ = lax.optimization_barrier((*fresh, self.last))
                self.last = add(values[0][cut], values[1][cut], values[2])
                self.done.append(lax.psum(self.last, "dp"))
            return
        routes, items = [], []
        back = len(self.sent) - self.lag
        if back >= 0:
            items += list(self.pairs[back])
            routes += [(1, 0), (2, 3)]
        if fresh:
            routes += [(0, 1), (3, 2)]
        pair = self.pairs[-1:] if settle else []
        *values, pair, _ = lax.optimization_barrier((*items, *fresh, pair, self.last))
        if settle:
            self.pairs[-1:] = pair
        total = part = None
        if fresh:
            keep, received, far = values[len(items) :]
            self.parts.append((keep, received, cut, far))
            part = add(keep[cut], received[cut], far)
        if back >= 0:
            total = add(*values[:2])
            self.totals.append(total)
        if total is None or part is None:
            operand = part if total is None else total
        else:
            rows = max(total.shape[0], part.shape[0])
            wide_total, part = [
                jnp.pad(v, ((0, rows - v.shape[0]), (0, 0))) for v in (total, part)
            ]
            operand = jnp.where(self.middle, wide_total, part)
        self.last = operand
        answer = lax.ppermute(operand, "dp", routes)
        self.sent.append(answer)
        if back >= 0:
            self.done.append(jnp.where(self.middle, total, answer[: total.shape[0]]))

    def inner(self):
        if self.size != 4:
            return
        keep, received, cut, far = self.parts[len(self.pairs)]
        answer = self.sent[len(self.pairs)]
        *values, _ = lax.optimization_barrier((keep, received, far, answer, self.last))
        keep, received, far, answer = values
        self.last = add(keep[cut], received[cut], far, answer[: far.shape[0]])
        self.pairs.append((self.last, lax.ppermute(self.last, "dp", [(1, 2), (2, 1)])))


def all_rows(own, near, far, both):
    place = lax.axis_index("tensor")
    low, high = place % 2 == 1, place // 2 == 1
    first = [jnp.where(low, near, own), jnp.where(low, own, near)]
    second = [jnp.where(low, both, far), jnp.where(low, far, both)]
    return [jnp.where(high, b, a) for a, b in zip(first, second)] + [
        jnp.where(high, a, b) for a, b in zip(first, second)
    ]


def body(
    ends_in,
    segment_ids,
    w_qkv,
    bias_qv,
    w_out,
    bias_out,
    gain_one,
    shift_one,
    w_up,
    bias_up,
    w_down,
    bias_down,
    gain_two,
    shift_two,
):
    section = lax.axis_index("section")
    place = lax.axis_index("tensor")
    _, micro, count, length, width = ends_in.shape
    share = count // lax.axis_size("tensor")
    own = lax.dynamic_slice_in_dim(ends_in[0], place * share, share, 1)
    own = own.reshape(micro * share * length, width)
    segments = lax.dynamic_slice_in_dim(segment_ids, place * share, share, 1)
    segments = segments.reshape(micro * share, length)
    third = w_qkv.shape[3]
    rotation = lax.axis_index("dp").astype(jnp.int32).reshape(1)
    w = {
        "rotation": rotation,
        "section": section.astype(jnp.int32).reshape(1),
        "place": place.astype(jnp.int32).reshape(1),
        "bias_out": bias_out,
        "gain_one": gain_one,
        "shift_one": shift_one,
        "bias_down": bias_down,
        "gain_two": gain_two,
        "shift_two": shift_two,
    }
    up, down, qkv = w_up[0], w_down[0], w_qkv[0].reshape(width, -1).T
    turns = lax.axis_size("dp") if lax.axis_size("dp") == 4 else 1
    outer, *piece = run_pack(turns, rotation, bias_qv[0], bias_up, w_out[0], up, down)
    piece = [to_partner(item, 2) for item in piece]
    outer_near, up_near, down_near = [to_partner(item, 1) for item in (outer, up, down)]
    near_sent, far_sent = run_head_attention(
        w["place"],
        share,
        ends_in[0].reshape(-1, width),
        segment_ids,
        [qkv, outer],
    )
    far_sent, near_sent, outer_near, up_near, down_near, *piece = lax.optimization_barrier(
        (far_sent, near_sent, outer_near, up_near, down_near, *piece)
    )

    def turned(item, turn):
        return lax.ppermute(item, "dp", [(i, (i + turn) % turns) for i in range(turns)])

    one, three = [[turned(item, turn) for item in piece] for turn in (1, turns - 1)]
    outer_far = to_partner(tie(outer, far_sent), 2)
    far_in = to_partner(far_sent, 2)
    near_in = to_partner(near_sent, 1)
    far_in, near_in, outer_far, *one = lax.optimization_barrier((far_in, near_in, outer_far, *one))
    both_in, outer_both = to_partner(far_in, 1), to_partner(outer_far, 1)
    two = [turned(item, 1) for item in one]
    direct = up.shape[0] - (TURNED if turns > 1 else 0)
    far = [to_partner(tie(up[:direct], far_in), 2)]
    if turns == 1:
        far.append(to_partner(tie(down, far_in), 2))
    w["mlp"] = [[up, down], [up_near, down_near]]
    outers = [outer, outer_near, outer_far, outer_both]
    w["mix"] = [[qkv, outer]]
    first, second = run_mlp_forward(
        NEAR_PAIR, [bias_out, near_sent, near_in, far_in, both_in], [ends_in[0]], outers, w
    )
    pieces, _ = lax.optimization_barrier((piece + one + two + three, first))
    pieces_near = [to_partner(item, 1) for item in pieces]
    far, pieces_near = lax.optimization_barrier((far, pieces_near))
    w["mlp"] += [far + pieces, [to_partner(item, 1) for item in far] + pieces_near]
    cut = 4 * qkv.shape[0] // 9
    query_far = to_partner(tie(qkv[:cut], *far), 2)
    qkv_near = to_partner(tie(qkv, *pieces_near), 1)
    (out,) = run_mlp_forward(FAR_PAIR, [], [first, second], outers[2:], w)
    out, query_far, qkv_near = lax.optimization_barrier((out, query_far, qkv_near))
    keys_far = to_partner(tie(qkv[cut:], query_far), 2)
    w["mix"] += [
        [qkv_near, outer_near],
        [query_far, keys_far, outer_far],
        [to_partner(query_far, 1), to_partner(keys_far, 1), outer_both],
    ]
    received = lax.ppermute(out, "section", [(0, 1)])
    out, grad_in, rows, kept = run_middle(received, own, segments, w)
    returned = lax.ppermute(grad_in, "section", [(1, 0)])

    line = Line()

    def swap(send):
        return to_partner(tie(send, line.last), 1)

    def halves(keep):
        half = keep.shape[0] // 2 // 16 * 16
        return slice(0, half), slice(half, None)

    def cross(keep, received):
        return [to_partner(line.add(keep, received, cut=cut), 2) for cut in halves(keep)]

    def chunks(keep, received, far):
        return [(keep, received, cut, item) for cut, item in zip(halves(keep), far)]

    down, branch_two, grad_second, sums = run_down_grads(own, returned, kept, w)
    line.last = branch_two
    down_far = cross(down[0], swap(down[1]))
    received = swap(down[3])
    up, grad_bias_up, sums, grad_first, branch_one = run_up_grads(
        tie(branch_two, line.last), grad_second, sums, kept, w
    )
    line.last = branch_one
    down = chunks(down[2], received, down_far)
    line.exchange(*down[0])
    received = swap(up[1])
    mixer, grad_in = run_attention_grads(
        tie(branch_one, line.last), grad_first, rows, sums, grad_bias_up, kept, w
    )
    line.last = grad_in
    up_far = cross(up[0], received)
    line.exchange(*down[1])
    line.inner()
    mixer_received, up_received = swap(mixer[1]), swap(up[3])
    up = chunks(up[2], up_received, up_far)
    mixer_far = cross(mixer[0], mixer_received)
    line.exchange(*up[0])
    line.inner()
    mixer = chunks(mixer[2], swap(mixer[3]), mixer_far)
    line.exchange(*up[1])
    line.inner()
    mine = jnp.where(section == 1, out, grad_in).reshape(micro, share, length, width)
    line.exchange(*mixer[0], settle=True)
    line.inner()
    line.exchange(*mixer[1])
    mine = tie(mine, line.last)
    mine_far = to_partner(mine, 2)
    line.inner()
    line.exchange()
    line.inner()
    line.exchange()
    mine, mine_far, _ = lax.optimization_barrier((mine, mine_far, line.last))
    near = to_partner(mine, 1), to_partner(mine_far, 1)
    line.exchange()
    mine, near, mine_far, both, _ = lax.optimization_barrier(
        (mine, near[0], mine_far, near[1], line.last)
    )
    ends = all_rows(mine, near, mine_far, both)
    down, up, mixer = line.done[:2], line.done[2:4], line.done[4:]
    half = mixer[0].shape[0]
    qkv = jnp.concatenate([mixer[0][third:], mixer[1][: 4 * third - half]], 0)
    small = mixer[1][4 * third - half :]
    results = (
        jnp.concatenate(ends, 1),
        qkv.T.reshape(width, 3, third),
        small[1:3, :third],
        mixer[0][:third],
        small[6],
        small[7],
        small[8],
        jnp.concatenate(up, 0),
        small[0],
        jnp.concatenate(down, 0),
        small[3],
        small[4],
        small[5],
    )
    return tuple(item.astype(f32)[None] for item in results)


def solution(mesh):
    return jax.shard_map(
        body,
        mesh=mesh,
        in_specs=(
            P("section", None, "dp", None, None),
            P(None, "dp", None),
            P("section", None, None, "tensor"),
            P("section", None, "tensor"),
            P("section", "tensor", None),
            P("section", None),
            P("section", None),
            P("section", None),
            P("section", None, "tensor"),
            P("section", "tensor"),
            P("section", "tensor", None),
            P("section", None),
            P("section", None),
            P("section", None),
        ),
        out_specs=(
            P("section", None, "dp", None, None),
            P("section", None, None, "tensor"),
            P("section", None, "tensor"),
            P("section", "tensor", None),
            P("section", None),
            P("section", None),
            P("section", None),
            P("section", None, "tensor"),
            P("section", "tensor"),
            P("section", "tensor", None),
            P("section", None),
            P("section", None),
            P("section", None),
        ),
        check_vma=False,
    )
```

```python
import functools
import jax
import jax.numpy as jnp
from jax import lax
from jax.experimental import pallas as pl
from jax.experimental.pallas import tpu as pltpu
from jax.sharding import PartitionSpec as P

HEAD = 64
LEN = 128
SHARDS = 4
SMALL = 16
TURNED = 256
ROOM = {"attention_grads": 46}
NEAR_PAIR, FAR_PAIR, ALL = (0, 1), (2, 3), (0, 1, 2, 3)
epsilon = 1e-05
bf16 = jnp.bfloat16
f32 = jnp.float32
ANY = pl.BlockSpec(memory_space=pl.ANY)
VM = pl.BlockSpec(memory_space=pltpu.VMEM)
SM = pl.BlockSpec(memory_space=pltpu.SMEM)


def nn(left, right):
    return lax.dot_general(left, right, (((1,), (0,)), ((), ())), preferred_element_type=f32)


def nt(left, right):
    return lax.dot_general(left, right, (((1,), (1,)), ((), ())), preferred_element_type=f32)


def tn(left, right):
    return lax.dot_general(left, right, (((0,), (0,)), ((), ())), preferred_element_type=f32)


def standardize(summed):
    center = summed - jnp.mean(summed, -1, keepdims=True)
    inverse = lax.rsqrt(jnp.mean(center * center, -1, keepdims=True) + epsilon)
    return center * inverse, inverse


def norm_back(normed, inverse, gain, grad_output):
    scaled = grad_output * gain
    return inverse * (
        scaled
        - jnp.mean(scaled, -1, keepdims=True)
        - normed * jnp.mean(scaled * normed, -1, keepdims=True)
    )


def wide(ref):
    return ref[...].astype(f32)


def load(sources, held, sems):
    copies = [
        pltpu.make_async_copy(src, held.at[n], sems.at[n]) for n, src in enumerate(sources)
    ]
    for copy in copies:
        copy.start()
    return copies


def load_mixers(groups, refs, held, sems, after=lambda n: None):
    refs = list(refs)
    loads = []
    for n, group in enumerate(groups):
        at, copies = 0, []
        for i in range(group):
            block = refs.pop(0)
            size = block.shape[0]
            target = held.at[n, pl.ds(at, size)]
            copies.append(pltpu.make_async_copy(block, target, sems.at[n, i]))
            copies[-1].start()
            at += size
        loads.append(copies)
        after(n)
    return loads


def load_mlp(kinds, refs, rotation, held_up, held_down, sems, up_first, before=lambda n: None):
    refs = list(refs)
    ups, downs = [], []
    for n, kind in enumerate(kinds):
        first = refs.pop(0)
        half = first.shape[0]
        up = [pltpu.make_async_copy(first, held_up.at[n, pl.ds(0, half)], sems.at[n, 0])]
        down = []
        if kind == 1:
            down.append(pltpu.make_async_copy(refs.pop(0), held_down.at[n], sems.at[n, 1]))
        else:
            size = held_down.shape[1] // kind
            rest = (held_up.shape[1] - half) // kind
            for turn in range(kind):
                piece = refs.pop(0)
                place = lax.rem(rotation[0] + (kind - turn), kind)
                at = pl.ds(pl.multiple_of(place * size, 16), size)
                down.append(
                    pltpu.make_async_copy(
                        piece.at[pl.ds(0, size)], held_down.at[n, at], sems.at[n, 1 + turn]
                    )
                )
                at = pl.ds(pl.multiple_of(half + place * rest, 16), rest)
                up.append(
                    pltpu.make_async_copy(
                        piece.at[pl.ds(size, rest)], held_up.at[n, at], sems.at[n, 1 + kind + turn]
                    )
                )
        before(n)
        for copy in up + down if up_first else down + up:
            copy.start()
        ups.append(up)
        downs.append(down)
    return ups, downs


def wait(copies):
    for copy in copies:
        copy.wait()


def fetch(pairs, sems):
    copies = [pltpu.make_async_copy(*pair, sems.at[n]) for n, pair in enumerate(pairs)]
    for copy in copies:
        copy.start()
    return copies


def fetch_own(place, ends, own, sems):
    micro, count, length, _ = ends.shape
    share = count // SHARDS
    pairs = [
        (ends.at[m, place[0] * share + j], own.at[pl.ds((m * share + j) * length, length)])
        for m in range(micro)
        for j in range(share)
    ]
    return fetch(pairs, sems)


def by_sequence(count, value):
    return jnp.concatenate([value(slice(i * LEN, (i + 1) * LEN)) for i in range(count)], 1)


def same_segment(segments):
    ids = segments[...].astype(f32)
    if ids.ndim == 3:
        ids = jnp.concatenate([ids[i] for i in range(ids.shape[0])], 0)
    count = ids.shape[0]
    ids_down = jnp.concatenate([ids, jnp.zeros((-count % 8, LEN), f32)], 0).T
    return jnp.concatenate([ids_down[:, i : i + 1] == ids[i : i + 1] for i in range(count)], 1)


def attend(weights, x, same, mixed_out, probs_out):
    count = x.shape[0] // LEN
    third = (weights.shape[0] - SMALL) // 4
    bias = weights[4 * third :].astype(f32)[:8].T[: 3 * third, :1]
    mixed = (nt(weights[: 3 * third], x) + bias).astype(bf16)
    mixed_out[:third] = mixed[:third] * HEAD**-0.5
    mixed_out[third:] = mixed[third:]
    heads = range(third // HEAD)
    for h in heads:
        query = mixed_out[h * HEAD : (h + 1) * HEAD]
        keys = mixed_out[third + h * HEAD : third + (h + 1) * HEAD]
        probs_out[h] = by_sequence(count, lambda cols: tn(keys[:, cols], query[:, cols]))
    for h in heads:
        scores = jnp.where(same, probs_out[h], -1e9)
        probs = jnp.exp(scores - jnp.max(scores, 0, keepdims=True))
        probs_out[h] = probs * (1.0 / jnp.sum(probs, 0, keepdims=True))
    attended = []
    for h in heads:
        value = mixed_out[2 * third + h * HEAD : 2 * third + (h + 1) * HEAD]
        low = probs_out[h].astype(bf16)
        attended.append(by_sequence(count, lambda cols: nn(value[:, cols], low[:, cols])))
    return jnp.concatenate(attended, 0).astype(bf16)


def attend_back(mixed, probs, grads, scores, result):
    third, size = grads.shape
    count = size // LEN
    heads = range(third // HEAD)
    for h in heads:
        at = slice(h * HEAD, (h + 1) * HEAD)
        value, grad = mixed[2 * third + at.start : 2 * third + at.stop], grads[at]
        scores[h] = by_sequence(count, lambda cols: tn(value[:, cols], grad[:, cols]))
    for h in heads:
        prob, grad = probs[h], scores[h]
        inner = jnp.sum(prob * grad, 0, keepdims=True)
        scores[h] = prob * (grad - inner)
    for h in heads:
        at = slice(h * HEAD, (h + 1) * HEAD)
        query, keys = mixed[at], mixed[third + at.start : third + at.stop]
        grad, low, score = grads[at], probs[h].astype(bf16), scores[h].astype(bf16)
        queries = by_sequence(count, lambda cols: nn(keys[:, cols], score[:, cols])) * HEAD**-0.5
        result[at] = queries.astype(bf16)
        result[third + at.start : third + at.stop] = by_sequence(
            count, lambda cols: nt(query[:, cols], score[:, cols])
        ).astype(bf16)
        result[2 * third + at.start : 2 * third + at.stop] = by_sequence(
            count, lambda cols: nt(grad[:, cols], low[:, cols])
        ).astype(bf16)


def head_attention(group, share, place, rows, segments, *refs):
    blocks, (near, far, held, mixed, probs, sems) = refs[:group], refs[group:]
    copies = load_mixers([group], blocks, held, sems)
    same = same_segment(segments)
    wait(copies[0])
    attended = attend(held.at[0], rows[...], same, mixed, probs)
    count = share * SHARDS
    for i in range(rows.shape[0] // LEN):
        owner = lax.bitwise_xor(place[0], i % count // share)
        at = i // count * share + i % share
        cols = slice(at * LEN, (at + 1) * LEN)
        block = attended[:, i * LEN : (i + 1) * LEN]

        @pl.when(owner < 2)
        def _(owner=owner, cols=cols, block=block):
            near[owner, :, cols] = block

        @pl.when(owner >= 2)
        def _(owner=owner, cols=cols, block=block):
            far[owner - 2, :, cols] = block


def gelu(upward):
    normal = 0.5 * (1.0 + lax.erf(upward * 0.7071067811865476))
    return normal, (upward * normal).astype(bf16)


def mlp_forward(kinds, last, *refs):
    rotation, *refs = refs
    if not last:
        place, *refs = refs
    gain_one, shift_one, gain_two, shift_two, bias_down, *rest = refs
    many = len(kinds)
    if last:
        kept, rest = rest[:2], rest[2:]
    else:
        bias_out, near, near_in, far_in, both_in, ends, *rest = rest
    count = many if last else SHARDS
    outers, rest = rest[:count], rest[count:]
    ins = sum(1 + kind for kind in kinds)
    weights, rest = rest[:ins], rest[ins:]
    if last:
        result, first, second, held_up, held_down, held_outer, sems, sem_outer, sem_kept = rest
        starts = fetch(zip(kept, (first, second)), sem_kept)
    else:
        result, second, rows, held_up, held_down, held_outer, sems, sem_outer, sem_own = rest
        own_loads = fetch_own(place, ends, rows, sem_own)
    loads = load(outers, held_outer, sem_outer)
    ups, downs = load_mlp(kinds, weights, rotation, held_up, held_down, sems, True)
    third = held_outer.shape[1] - SMALL
    if not last:
        first = result
        wait(own_loads)
        first[...] = rows[...].astype(f32) + wide(bias_out)
        parts = near[0], near_in[1], far_in[0], both_in[1]
        for n, part in enumerate(parts):
            loads[n].wait()
            first[...] += tn(part, held_outer[n, :third])
    else:
        starts[0].wait()
    normed, _ = standardize(first[...])
    hidden = normed * wide(gain_one) + wide(shift_one)
    hidden_low = hidden.astype(bf16)
    if last:
        wait([*loads, starts[1]])
    else:
        second[...] = hidden + wide(bias_down)
    for n in range(many):
        wait(ups[n])
        upward = nn(hidden_low, held_up[n]) + held_outer[n, third:].astype(f32)[1:2]
        _, active = gelu(upward)
        wait(downs[n])
        second[...] += nn(active, held_down[n])
    if last:
        normed, _ = standardize(second[...])
        result[...] = (normed * wide(gain_two) + wide(shift_two)).astype(bf16)


KEPT = ("first", "mixed", "probs", "attended", "hidden", "active", "slope", "second")


def middle(kinds, groups, *refs):
    rotation, section, received, cotangent, segments, *rest = refs
    gain_one, shift_one, gain_two, shift_two, bias_out, bias_down, *rest = rest
    many = len(kinds)
    mixers, rest = rest[: sum(groups)], rest[sum(groups) :]
    ins = sum(1 + kind for kind in kinds)
    weights, rest = rest[:ins], rest[ins:]
    out, grad_in, rows, *rest = rest
    leaving, rest = rest[: len(KEPT)], rest[len(KEPT) :]
    first, mixed, probs, attended, hidden_out, active_out, slope_out, second = rest[: len(KEPT)]
    held, held_up, held_down, total, scores, grad_mixed, *rest = rest[len(KEPT) :]
    sem_mix, sem_mlp, sem_out = rest
    staying = first, mixed, probs, attended, hidden_out, active_out, slope_out, second
    leave = [pltpu.make_async_copy(*pair, sem_out.at[n]) for n, pair in enumerate(zip(staying, leaving))]

    copies = load_mixers(groups, mixers, held, sem_mix)
    x = jnp.where(section[0] == 0, wide(cotangent), wide(received)).astype(bf16)
    rows[...] = x
    first[...] = x.astype(f32) + wide(bias_out)
    same = same_segment(segments)
    third = (held.shape[1] - SMALL) // 4
    wait(sum(copies, []))
    ups, downs = load_mlp(kinds, weights, rotation, held_up, held_down, sem_mlp, True)

    @pl.loop(0, many, unroll=2)
    def _(n):
        attended[n] = attend(held.at[n], x, same, mixed.at[n], probs.at[n])
        first[...] += tn(attended[n], held[n, 3 * third : 4 * third])

    for copy in leave[:4]:
        copy.start()
    normed_one, inverse_one = standardize(first[...])
    hidden = normed_one * wide(gain_one) + wide(shift_one)
    hidden_low = hidden.astype(bf16)
    hidden_out[...] = hidden_low
    second[...] = hidden + wide(bias_down)
    wait(sum(ups + downs, []))

    @pl.loop(0, many, unroll=4)
    def _(n):
        upward = nn(hidden_out[...], held_up[n]) + held[n, 4 * third :].astype(f32)[1:2]
        normal, active = gelu(upward)
        active_out[n] = active
        density = jnp.exp(-0.5 * upward * upward) * 0.3989422804014327
        slope_out[n] = (normal + upward * density).astype(bf16)
        second[...] += nn(active, held_down[n])

    for copy in leave[4:]:
        copy.start()
    normed, inverse = standardize(second[...])
    out[...] = (normed * wide(gain_two) + wide(shift_two)).astype(bf16)

    back = norm_back(normed, inverse, wide(gain_two), wide(cotangent))
    grad_in[...] = back.astype(bf16)
    total[...] = back

    @pl.loop(0, many, unroll=4)
    def _(n):
        grad_upward = (nt(grad_in[...], held_down[n]) * slope_out[n].astype(f32)).astype(bf16)
        total[...] += nt(grad_upward, held_up[n])

    normed, inverse = standardize(first[...])
    back = norm_back(normed, inverse, wide(gain_one), total[...])
    grad_in[...] = back.astype(bf16)
    total[...] = back

    @pl.loop(0, many, unroll=2)
    def _(n):
        grads = nt(held[n, 3 * third : 4 * third], grad_in[...]).astype(bf16)
        attend_back(mixed.at[n], probs.at[n], grads, scores, grad_mixed)
        total[...] += tn(grad_mixed[...], held[n, : 3 * third])

    grad_in[...] = total[...].astype(bf16)
    wait(leave)


ORDER = (2, 3, 0, 1)


def down_grads(*refs):
    section, own, returned, gain_two, *rest = refs
    kept, parts, rest = rest[:2], rest[2 : 2 + SHARDS], rest[2 + SHARDS :]
    branch_two, grad_second, sums, second, active, store, sem_kept, sem_out = rest
    loads = fetch(
        [(kept[0], second)] + [(kept[1].at[s], active.at[s]) for s in ORDER], sem_kept
    )
    g = jnp.where(section[0] == 0, wide(returned), wide(own))
    loads[0].wait()
    normed, inverse = standardize(second[...])
    back = norm_back(normed, inverse, wide(gain_two), g)
    grad_second[...] = back
    low = back.astype(bf16)
    branch_two[...] = low
    leave = []
    for n, s in enumerate(ORDER):
        loads[1 + n].wait()
        store[n] = tn(active[s], low).astype(bf16)
        leave.append(pltpu.make_async_copy(store.at[n], parts[n], sem_out.at[n]))
        leave[-1].start()
    sums[0:1] = jnp.sum(back, 0, keepdims=True)
    sums[1:2] = jnp.sum(g * normed, 0, keepdims=True)
    sums[2:3] = jnp.sum(g, 0, keepdims=True)
    wait(leave)


def up_grads(kinds, *refs):
    rotation, branch_two, gain_one, sums_two, *rest = refs
    kept, rest = rest[:4], rest[4:]
    many = len(kinds)
    ins = sum(1 + kind for kind in kinds)
    weights, rest = rest[:ins], rest[ins:]
    parts, rest = rest[:many], rest[many:]
    grad_bias_up, sums, grad_first, branch_one, *rest = rest
    total, slope, hidden, first, held_up, held_down, store, *rest = rest
    sem_kept, sem_mlp, sem_out = rest
    loads = [
        pltpu.make_async_copy(source, target, sem_kept.at[n])
        for n, (source, target) in enumerate(
            [(kept[0], hidden)]
            + [(kept[1].at[s], slope.at[s]) for s in ORDER]
            + [(kept[2], total), (kept[3], first)]
        )
    ]
    loads[0].start()
    ups, downs = load_mlp(
        kinds, weights, rotation, held_up, held_down, sem_mlp, False, lambda n: loads[1 + n].start()
    )
    loads[-2].start()
    loads[-1].start()
    low = branch_two[...]
    loads[0].wait()
    flipped = hidden[...].T
    leave = []
    for n, s in enumerate(ORDER):
        wait(downs[n])
        loads[1 + n].wait()
        grad_upward = (nt(low, held_down[n]) * slope[s].astype(f32)).astype(bf16)
        store[n] = nn(flipped, grad_upward).astype(bf16)
        leave.append(pltpu.make_async_copy(store.at[n], parts[n], sem_out.at[n]))
        leave[-1].start()
        grad_bias_up[n] = jnp.sum(grad_upward.astype(f32), 0, keepdims=True)
        wait(ups[n])
        if n == 0:
            loads[-2].wait()
        total[...] += nt(grad_upward, held_up[n])
    grad_hidden = total[...]
    loads[-1].wait()
    normed, inverse = standardize(first[...])
    back = norm_back(normed, inverse, wide(gain_one), grad_hidden)
    grad_first[...] = back
    branch_one[...] = back.astype(bf16)
    sums[0:3] = sums_two[...]
    sums[3:4] = jnp.sum(back, 0, keepdims=True)
    sums[4:5] = jnp.sum(grad_hidden * normed, 0, keepdims=True)
    sums[5:6] = jnp.sum(grad_hidden, 0, keepdims=True)
    wait(leave)


def attention_grads(groups, *refs):
    branch_one, rows, sums, grad_bias_up, *rest = refs
    kept, rest = rest[:4], rest[4:]
    mixers, rest = rest[: sum(groups)], rest[sum(groups) :]
    parts, rest = rest[:SHARDS], rest[SHARDS:]
    grad_in, total, mixed, probs, attended, held, store, scores, grad_mixed, *rest = rest
    sem_kept, sem_mix, sem_out = rest
    pairs = []
    for s in ORDER:
        pairs += [(kept[i].at[s], item.at[s]) for i, item in enumerate((mixed, probs, attended))]
    pairs.append((kept[3], total))
    loads = [pltpu.make_async_copy(*pair, sem_kept.at[n]) for n, pair in enumerate(pairs)]

    def begin(n):
        for copy in loads[3 * n : 3 * n + 3]:
            copy.start()

    copies = load_mixers(groups, mixers, held, sem_mix, begin)
    loads[-1].start()
    branch = branch_one[...]
    x = rows[...]
    ones = jnp.ones((16, x.shape[0]), bf16)
    third = (held.shape[1] - SMALL) // 4
    blank = jnp.zeros((1, x.shape[1] - third), f32)
    leave = []
    for n, s in enumerate(ORDER):
        wait(copies[n])
        wait(loads[3 * n : 3 * n + 3])
        grads = nt(held[n, 3 * third : 4 * third], branch).astype(bf16)
        store[n, :third] = nn(attended[s], branch).astype(bf16)
        attend_back(mixed.at[s], probs.at[s], grads, scores.at[n], grad_mixed.at[n])
        back = grad_mixed[n]
        store[n, third : 4 * third] = nn(back, x).astype(bf16)
        columns = nt(ones, back)
        small = [
            grad_bias_up[n],
            jnp.concatenate([columns[:1, :third], blank], 1),
            jnp.concatenate([columns[:1, 2 * third :], blank], 1),
            sums[...],
            jnp.zeros((SMALL - 9, x.shape[1]), f32),
        ]
        store[n, 4 * third :] = jnp.concatenate(small, 0).astype(bf16)
        leave.append(pltpu.make_async_copy(store.at[n], parts[n], sem_out.at[n]))
        leave[-1].start()
        if n == 0:
            loads[-1].wait()
        total[...] += tn(back, held[n, : 3 * third])
    grad_in[...] = total[...].astype(bf16)
    wait(leave)


def pack(count, rotation, bias_qv, bias_up, outer, up, down, *refs):
    third = outer.shape[0]
    result, *refs = refs
    copies = [(outer, result.at[pl.ds(0, third)])]
    if count > 1:
        piece, *refs = refs
        size, part = down.shape[0] // count, TURNED // count
        at = pl.multiple_of(rotation[0] * size, 16)
        copies.append((down.at[pl.ds(at, size)], piece.at[pl.ds(0, size)]))
        at = pl.multiple_of(up.shape[0] - TURNED + rotation[0] * part, 16)
        copies.append((up.at[pl.ds(at, part)], piece.at[pl.ds(size, part)]))
    copies = [pltpu.make_async_copy(*pair, refs[0].at[n]) for n, pair in enumerate(copies)]
    for copy in copies:
        copy.start()
    none = jnp.zeros((1, third), f32)
    biases = jnp.concatenate([wide(bias_qv)[:1], none, wide(bias_qv)[1:], none], 1)
    rest = jnp.zeros((SMALL - 2, biases.shape[1]), f32)
    result[third:] = jnp.concatenate([biases, wide(bias_up), rest], 0).astype(bf16)
    wait(copies)


def run_pack(count, rotation, bias_qv, bias_up, outer, up, down):
    third, width = outer.shape
    outputs = [shape((third + SMALL, width), bf16)]
    if count > 1:
        outputs += [shape(((down.shape[0] + TURNED) // count, width), bf16)]
    return pl.pallas_call(
        functools.partial(pack, count),
        name="pack",
        out_shape=outputs,
        in_specs=[SM, VM, VM, ANY, ANY, ANY],
        out_specs=[VM] * len(outputs),
        scratch_shapes=[pltpu.SemaphoreType.DMA((3,))],
    )(rotation, bias_qv, bias_up, outer, up, down)


def shape(dims, dtype):
    return jax.ShapeDtypeStruct(dims, dtype)


def launch(kernel, name, operands, weights, outputs, leaving, scratch, flops, scalars=0):
    size = sum(i.size * i.dtype.itemsize for i in [*operands, *weights, *outputs, *leaving])
    return pl.pallas_call(
        kernel,
        name=name,
        out_shape=list(leaving) + list(outputs),
        in_specs=[SM] * scalars + [VM] * (len(operands) - scalars) + [ANY] * len(weights),
        out_specs=[ANY] * len(leaving) + [VM] * len(outputs),
        scratch_shapes=scratch,
        compiler_params=pltpu.CompilerParams(vmem_limit_bytes=ROOM.get(name, 56) << 20),
        cost_estimate=pl.CostEstimate(flops=flops, bytes_accessed=size, transcendentals=0),
    )(*operands, *weights)


def vmem(*items):
    return [pltpu.VMEM(item.shape, item.dtype) for item in items]


def sems(*counts):
    return [pltpu.SemaphoreType.DMA((count if isinstance(count, tuple) else (count,))) for count in counts]


def sizes(w, which):
    up = w["mlp"][0][0].shape
    most = max(len(w["mlp"][s]) - 1 for s in which)
    rows = sum(block.shape[0] for block in w["mix"][0])
    return (
        shape((len(which), rows, up[0]), bf16),
        shape((len(which),) + up, bf16),
        shape((len(which),) + up[::-1], bf16),
        (len(which), 1 + 2 * most),
    )


def groups_of(w, which):
    return tuple(len(w["mix"][s]) for s in which)


def kinds_of(w, which):
    return tuple(len(w["mlp"][s]) - 1 for s in which)


def take(items, which):
    return [items[s] for s in which]


def flat(items, which):
    return [item for s in which for item in items[s]]


def kept_shapes(rows, w, which):
    size, width = rows.shape
    many, units = len(which), w["mlp"][0][0].shape[1]
    third = w["mix"][0][-1].shape[0] - SMALL
    return (
        shape((size, width), f32),
        shape((many, 3 * third, size), bf16),
        shape((many, third // HEAD, LEN, size), f32),
        shape((many, third, size), bf16),
        shape((size, width), bf16),
        shape((many, size, units), bf16),
        shape((many, size, units), bf16),
        shape((size, width), f32),
    )


def run_head_attention(place, share, rows, segments, blocks):
    size, width = rows.shape
    third = blocks[-1].shape[0] - SMALL
    sorted_rows = shape((2, third, size // SHARDS), bf16)
    return launch(
        functools.partial(head_attention, len(blocks), share),
        "head_attention",
        [place, rows, segments],
        blocks,
        [sorted_rows, sorted_rows],
        [],
        vmem(
            shape((1, 4 * third + SMALL, width), bf16),
            shape((3 * third, size), bf16),
            shape((third // HEAD, LEN, size), f32),
        )
        + sems((1, len(blocks))),
        6 * size * width * third,
        1,
    )


def run_mlp_forward(which, operands, sources, outers, w):
    last = which == FAR_PAIR
    width = w["bias_out"].shape[1]
    size = sources[0].size // width // (1 if last else SHARDS)
    names = ("gain_one", "shift_one", "gain_two", "shift_two", "bias_down")
    whole = shape((size, width), f32)
    low = shape((size, width), bf16)
    _, held_up, held_down, sem_mlp = sizes(w, which)
    many = len(outers)
    scratch = vmem(held_up, held_down, shape((many,) + outers[0].shape, bf16)) + sems(sem_mlp, many)
    scalars = [w["rotation"]] if last else [w["rotation"], w["place"]]
    return launch(
        functools.partial(mlp_forward, kinds_of(w, which), last),
        "mlp_forward",
        [*scalars, *[w[name] for name in names], *operands],
        sources + outers + flat(w["mlp"], which),
        [low] if last else [whole, whole],
        [],
        vmem(whole, whole) + scratch + sems(2)
        if last
        else vmem(low) + scratch + sems(size // LEN),
        4 * size * held_up.size,
        len(scalars),
    )


def run_middle(received, cotangent, segments, w):
    size, width = received.shape
    held, held_up, held_down, sem_mlp = sizes(w, ALL)
    kept = kept_shapes(received, w, ALL)
    names = ("gain_one", "shift_one", "gain_two", "shift_two", "bias_out", "bias_down")
    low = shape((size, width), bf16)
    _, mixed, probs, *_ = kept
    scratch = (
        vmem(*kept, held, held_up, held_down, shape((size, width), f32))
        + vmem(shape(probs.shape[1:], f32), shape(mixed.shape[1:], bf16))
        + sems((SHARDS, 3), sem_mlp, len(kept))
    )

    def kernel(*refs):
        ins = 11 + len(flat(w["mix"], ALL) + flat(w["mlp"], ALL))
        ends = ins + len(kept)
        middle(
            kinds_of(w, ALL),
            groups_of(w, ALL),
            *refs[:ins],
            *refs[ends : ends + 3],
            *refs[ins:ends],
            *refs[ends + 3 :],
        )

    *kept, out, grad_in, rows = launch(
        kernel,
        "middle",
        [w["rotation"], w["section"], received, cotangent, segments, *[w[name] for name in names]],
        flat(w["mix"], ALL) + flat(w["mlp"], ALL),
        [low, low, low],
        kept,
        scratch,
        8 * size * (held.size + held_up.size),
        2,
    )
    return out, grad_in, rows, dict(zip(KEPT, kept))


def run_down_grads(own, returned, kept, w):
    size, width = own.shape
    second, active = kept["second"], kept["active"]
    units = active.shape[2]
    part = shape((units, width), bf16)
    *parts, branch_two, grad_second, sums = launch(
        down_grads,
        "down_grads",
        [w["section"], own, returned, w["gain_two"]],
        [second, active],
        [shape((size, width), bf16), shape((size, width), f32), shape((3, width), f32)],
        [part] * SHARDS,
        vmem(second, active, shape((SHARDS,) + part.shape, bf16)) + sems(1 + SHARDS, SHARDS),
        2 * SHARDS * size * units * width,
        1,
    )
    return parts, branch_two, grad_second, sums


def run_up_grads(branch_two, grad_second, sums, kept, w):
    size, width = branch_two.shape
    _, held_up, held_down, sem_mlp = sizes(w, ORDER)
    names = ("hidden", "slope", "first")
    hidden, slope, first = take(kept, names)
    part = shape(held_up.shape[1:], bf16)
    whole = shape((size, width), f32)
    *parts, grad_bias_up, sums, grad_first, branch_one = launch(
        functools.partial(up_grads, kinds_of(w, ORDER)),
        "up_grads",
        [w["rotation"], branch_two, w["gain_one"], sums],
        [hidden, slope, grad_second, first] + flat(w["mlp"], ORDER),
        [
            shape((SHARDS, 1, held_up.shape[2]), f32),
            shape((6, width), f32),
            whole,
            shape((size, width), bf16),
        ],
        [part] * SHARDS,
        vmem(whole, slope, hidden, first, held_up, held_down, held_up)
        + sems(3 + SHARDS, sem_mlp, SHARDS),
        6 * size * held_up.size,
        1,
    )
    return parts, grad_bias_up, sums, grad_first, branch_one


def run_attention_grads(branch_one, grad_first, rows, sums, grad_bias_up, kept, w):
    size, width = rows.shape
    held, _, _, _ = sizes(w, ORDER)
    names = ("mixed", "probs", "attended")
    mixed, probs, attended = take(kept, names)
    part = shape(held.shape[1:], bf16)
    *parts, grad_in = launch(
        functools.partial(attention_grads, groups_of(w, ORDER)),
        "attention_grads",
        [branch_one, rows, sums, grad_bias_up],
        [mixed, probs, attended, grad_first] + flat(w["mix"], ORDER),
        [shape((size, width), bf16)],
        [part] * SHARDS,
        vmem(grad_first, mixed, probs, attended, held, held, probs, mixed)
        + sems(3 * SHARDS + 1, (SHARDS, 3), SHARDS),
        4 * size * held.size,
    )
    return parts, grad_in


def to_partner(x, bits):
    size = lax.axis_size("tensor")
    return lax.ppermute(x, "tensor", [(i, i ^ bits) for i in range(size)])


def add(*items):
    return sum(item.astype(f32) for item in items).astype(bf16)


def tie(value, *others):
    return lax.optimization_barrier((value, *others))[0]


class Line:
    lag = 3

    def __init__(self):
        self.size = lax.axis_size("dp")
        place = lax.axis_index("dp")
        self.middle = (place == 1) | (place == 2)
        self.parts, self.sent, self.pairs, self.totals, self.done = [], [], [], [], []
        self.last = jnp.zeros((8, 128), bf16)

    def add(self, *items, cut=slice(None)):
        *items, _ = lax.optimization_barrier((*items, self.last))
        self.last = add(*[item[cut] for item in items])
        return self.last

    def exchange(self, keep=None, received=None, cut=None, far=None, settle=False):
        fresh = [] if far is None else [keep, received, far]
        if self.size != 4:
            if fresh:
                *values, _ = lax.optimization_barrier((*fresh, self.last))
                self.last = add(values[0][cut], values[1][cut], values[2])
                self.done.append(lax.psum(self.last, "dp"))
            return
        routes, items = [], []
        back = len(self.sent) - self.lag
        if back >= 0:
            items += list(self.pairs[back])
            routes += [(1, 0), (2, 3)]
        if fresh:
            routes += [(0, 1), (3, 2)]
        pair = self.pairs[-1:] if settle else []
        *values, pair, _ = lax.optimization_barrier((*items, *fresh, pair, self.last))
        if settle:
            self.pairs[-1:] = pair
        total = part = None
        if fresh:
            keep, received, far = values[len(items) :]
            self.parts.append((keep, received, cut, far))
            part = add(keep[cut], received[cut], far)
        if back >= 0:
            total = add(*values[:2])
            self.totals.append(total)
        if total is None or part is None:
            operand = part if total is None else total
        else:
            rows = max(total.shape[0], part.shape[0])
            wide_total, part = [
                jnp.pad(v, ((0, rows - v.shape[0]), (0, 0))) for v in (total, part)
            ]
            operand = jnp.where(self.middle, wide_total, part)
        self.last = operand
        answer = lax.ppermute(operand, "dp", routes)
        self.sent.append(answer)
        if back >= 0:
            self.done.append(jnp.where(self.middle, total, answer[: total.shape[0]]))

    def inner(self):
        if self.size != 4:
            return
        keep, received, cut, far = self.parts[len(self.pairs)]
        answer = self.sent[len(self.pairs)]
        *values, _ = lax.optimization_barrier((keep, received, far, answer, self.last))
        keep, received, far, answer = values
        self.last = add(keep[cut], received[cut], far, answer[: far.shape[0]])
        self.pairs.append((self.last, lax.ppermute(self.last, "dp", [(1, 2), (2, 1)])))


def all_rows(own, near, far, both):
    place = lax.axis_index("tensor")
    low, high = place % 2 == 1, place // 2 == 1
    first = [jnp.where(low, near, own), jnp.where(low, own, near)]
    second = [jnp.where(low, both, far), jnp.where(low, far, both)]
    return [jnp.where(high, b, a) for a, b in zip(first, second)] + [
        jnp.where(high, a, b) for a, b in zip(first, second)
    ]


def body(
    ends_in,
    segment_ids,
    w_qkv,
    bias_qv,
    w_out,
    bias_out,
    gain_one,
    shift_one,
    w_up,
    bias_up,
    w_down,
    bias_down,
    gain_two,
    shift_two,
):
    section = lax.axis_index("section")
    place = lax.axis_index("tensor")
    _, micro, count, length, width = ends_in.shape
    share = count // lax.axis_size("tensor")
    own = lax.dynamic_slice_in_dim(ends_in[0], place * share, share, 1)
    own = own.reshape(micro * share * length, width)
    segments = lax.dynamic_slice_in_dim(segment_ids, place * share, share, 1)
    segments = segments.reshape(micro * share, length)
    third = w_qkv.shape[3]
    rotation = lax.axis_index("dp").astype(jnp.int32).reshape(1)
    w = {
        "rotation": rotation,
        "section": section.astype(jnp.int32).reshape(1),
        "place": place.astype(jnp.int32).reshape(1),
        "bias_out": bias_out,
        "gain_one": gain_one,
        "shift_one": shift_one,
        "bias_down": bias_down,
        "gain_two": gain_two,
        "shift_two": shift_two,
    }
    up, down, qkv = w_up[0], w_down[0], w_qkv[0].reshape(width, -1).T
    turns = lax.axis_size("dp") if lax.axis_size("dp") == 4 else 1
    outer, *piece = run_pack(turns, rotation, bias_qv[0], bias_up, w_out[0], up, down)
    piece = [to_partner(item, 2) for item in piece]
    outer_near, up_near, down_near = [to_partner(item, 1) for item in (outer, up, down)]
    near_sent, far_sent = run_head_attention(
        w["place"],
        share,
        ends_in[0].reshape(-1, width),
        segment_ids,
        [qkv, outer],
    )
    far_sent, near_sent, outer_near, up_near, down_near, *piece = lax.optimization_barrier(
        (far_sent, near_sent, outer_near, up_near, down_near, *piece)
    )

    def turned(item, turn):
        return lax.ppermute(item, "dp", [(i, (i + turn) % turns) for i in range(turns)])

    one, three = [[turned(item, turn) for item in piece] for turn in (1, turns - 1)]
    outer_far = to_partner(tie(outer, far_sent), 2)
    far_in = to_partner(far_sent, 2)
    near_in = to_partner(near_sent, 1)
    far_in, near_in, outer_far, *one = lax.optimization_barrier((far_in, near_in, outer_far, *one))
    both_in, outer_both = to_partner(far_in, 1), to_partner(outer_far, 1)
    two = [turned(item, 1) for item in one]
    direct = up.shape[0] - (TURNED if turns > 1 else 0)
    far = [to_partner(tie(up[:direct], far_in), 2)]
    if turns == 1:
        far.append(to_partner(tie(down, far_in), 2))
    w["mlp"] = [[up, down], [up_near, down_near]]
    outers = [outer, outer_near, outer_far, outer_both]
    w["mix"] = [[qkv, outer]]
    first, second = run_mlp_forward(
        NEAR_PAIR, [bias_out, near_sent, near_in, far_in, both_in], [ends_in[0]], outers, w
    )
    pieces, _ = lax.optimization_barrier((piece + one + two + three, first))
    pieces_near = [to_partner(item, 1) for item in pieces]
    far, pieces_near = lax.optimization_barrier((far, pieces_near))
    w["mlp"] += [far + pieces, [to_partner(item, 1) for item in far] + pieces_near]
    cut = 4 * qkv.shape[0] // 9
    query_far = to_partner(tie(qkv[:cut], *far), 2)
    qkv_near = to_partner(tie(qkv, *pieces_near), 1)
    (out,) = run_mlp_forward(FAR_PAIR, [], [first, second], outers[2:], w)
    out, query_far, qkv_near = lax.optimization_barrier((out, query_far, qkv_near))
    keys_far = to_partner(tie(qkv[cut:], query_far), 2)
    w["mix"] += [
        [qkv_near, outer_near],
        [query_far, keys_far, outer_far],
        [to_partner(query_far, 1), to_partner(keys_far, 1), outer_both],
    ]
    received = lax.ppermute(out, "section", [(0, 1)])
    out, grad_in, rows, kept = run_middle(received, own, segments, w)
    returned = lax.ppermute(grad_in, "section", [(1, 0)])

    line = Line()

    def swap(send):
        return to_partner(tie(send, line.last), 1)

    def halves(keep):
        half = keep.shape[0] // 2 // 16 * 16
        return slice(0, half), slice(half, None)

    def cross(keep, received):
        return [to_partner(line.add(keep, received, cut=cut), 2) for cut in halves(keep)]

    def chunks(keep, received, far):
        return [(keep, received, cut, item) for cut, item in zip(halves(keep), far)]

    down, branch_two, grad_second, sums = run_down_grads(own, returned, kept, w)
    line.last = branch_two
    down_far = cross(down[0], swap(down[1]))
    received = swap(down[3])
    up, grad_bias_up, sums, grad_first, branch_one = run_up_grads(
        tie(branch_two, line.last), grad_second, sums, kept, w
    )
    line.last = branch_one
    down = chunks(down[2], received, down_far)
    line.exchange(*down[0])
    received = swap(up[1])
    mixer, grad_in = run_attention_grads(
        tie(branch_one, line.last), grad_first, rows, sums, grad_bias_up, kept, w
    )
    line.last = grad_in
    up_far = cross(up[0], received)
    line.exchange(*down[1])
    line.inner()
    mixer_received, up_received = swap(mixer[1]), swap(up[3])
    up = chunks(up[2], up_received, up_far)
    mixer_far = cross(mixer[0], mixer_received)
    line.exchange(*up[0])
    line.inner()
    mixer = chunks(mixer[2], swap(mixer[3]), mixer_far)
    line.exchange(*up[1])
    line.inner()
    mine = jnp.where(section == 1, out, grad_in).reshape(micro, share, length, width)
    line.exchange(*mixer[0], settle=True)
    line.inner()
    line.exchange(*mixer[1])
    mine = tie(mine, line.last)
    mine_far = to_partner(mine, 2)
    line.inner()
    line.exchange()
    line.inner()
    line.exchange()
    mine, mine_far, _ = lax.optimization_barrier((mine, mine_far, line.last))
    near = to_partner(mine, 1), to_partner(mine_far, 1)
    line.exchange()
    mine, near, mine_far, both, _ = lax.optimization_barrier(
        (mine, near[0], mine_far, near[1], line.last)
    )
    ends = all_rows(mine, near, mine_far, both)
    down, up, mixer = line.done[:2], line.done[2:4], line.done[4:]
    half = mixer[0].shape[0]
    qkv = jnp.concatenate([mixer[0][third:], mixer[1][: 4 * third - half]], 0)
    small = mixer[1][4 * third - half :]
    results = (
        jnp.concatenate(ends, 1),
        qkv.T.reshape(width, 3, third),
        small[1:3, :third],
        mixer[0][:third],
        small[6],
        small[7],
        small[8],
        jnp.concatenate(up, 0),
        small[0],
        jnp.concatenate(down, 0),
        small[3],
        small[4],
        small[5],
    )
    return tuple(item.astype(f32)[None] for item in results)


def solution(mesh):
    return jax.shard_map(
        body,
        mesh=mesh,
        in_specs=(
            P("section", None, "dp", None, None),
            P(None, "dp", None),
            P("section", None, None, "tensor"),
            P("section", None, "tensor"),
            P("section", "tensor", None),
            P("section", None),
            P("section", None),
            P("section", None),
            P("section", None, "tensor"),
            P("section", "tensor"),
            P("section", "tensor", None),
            P("section", None),
            P("section", None),
            P("section", None),
        ),
        out_specs=(
            P("section", None, "dp", None, None),
            P("section", None, None, "tensor"),
            P("section", None, "tensor"),
            P("section", "tensor", None),
            P("section", None),
            P("section", None),
            P("section", None),
            P("section", None, "tensor"),
            P("section", "tensor"),
            P("section", "tensor", None),
            P("section", None),
            P("section", None),
            P("section", None),
        ),
        check_vma=False,
    )
```
